32 devices in a mesh: dp: 16 (over z, x, core), tensor: 2 (over y).
Axes of the slice: x: 2, y: 2, z: 4, core: 2. Of those that a mesh axis runs over, the one named last changes fastest.
Arguments:
- target_tokens: bfloat16 [16, 1024, 768], P('dp'), may hold values from -6 to 6
- memory_tokens: bfloat16 [16, 1024, 768], P('dp'), may hold values from -6 to 6
- output_grad: bfloat16 [16, 1024, 768], P('dp'), may hold values from -6 to 6
- target_segments: int32 [16, 1024], P('dp'), may hold values from 0 to 3, as said below
- memory_segments: int32 [16, 1024], P('dp'), may hold values from 0 to 3, as said below
- norm1_gain: float32 [768], replicated, may hold values from 0.25 to 1.75
- norm1_shift: float32 [768], replicated, may hold values from -1.5 to 1.5
- self_query: bfloat16 [768, 768], P(None, 'tensor'), may hold values from -0.21875 to 0.21875
- self_key: bfloat16 [768, 768], P(None, 'tensor'), may hold values from -0.21875 to 0.21875
- self_value: bfloat16 [768, 768], P(None, 'tensor'), may hold values from -0.21875 to 0.21875
- self_out: bfloat16 [768, 768], P('tensor'), may hold values from -0.875 to 0.875
- norm2_gain: float32 [768], replicated, may hold values from 0.25 to 1.75
- norm2_shift: float32 [768], replicated, may hold values from -1.5 to 1.5
- cross_query: bfloat16 [768, 768], P(None, 'tensor'), may hold values from -0.21875 to 0.21875
- cross_key: bfloat16 [768, 768], P(None, 'tensor'), may hold values from -0.21875 to 0.21875
- cross_value: bfloat16 [768, 768], P(None, 'tensor'), may hold values from -0.21875 to 0.21875
- cross_out: bfloat16 [768, 768], P('tensor'), may hold values from -0.875 to 0.875
- norm3_gain: float32 [768], replicated, may hold values from 0.25 to 1.75
- norm3_shift: float32 [768], replicated, may hold values from -1.5 to 1.5
- ffn_up: bfloat16 [768, 3072], P(None, 'tensor'), may hold values from -0.21875 to 0.21875
- ffn_down: bfloat16 [3072, 768], P('tensor'), may hold values from -0.109375 to 0.109375
Outputs:
- layer_output: bfloat16 [16, 1024, 768], P('dp', 'tensor')
- input_grad: float32 [16, 1024, 768], P('dp', 'tensor')
- memory_grad: float32 [16, 1024, 768], P('dp', 'tensor')
- self_query_grad: float32 [768, 768], P('dp', 'tensor')
- self_key_grad: float32 [768, 768], P('dp', 'tensor')
- self_value_grad: float32 [768, 768], P('dp', 'tensor')
- self_out_grad: float32 [768, 768], P('tensor', 'dp')
- cross_query_grad: float32 [768, 768], P('dp', 'tensor')
- cross_key_grad: float32 [768, 768], P('dp', 'tensor')
- cross_value_grad: float32 [768, 768], P('dp', 'tensor')
- cross_out_grad: float32 [768, 768], P('tensor', 'dp')
- ffn_up_grad: float32 [768, 3072], P('dp', 'tensor')
- ffn_down_grad: float32 [3072, 768], P('tensor', 'dp')
- norm1_gain_grad: float32 [768], replicated
- norm1_shift_grad: float32 [768], replicated
- norm2_gain_grad: float32 [768], replicated
- norm2_shift_grad: float32 [768], replicated
- norm3_gain_grad: float32 [768], replicated
- norm3_shift_grad: float32 [768], replicated
The draws below stay inside these ranges and needn't reach their ends.
Inputs may be any that keep to these rules, and one draw needn't show every extreme that they name: `target_segments`: per sequence the ids never fall, start at 0, and every id 0 to 3 occurs. `memory_segments`: per sequence the ids never fall, start at 0, and every id 0 to 3 occurs, so every target position has memory positions of its document.
All inputs are finite; a program needn't handle non-finite values.
Results may differ from the reference program's by a relative error of at most 0.028.
Values may be sent and summed in bfloat16 or wider, within the bound.
No kernel may reach another device: no remote copies, remote signals or barrier semaphores. Data moves between devices by JAX's collectives and lax.ppermute only.
A program may use at most 192 MiB of HBM per device.

```python
import jax
import jax.numpy as jnp
from jax import lax

D = 768
HEADS = 12
HEAD_DIM = 64
FF = 3072
TGT = 1024
MEM = 1024
DOCS = 4
SEQS = 16
N_TENSOR = 2


def segment_row(row_key, length):
    borders = jnp.sort(jax.random.permutation(row_key, length - 1)[:DOCS - 1]) + 1
    places = jnp.arange(length)
    return jnp.sum((places[:, None] >= borders[None, :]).astype(jnp.int32), 1).astype(jnp.int32)


def draw_target_segments(key, part):
    key = jax.random.fold_in(key, 11)
    row_keys = jax.random.split(key, SEQS)
    return jax.vmap(lambda row_key: segment_row(row_key, TGT))(row_keys)


def draw_memory_segments(key, part):
    key = jax.random.fold_in(key, 23)
    row_keys = jax.random.split(key, SEQS)
    return jax.vmap(lambda row_key: segment_row(row_key, MEM))(row_keys)


def spiked(array, key, source, target, shards_of, factor):
    def block_of(axis_at):
        return (jnp.arange(array.shape[axis_at]) // (array.shape[axis_at] // shards_of)).reshape((-1,) + (1,) * (array.ndim - 1 - axis_at))

    first = jax.random.permutation(key, shards_of)[block_of(target)]
    other_side = (block_of(target) + shards_of // 2) % shards_of
    return jnp.where((block_of(source) == first) | (block_of(source) == other_side), factor * array, array)


def block_levels(key, extent, shards, low, largest):
    def one(axis_at, blocks):
        steps = jax.random.uniform(jax.random.fold_in(jax.random.fold_in(key, 6), axis_at), (blocks,), jnp.float32, low / len(shards), largest / len(shards))
        return jnp.repeat(jnp.exp(steps), extent[axis_at] // blocks).reshape((-1,) + (1,) * (len(extent) - axis_at - 1))

    level = one(*shards[0])
    for cut in shards[1:]:
        level = level * one(*cut)
    return level


def centred(stream_key, shape, width, bound, cuts=(), kind=jnp.bfloat16):
    entries = jax.random.normal(stream_key, shape, jnp.float32) * width
    if len(cuts) > 0:
        entries = block_levels(stream_key, shape, cuts, -0.22, 0.18) * entries
    return jnp.clip(entries, min=-bound, max=bound).astype(kind)


def heavy_noise(own_key, dims, scale, most, cuts, heavy, held_as=jnp.bfloat16):
    values = scale * jax.random.normal(own_key, dims, jnp.float32)
    if cuts:
        values = values * block_levels(own_key, dims, cuts, -0.22, 0.18)
    return jnp.clip(spiked(values, jax.random.fold_in(own_key, 3), *heavy), -most, most).astype(held_as)


def setup_inputs(seed: int = 0) -> dict:
    key_list = jax.random.split(jax.random.key(seed), 22)
    target_tokens = centred(key_list[0], (SEQS, TGT, D), 1.0, 6.0, ((0, 16),))
    memory_tokens = centred(key_list[1], (SEQS, MEM, D), 1.0, 6.0, ((0, 16),))
    output_grad = heavy_noise(key_list[2], (SEQS, TGT, D), 1.0, 6.0, ((0, 16),), (0, 2, 16, 2.0))
    target_segments = draw_target_segments(jax.random.fold_in(key_list[21], 71), 0)
    memory_segments = draw_memory_segments(jax.random.fold_in(key_list[21], 71), 0)
    norm1_gain = jnp.clip(1.0 + 0.15 * jax.random.normal(key_list[5], (D,), jnp.float32), 0.25, 1.75)
    norm1_shift = centred(key_list[6], (D,), 0.3, 1.5, (), jnp.float32)
    self_query = centred(key_list[7], (D, HEADS * HEAD_DIM), D ** -0.5, 0.21875, ((1, 2),))
    self_key = centred(key_list[8], (D, HEADS * HEAD_DIM), D ** -0.5, 0.21875, ((1, 2),))
    self_value = centred(key_list[9], (D, HEADS * HEAD_DIM), D ** -0.5, 0.21875, ((1, 2),))
    self_out = centred(key_list[10], (HEADS * HEAD_DIM, D), (D // 16) ** -0.5, 0.875, ((0, 2),))
    norm2_gain = jnp.clip(1.0 + 0.15 * jax.random.normal(key_list[11], (D,), jnp.float32), 0.25, 1.75)
    norm2_shift = centred(key_list[12], (D,), 0.3, 1.5, (), jnp.float32)
    cross_query = centred(key_list[13], (D, HEADS * HEAD_DIM), D ** -0.5, 0.21875, ((1, 2),))
    cross_key = centred(key_list[14], (D, HEADS * HEAD_DIM), D ** -0.5, 0.21875, ((1, 2),))
    cross_value = centred(key_list[15], (D, HEADS * HEAD_DIM), D ** -0.5, 0.21875, ((1, 2),))
    cross_out = centred(key_list[16], (HEADS * HEAD_DIM, D), (D // 16) ** -0.5, 0.875, ((0, 2),))
    norm3_gain = jnp.clip(1.0 + 0.15 * jax.random.normal(key_list[17], (D,), jnp.float32), 0.25, 1.75)
    norm3_shift = centred(key_list[18], (D,), 0.3, 1.5, (), jnp.float32)
    ffn_up = centred(key_list[19], (D, FF), D ** -0.5, 0.21875, ((1, 2),))
    ffn_down = centred(key_list[20], (FF, D), FF ** -0.5, 0.109375, ((0, 2),))
    return {"target_tokens": target_tokens, "memory_tokens": memory_tokens, "output_grad": output_grad, "target_segments": target_segments, "memory_segments": memory_segments, "norm1_gain": norm1_gain, "norm1_shift": norm1_shift, "self_query": self_query, "self_key": self_key, "self_value": self_value, "self_out": self_out, "norm2_gain": norm2_gain, "norm2_shift": norm2_shift, "cross_query": cross_query, "cross_key": cross_key, "cross_value": cross_value, "cross_out": cross_out, "norm3_gain": norm3_gain, "norm3_shift": norm3_shift, "ffn_up": ffn_up, "ffn_down": ffn_down}


@jax.custom_vjp
def low(v):
    return lax.optimization_barrier(v.astype(jnp.bfloat16)).astype(jnp.float32)

@jax.custom_vjp
def low_back(v):
    return v

def low_keep(v):
    return (low(v), None)

def low_pass(kept, grad):
    return (grad,)

def back_keep(v):
    return (v, None)

def back_low(kept, grad):
    return (low(grad),)
low.defvjp(low_keep, low_pass)
low_back.defvjp(back_keep, back_low)

def layer_norm(values, gain, shift):
    centered = values - lax.optimization_barrier(jnp.mean(values, -1, keepdims=True))
    variance = lax.optimization_barrier(jnp.mean(centered * centered, -1, keepdims=True))
    return centered * lax.rsqrt(variance + 1e-05) * gain + shift

def product(left, right):
    return jnp.dot(left, right, precision=lax.Precision.HIGHEST)

def split_heads(matrix):
    return low(low_back(matrix)).reshape(matrix.shape[0], HEADS, HEAD_DIM)

def attend(queries, key_rows, value_rows, allowed):
    factor = HEAD_DIM ** (-0.5)
    scores = jnp.einsum('qhd,khd->hqk', queries, key_rows, precision=lax.Precision.HIGHEST)
    scores = low_back(scores * factor)
    scores = jnp.where(allowed[None], scores, -1e+30)
    shifted = jnp.exp(scores - lax.optimization_barrier(jnp.max(scores, -1, keepdims=True)))
    weights = shifted / lax.optimization_barrier(jnp.sum(shifted, -1, keepdims=True))
    mixed = jnp.einsum('hqk,khd->qhd', low(weights), value_rows, precision=lax.Precision.HIGHEST)
    return low(low_back(mixed.reshape(queries.shape[0], HEADS * HEAD_DIM)))

def branch_sum(merged, weight):
    grouped = merged.reshape(merged.shape[0], N_TENSOR, -1)
    blocks = weight.reshape(N_TENSOR, -1, D)
    parts = jnp.einsum('stk,tkd->tsd', grouped, blocks, precision=lax.Precision.HIGHEST)
    return low_back(lax.optimization_barrier(jnp.sum(low(parts), 0)))

def sequence_layer(params, stream, memory_rows, target_ids, memory_ids):
    norm1_gain, norm1_shift, self_query, self_key, self_value, self_out, norm2_gain, norm2_shift, cross_query, cross_key, cross_value, cross_out, norm3_gain, norm3_shift, ffn_up, ffn_down = params
    positions = jnp.arange(TGT)
    causal = (target_ids[:, None] == target_ids[None, :]) & (positions[None, :] <= positions[:, None])
    across = target_ids[:, None] == memory_ids[None, :]
    normed = low(layer_norm(stream, norm1_gain, norm1_shift))
    mixed = attend(split_heads(product(normed, self_query)), split_heads(product(normed, self_key)), split_heads(product(normed, self_value)), causal)
    stream = stream + branch_sum(mixed, self_out)
    normed = low(layer_norm(stream, norm2_gain, norm2_shift))
    mixed = attend(split_heads(product(normed, cross_query)), split_heads(product(memory_rows, cross_key)), split_heads(product(memory_rows, cross_value)), across)
    stream = stream + branch_sum(mixed, cross_out)
    normed = low(layer_norm(stream, norm3_gain, norm3_shift))
    hidden = low(jax.nn.gelu(low_back(product(normed, ffn_up)), approximate=True))
    return stream + branch_sum(hidden, ffn_down)

def reference(target_tokens, memory_tokens, output_grad, target_segments, memory_segments, norm1_gain, norm1_shift, self_query, self_key, self_value, self_out, norm2_gain, norm2_shift, cross_query, cross_key, cross_value, cross_out, norm3_gain, norm3_shift, ffn_up, ffn_down):
    params = tuple((weight.astype(jnp.float32) for weight in (norm1_gain, norm1_shift, self_query, self_key, self_value, self_out, norm2_gain, norm2_shift, cross_query, cross_key, cross_value, cross_out, norm3_gain, norm3_shift, ffn_up, ffn_down)))

    def one_sequence(totals, items):
        tokens, memory, grad_in, target_ids, memory_ids = items

        def forward(weights_in, stream_in, memory_in):
            return sequence_layer(weights_in, stream_in, memory_in, target_ids, memory_ids)
        result, pullback = jax.vjp(forward, params, tokens.astype(jnp.float32), memory.astype(jnp.float32))
        grad_params, grad_tokens, grad_memory = pullback(grad_in.astype(jnp.float32))
        totals = jax.tree.map(jnp.add, totals, grad_params)
        return (totals, (result.astype(jnp.bfloat16), grad_tokens, grad_memory))
    zeros = jax.tree.map(jnp.zeros_like, params)
    totals, (outputs, grad_tokens, grad_memory) = lax.scan(one_sequence, zeros, (target_tokens, memory_tokens, output_grad, target_segments, memory_segments))
    return (outputs, grad_tokens, grad_memory, totals[2], totals[3], totals[4], totals[5], totals[8], totals[9], totals[10], totals[11], totals[14], totals[15], totals[0], totals[1], totals[6], totals[7], totals[12], totals[13])
```

```python
from functools import partial

import jax
import jax.numpy as jnp
from jax import lax
from jax.experimental import pallas as pl
from jax.experimental.pallas import tpu as pltpu
from jax.sharding import PartitionSpec as P

HEAD_DIM = 64
DOCS = 4
BLOCK = 256
LOW = -1e30
F32 = jnp.float32
BF16 = jnp.bfloat16
VMEM_LIMIT = 56 * 1024 * 1024


def dot(left, right):
    return jnp.dot(left, right, preferred_element_type=F32)


def dot_nt(left, right):
    return lax.dot_general(left, right, (((1,), (1,)), ((), ())), preferred_element_type=F32)


def dot_tn(left, right):
    return lax.dot_general(left, right, (((0,), (0,)), ((), ())), preferred_element_type=F32)


def normalise(values):
    centered = values - jnp.mean(values, -1, keepdims=True)
    rstd = lax.rsqrt(jnp.mean(centered * centered, -1, keepdims=True) + 1e-05)
    return centered * rstd, rstd


def norm_backward(unit, rstd, gain, cotangent):
    scaled = cotangent * gain
    return rstd * (
        scaled
        - jnp.mean(scaled, -1, keepdims=True)
        - unit * jnp.mean(scaled * unit, -1, keepdims=True)
    )


def call(kernel, out_shape, *, flops=0, bytes_accessed=0, scalars=0, grid=(), in_specs=None, out_specs=None, scratch=()):
    whole = pl.BlockSpec(memory_space=pltpu.VMEM)
    return pl.pallas_call(
        kernel,
        out_shape=out_shape,
        grid_spec=pltpu.PrefetchScalarGridSpec(
            num_scalar_prefetch=scalars,
            grid=grid,
            in_specs=in_specs,
            out_specs=out_specs if out_specs is not None else jax.tree.map(lambda _: whole, out_shape),
            scratch_shapes=scratch,
        ),
        compiler_params=pltpu.CompilerParams(vmem_limit_bytes=VMEM_LIMIT),
        cost_estimate=pl.CostEstimate(
            flops=int(flops), bytes_accessed=int(bytes_accessed), transcendentals=0
        ),
    )


def shape(dims, dtype):
    return jax.ShapeDtypeStruct(dims, dtype)


def rows_spec(width, block=BLOCK):
    return pl.BlockSpec((block, width), lambda i, *_: (i, 0))


def full_spec(dims):
    return pl.BlockSpec(dims, lambda *_: (0,) * len(dims))


def norm_project_kernel(x_ref, gain_ref, shift_ref, wq_ref, wk_ref, wv_ref, a_ref, q_ref, k_ref, v_ref):
    unit, _ = normalise(x_ref[...].astype(F32))
    a = (unit * gain_ref[...] + shift_ref[...]).astype(BF16)
    a_ref[...] = a
    q_ref[...] = dot(a, wq_ref[...]).astype(BF16)
    k_ref[...] = dot(a, wk_ref[...]).astype(BF16)
    v_ref[...] = dot(a, wv_ref[...]).astype(BF16)


def norm_project(x, gain, shift, wq, wk, wv):
    rows, width = x.shape
    cols = wq.shape[1]
    weight = full_spec((width, cols))
    return call(
        norm_project_kernel,
        (shape((rows, width), BF16),) + (shape((rows, cols), BF16),) * 3,
        flops=6 * rows * width * cols,
        bytes_accessed=4 * rows * width,
        grid=(rows // BLOCK,),
        in_specs=[rows_spec(width), full_spec((1, width)), full_spec((1, width)), weight, weight, weight],
        out_specs=(rows_spec(width),) + (rows_spec(cols),) * 3,
    )(x, gain, shift, wq, wk, wv)


def first_doc(starts_ref, row):
    doc = 0
    for number in range(1, DOCS):
        doc = doc + (starts_ref[0, number] <= row).astype(jnp.int32)
    return doc


def key_range(starts_ref, block_number, causal):
    first = block_number * BLOCK
    low = starts_ref[1, first_doc(starts_ref, first)]
    if causal:
        return low // BLOCK, block_number
    high = starts_ref[1, first_doc(starts_ref, first + BLOCK - 1) + 1]
    return low // BLOCK, (high + BLOCK - 1) // BLOCK


def lanes(rows):
    return lax.broadcasted_iota(jnp.int32, (rows, 128), 1)


def causal_mask(keys_first):
    first = lax.broadcasted_iota(jnp.int32, (BLOCK, BLOCK), 0)
    second = lax.broadcasted_iota(jnp.int32, (BLOCK, BLOCK), 1)
    return first <= second if keys_first else second <= first


def pair_of(ref, pair, rows=slice(None)):
    return ref[rows, pair * 128 : (pair + 1) * 128]


def attend_kernel(
    causal, heads, where_ref, starts_ref, q_ref, k_ref, v_ref, dq_ref, dk_ref, o_ref, qa_ref,
    ka_ref, va_ref, qs_ref, acc_ref, max_ref,
):
    step = pl.program_id(0)
    keys = k_ref.shape[0]

    @pl.when(step == 0)
    def _():
        left = lanes(keys) < 64
        for head in range(heads):
            mine = left if head % 2 == 0 else ~left
            ka_ref[head] = jnp.where(mine, pair_of(k_ref, head // 2), dk_ref[...])
            va_ref[head] = jnp.where(mine, pair_of(v_ref, head // 2), jnp.ones((), BF16))

    left = lanes(BLOCK) < 64
    for head in range(heads):
        mine = left if head % 2 == 0 else ~left
        qs_ref[head] = jnp.where(mine, pair_of(q_ref, head // 2) * jnp.array(HEAD_DIM**-0.5, BF16), dq_ref[...])
    max_ref[...] = jnp.full_like(max_ref, LOW)
    acc_ref[...] = jnp.zeros_like(acc_ref)

    def one_block(number, mask):
        at = pl.ds(pl.multiple_of(number * BLOCK, BLOCK), BLOCK)
        for head in range(heads):
            scores = dot_nt(qs_ref[head], ka_ref[head, at, :])
            if mask is not None:
                scores = jnp.where(mask, scores, LOW)
            old = max_ref[head]
            new = jnp.maximum(old, jnp.max(scores, -1, keepdims=True))
            weights = jnp.exp(scores - new[:, :1]).astype(BF16)
            acc_ref[head] = acc_ref[head] * jnp.exp(old - new) + dot(weights, va_ref[head, at, :])
            max_ref[head] = new

    block_number = where_ref[0] + step
    low, high = key_range(starts_ref, block_number, causal)
    if causal:
        one_block(block_number, causal_mask(False))
    lax.fori_loop(low, high, lambda number, _: (one_block(number, None), 0)[1], 0)

    place = lanes(BLOCK) % 64
    outs = []
    for head in range(heads):
        mine = left if head % 2 == 0 else ~left
        acc = acc_ref[head]
        total = pltpu.roll(acc, 64, 1)
        outs.append(acc / total)
        lse = max_ref[head] + jnp.log(jnp.where(mine, total, acc))
        high_part = (-lse).astype(BF16)
        rest = -lse - high_part.astype(F32)
        mid_part = rest.astype(BF16)
        low_part = (rest - mid_part.astype(F32)).astype(BF16)
        extra = jnp.where(
            place == 4, high_part, jnp.where(place == 5, mid_part, jnp.where(place == 6, low_part, dq_ref[...]))
        )
        qa_ref[head] = jnp.where(mine, qs_ref[head], extra)
    for pair in range(heads // 2):
        o_ref[:, pair * 128 : (pair + 1) * 128] = jnp.where(
            left, outs[2 * pair], outs[2 * pair + 1]
        ).astype(BF16)


def attend(where, starts, q, k, v, doc_rows, doc_keys, rows, causal):
    cols = q.shape[1]
    heads = cols // HEAD_DIM
    keys = k.shape[0]
    q_rows = pl.BlockSpec((BLOCK, cols), lambda i, w, s: (i + w[1], 0))
    doc_spec = pl.BlockSpec((BLOCK, 128), lambda i, w, s: (i + w[0], 0))
    return call(
        partial(attend_kernel, causal, heads),
        (shape((rows, cols), BF16), shape((heads, rows, 128), BF16)),
        flops=16 * rows * keys * cols // 2,
        bytes_accessed=8 * keys * cols,
        scalars=2,
        grid=(rows // BLOCK,),
        in_specs=[
            q_rows, full_spec((keys, cols)), full_spec((keys, cols)), doc_spec, full_spec((keys, 128)),
        ],
        out_specs=(rows_spec(cols), pl.BlockSpec((heads, BLOCK, 128), lambda i, *_: (0, i, 0))),
        scratch=[
            pltpu.VMEM((heads, keys, 128), BF16),
            pltpu.VMEM((heads, keys, 128), BF16),
            pltpu.VMEM((heads, BLOCK, 128), BF16),
            pltpu.VMEM((heads, BLOCK, 128), F32),
            pltpu.VMEM((heads, BLOCK, 128), F32),
        ],
    )(where, starts, q, k, v, doc_rows, doc_keys)


def attend_back_kernel(
    causal, heads, where_ref, starts_ref, qa_ref, k_ref, v_ref, do_ref, o_ref, dk_doc_ref,
    dq_ref, dk_ref, dv_ref, ka_ref, va_ref, da_ref, dqa_ref, dka_ref, dva_ref,
):
    step = pl.program_id(0)
    keys = k_ref.shape[0]

    @pl.when(step == 0)
    def _():
        lane = lanes(keys)
        left = lane < 64
        place = lane % 64
        ones = jnp.where((place >= 4) & (place < 7), 1.0, 0.0).astype(BF16)
        for head in range(heads):
            mine = left if head % 2 == 0 else ~left
            ka_ref[head] = jnp.where(mine, pair_of(k_ref, head // 2), dk_doc_ref[...] + ones)
            va_ref[head] = jnp.where(mine, pair_of(v_ref, head // 2), ones)
        dka_ref[...] = jnp.zeros_like(dka_ref)
        dva_ref[...] = jnp.zeros_like(dva_ref)

    left = lanes(BLOCK) < 64
    place = lanes(BLOCK) % 64
    for head in range(heads):
        mine = left if head % 2 == 0 else ~left
        grad = pair_of(do_ref, head // 2)
        product = grad.astype(F32) * pair_of(o_ref, head // 2).astype(F32)
        delta = -jnp.sum(jnp.where(mine, product, 0.0), -1, keepdims=True)
        delta = jnp.broadcast_to(delta, (BLOCK, 128))
        high_part = delta.astype(BF16)
        rest = delta - high_part.astype(F32)
        mid_part = rest.astype(BF16)
        low_part = (rest - mid_part.astype(F32)).astype(BF16)
        extra = jnp.where(
            place == 4, high_part, jnp.where(place == 5, mid_part, jnp.where(place == 6, low_part, jnp.zeros((), BF16)))
        )
        da_ref[head] = jnp.where(mine, grad, extra)
    dqa_ref[...] = jnp.zeros_like(dqa_ref)

    def one_block(number, mask):
        at = pl.ds(pl.multiple_of(number * BLOCK, BLOCK), BLOCK)
        for pair in range(heads // 2):
            grads = []
            for head in (2 * pair, 2 * pair + 1):
                scores = dot_nt(ka_ref[head, at, :], qa_ref[head])
                if mask is not None:
                    scores = jnp.where(mask, scores, LOW)
                weights = jnp.exp(scores)
                grad_scores = (weights * dot_nt(va_ref[head, at, :], da_ref[head])).astype(BF16)
                value_grad = dot(weights.astype(BF16), da_ref[head])
                key_grad = dot(grad_scores, qa_ref[head])
                query_grad = dot_tn(grad_scores, ka_ref[head, at, :])
                grads.append((value_grad, key_grad, query_grad))
            dva_ref[pair, at, :] += jnp.where(left, grads[0][0], grads[1][0])
            dka_ref[pair, at, :] += jnp.where(left, grads[0][1], grads[1][1])
            dqa_ref[pair] += jnp.where(left, grads[0][2], grads[1][2])

    block_number = where_ref[0] + step
    low, high = key_range(starts_ref, block_number, causal)
    if causal:
        one_block(block_number, causal_mask(True))
    lax.fori_loop(low, high, lambda number, _: (one_block(number, None), 0)[1], 0)

    for pair in range(heads // 2):
        dq_ref[:, pair * 128 : (pair + 1) * 128] = (dqa_ref[pair] * HEAD_DIM**-0.5).astype(BF16)

    @pl.when(step == pl.num_programs(0) - 1)
    def _():
        for pair in range(heads // 2):
            dk_ref[:, pair * 128 : (pair + 1) * 128] = dka_ref[pair].astype(BF16)
            dv_ref[:, pair * 128 : (pair + 1) * 128] = dva_ref[pair].astype(BF16)


def attend_back(where, starts, qa, k, v, do, o, doc_keys, causal):
    rows, cols = do.shape
    heads = cols // HEAD_DIM
    keys = k.shape[0]
    return call(
        partial(attend_back_kernel, causal, heads),
        (shape((rows, cols), BF16), shape((keys, cols), BF16), shape((keys, cols), BF16)),
        flops=40 * rows * keys * cols // 2,
        bytes_accessed=12 * keys * cols,
        scalars=2,
        grid=(rows // BLOCK,),
        in_specs=[
            pl.BlockSpec((heads, BLOCK, 128), lambda i, *_: (0, i, 0)),
            full_spec((keys, cols)), full_spec((keys, cols)), rows_spec(cols), rows_spec(cols), full_spec((keys, 128)),
        ],
        out_specs=(rows_spec(cols), full_spec((keys, cols)), full_spec((keys, cols))),
        scratch=[
            pltpu.VMEM((heads, keys, 128), BF16),
            pltpu.VMEM((heads, keys, 128), BF16),
            pltpu.VMEM((heads, BLOCK, 128), BF16),
            pltpu.VMEM((heads // 2, BLOCK, 128), F32),
            pltpu.VMEM((heads // 2, keys, 128), F32),
            pltpu.VMEM((heads // 2, keys, 128), F32),
        ],
    )(where, starts, qa, k, v, do, o, doc_keys)


def out_project(own, other, own_weight, other_weight):
    half = own_weight.shape[1]
    left = dot(own, own_weight[:half]) + dot(other, other_weight[:half])
    right = dot(own, own_weight[half:]) + dot(other, other_weight[half:])
    return jnp.concatenate([left, right], axis=1)


def after_self_kernel(
    where_ref, x_ref, own_ref, other_ref, wo_ref, wp_ref, gain_ref, shift_ref, wq_ref, wr_ref, s_ref, a_ref, q_ref, r_ref
):
    stream = x_ref[...].astype(F32) + out_project(own_ref[...], other_ref[...], wo_ref[...], wp_ref[...])
    s_ref[...] = stream
    unit, _ = normalise(stream)
    a = (unit * gain_ref[...] + shift_ref[...]).astype(BF16)
    a_ref[...] = a
    q_ref[...] = dot(a, wq_ref[...]).astype(BF16)
    r_ref[...] = dot(a, wr_ref[...]).astype(BF16)


def after_self(where, x, own, other, wo, wp, gain, shift, wq, wr):
    rows, cols = own.shape
    width = x.shape[1]
    weight = full_spec((width, cols))
    return call(
        after_self_kernel,
        (shape((rows, width), F32), shape((rows, width), BF16)) + (shape((rows, cols), BF16),) * 2,
        flops=8 * rows * width * cols,
        bytes_accessed=12 * rows * width,
        scalars=1,
        grid=(rows // BLOCK,),
        in_specs=[
            pl.BlockSpec((BLOCK, width), lambda i, w: (i + w[0], 0)),
            rows_spec(cols), rows_spec(cols), weight, weight, full_spec((1, width)), full_spec((1, width)), weight, weight,
        ],
        out_specs=(rows_spec(width), rows_spec(width), rows_spec(cols), rows_spec(cols)),
    )(where, x, own, other, wo, wp, gain, shift, wq, wr)


def after_cross_kernel(s_ref, own_ref, other_ref, wo_ref, wp_ref, gain_ref, shift_ref, t_ref, a_ref):
    stream = s_ref[...] + out_project(own_ref[...], other_ref[...], wo_ref[...], wp_ref[...])
    t_ref[...] = stream
    unit, _ = normalise(stream)
    a_ref[...] = (unit * gain_ref[...] + shift_ref[...]).astype(BF16)


def after_cross(stream, own, other, wo, wp, gain, shift):
    rows, cols = own.shape
    width = stream.shape[1]
    weight = full_spec((width, cols))
    return call(
        after_cross_kernel,
        (shape((rows, width), F32), shape((rows, width), BF16)),
        flops=4 * rows * width * cols,
        bytes_accessed=12 * rows * width,
        grid=(rows // BLOCK,),
        in_specs=[
            rows_spec(width), rows_spec(cols), rows_spec(cols), weight, weight, full_spec((1, width)), full_spec((1, width)),
        ],
        out_specs=(rows_spec(width), rows_spec(width)),
    )(stream, own, other, wo, wp, gain, shift)


def feed_kernel(where_ref, a_ref, e_ref, up_ref, down_ref, h_ref, du_ref, out_ref, r_ref, out_acc, r_acc):
    step = pl.program_id(0)

    @pl.when(step == 0)
    def _():
        out_acc[...] = jnp.zeros_like(out_acc)
        r_acc[...] = jnp.zeros_like(r_acc)

    up = up_ref[...]
    down = down_ref[...]
    rows = a_ref.shape[0]
    for first in range(0, rows, BLOCK):
        at = slice(first, first + BLOCK)
        u = dot(a_ref[at], up)
        square = u * u
        inner = 0.7978845608028654 * u * (1.0 + 0.044715 * square)
        curve = jnp.tanh(inner)
        half = 0.5 * (1.0 + curve)
        h = (u * half).astype(BF16)
        slope = half + 0.5 * u * (1.0 - curve * curve) * (0.7978845608028654 * (1.0 + 0.134145 * square))
        du = (dot_nt(e_ref[at], down) * slope).astype(BF16)
        h_ref[at] = h
        du_ref[at] = du
        out_acc[at] += dot(h, down)
        r_acc[at] += dot_nt(du, up)

    @pl.when(step == pl.num_programs(0) - 1)
    def _():
        out_ref[...] = out_acc[...].astype(out_ref.dtype)
        r_ref[...] = r_acc[...].astype(r_ref.dtype)


def feed(where, a, e, up, down, dtype, chunk=512):
    rows, width = a.shape
    hidden = up.shape[1]
    return call(
        feed_kernel,
        (shape((rows, hidden), BF16),) * 2 + (shape((rows, width), dtype),) * 2,
        flops=8 * rows * width * hidden,
        bytes_accessed=4 * hidden * width,
        scalars=1,
        grid=(hidden // chunk,),
        in_specs=[
            full_spec((rows, width)),
            pl.BlockSpec((rows, width), lambda i, w: (w[0], 0)),
            pl.BlockSpec((width, chunk), lambda i, w: (0, i)),
            pl.BlockSpec((chunk, width), lambda i, w: (i, 0)),
        ],
        out_specs=(pl.BlockSpec((rows, chunk), lambda i, w: (0, i)),) * 2 + (full_spec((rows, width)),) * 2,
        scratch=[pltpu.VMEM((rows, width), F32)] * 2,
    )(where, a, e, up, down)


def grad_into_heads(e, weight):
    half = weight.shape[1]
    return (dot_nt(e[:, :half], weight[:half]) + dot_nt(e[:, half:], weight[half:])).astype(BF16)


def add_rows(ref, value):
    total = jnp.sum(value, 0, keepdims=True)

    @pl.when(pl.program_id(0) == 0)
    def _():
        ref[...] = total

    @pl.when(pl.program_id(0) > 0)
    def _():
        ref[...] += total


def after_feed_kernel(
    where_ref, s_ref, r_ref, recv_ref, e_ref, gain_ref, wo_ref, wp_ref, g_ref, eb_ref, own_ref, other_ref, dgain_ref, dshift_ref
):
    unit, rstd = normalise(s_ref[...])
    cotangent = r_ref[...] + recv_ref[...].astype(F32)
    add_rows(dgain_ref, cotangent * unit)
    add_rows(dshift_ref, cotangent)
    grad = e_ref[...].astype(F32) + norm_backward(unit, rstd, gain_ref[...], cotangent)
    g_ref[...] = grad
    e = grad.astype(BF16)
    eb_ref[...] = e
    own_ref[...] = grad_into_heads(e, wo_ref[...])
    other_ref[...] = grad_into_heads(e, wp_ref[...])


def after_feed(where, stream, kept, received, e, gain, wo, wp):
    rows, width = stream.shape
    cols = wo.shape[1]
    weight = full_spec((width, cols))
    vector = full_spec((1, width))
    return call(
        after_feed_kernel,
        (shape((rows, width), F32), shape((rows, width), BF16)) + (shape((rows, cols), BF16),) * 2
        + (shape((1, width), F32),) * 2,
        flops=4 * rows * width * cols,
        bytes_accessed=16 * rows * width,
        scalars=1,
        grid=(rows // BLOCK,),
        in_specs=[
            rows_spec(width), rows_spec(width), rows_spec(width),
            pl.BlockSpec((BLOCK, width), lambda i, w: (i + w[0], 0)), vector, weight, weight,
        ],
        out_specs=(rows_spec(width), rows_spec(width), rows_spec(cols), rows_spec(cols), vector, vector),
    )(where, stream, kept, received, e, gain, wo, wp)


def after_cross_back_kernel(
    s_ref, g_ref, dq_ref, dr_ref, wq_ref, wr_ref, gain_ref, wo_ref, wp_ref, out_ref, eb_ref, own_ref, other_ref, dgain_ref, dshift_ref
):
    unit, rstd = normalise(s_ref[...])
    cotangent = dot_nt(dq_ref[...], wq_ref[...]) + dot_nt(dr_ref[...], wr_ref[...])
    add_rows(dgain_ref, cotangent * unit)
    add_rows(dshift_ref, cotangent)
    grad = g_ref[...] + norm_backward(unit, rstd, gain_ref[...], cotangent)
    out_ref[...] = grad
    e = grad.astype(BF16)
    eb_ref[...] = e
    own_ref[...] = grad_into_heads(e, wo_ref[...])
    other_ref[...] = grad_into_heads(e, wp_ref[...])


def after_cross_back(stream, grad, dq, dr, wq, wr, gain, wo, wp):
    rows, width = stream.shape
    cols = wo.shape[1]
    weight = full_spec((width, cols))
    vector = full_spec((1, width))
    return call(
        after_cross_back_kernel,
        (shape((rows, width), F32), shape((rows, width), BF16)) + (shape((rows, cols), BF16),) * 2
        + (shape((1, width), F32),) * 2,
        flops=8 * rows * width * cols,
        bytes_accessed=16 * rows * width,
        grid=(rows // BLOCK,),
        in_specs=[
            rows_spec(width), rows_spec(width), rows_spec(cols), rows_spec(cols), weight, weight, vector, weight, weight,
        ],
        out_specs=(rows_spec(width), rows_spec(width), rows_spec(cols), rows_spec(cols), vector, vector),
    )(stream, grad, dq, dr, wq, wr, gain, wo, wp)


def key_value_back_kernel(
    half, with_queries, where_ref, dk_ref, dv_ref, dm_ref, dw_ref, wk_ref, wv_ref, wm_ref, ww_ref, *refs
):
    step = pl.program_id(0)
    total = (
        dot_nt(dk_ref[...], wk_ref[...]) + dot_nt(dv_ref[...], wv_ref[...])
        + dot_nt(dm_ref[...], wm_ref[...]) + dot_nt(dw_ref[...], ww_ref[...])
    )
    if with_queries:
        dq_ref, dr_ref, wq_ref, wr_ref, x_ref, send_ref, keep_ref, dgain_ref, dshift_ref, tot_ref = refs
    else:
        send_ref, keep_ref, tot_ref = refs
    tot_ref[...] = total

    @pl.when(step < half)
    def _():
        send_ref[...] = tot_ref[...].astype(BF16)

    @pl.when(step >= half)
    def _():
        if with_queries:
            tot_ref[...] += dot_nt(dq_ref[...], wq_ref[...]) + dot_nt(dr_ref[...], wr_ref[...])
        keep_ref[...] = tot_ref[...]

    if with_queries:
        unit, _ = normalise(x_ref[...].astype(F32))
        cotangent = tot_ref[...]
        add_rows(dgain_ref, cotangent * unit)
        add_rows(dshift_ref, cotangent)


def key_value_back(where, dk, dv, dm, dw, wk, wv, wm, ww, queries=None):
    rows, cols = dk.shape
    width = wk.shape[0]
    blocks = rows // BLOCK
    half = blocks // 2
    weight = full_spec((width, cols))
    vector = full_spec((1, width))
    turned = lambda i, w: (lax.rem(i + half - w[0] + blocks, blocks), 0)
    grads = pl.BlockSpec((BLOCK, cols), turned)
    late = lambda i, w: (jnp.maximum(i - half, 0), 0)
    in_specs = [grads] * 4 + [weight] * 4
    out_shapes = (shape((rows // 2, width), BF16), shape((rows // 2, width), F32))
    out_specs = (
        pl.BlockSpec((BLOCK, width), lambda i, w: (jnp.minimum(i, half - 1), 0)),
        pl.BlockSpec((BLOCK, width), late),
    )
    operands = (dk, dv, dm, dw, wk, wv, wm, ww)
    if queries is not None:
        in_specs += [pl.BlockSpec((BLOCK, cols), late)] * 2 + [weight] * 2 + [pl.BlockSpec((BLOCK, width), turned)]
        out_shapes += (shape((1, width), F32),) * 2
        out_specs += (vector, vector)
        operands += queries
    return call(
        partial(key_value_back_kernel, half, queries is not None),
        out_shapes,
        flops=10 * rows * width * cols,
        bytes_accessed=12 * rows * width,
        scalars=1,
        grid=(blocks,),
        in_specs=in_specs,
        out_specs=out_specs,
        scratch=[pltpu.VMEM((BLOCK, width), F32)],
    )(where, *operands)


def input_grad_kernel(where_ref, x_ref, g_ref, keep_ref, recv_ref, gain_ref, out_ref):
    unit, rstd = normalise(x_ref[...].astype(F32))
    cotangent = keep_ref[...] + recv_ref[...].astype(F32)
    out_ref[...] = g_ref[...] + norm_backward(unit, rstd, gain_ref[...], cotangent)


def input_grad(where, x, grad, kept, received, gain):
    rows, width = grad.shape
    return call(
        input_grad_kernel,
        shape((rows, width), F32),
        flops=rows * width * 20,
        bytes_accessed=16 * rows * width,
        scalars=1,
        grid=(rows // BLOCK,),
        in_specs=[pl.BlockSpec((BLOCK, width), lambda i, w: (i + w[0], 0))] + [rows_spec(width)] * 3 + [full_spec((1, width))],
        out_specs=rows_spec(width),
    )(where, x, grad, kept, received, gain)


def bit_reversed(number, bits):
    turned = 0
    for bit in range(bits):
        turned |= ((number >> bit) & 1) << (bits - 1 - bit)
    return turned


def store_parts(product, keep, send, core, parts):
    bits = parts.bit_length() - 1
    rows = product.shape[0] // parts
    product = product.astype(BF16)

    def write(target, wanted):
        for number in range(parts // 2):
            block = bit_reversed(number, bits - 1) * 2 + wanted
            target(number * rows, rows, product[block * rows : (block + 1) * rows])

    for value in (0, 1):
        @pl.when(core == value)
        def _():
            write(keep, value)
            write(send, 1 - value)


def attention_grads_kernel(
    parts, where_ref, wide_ref, a_ref, e_ref,
    dq0, dk0, dv0, o0, dq1, dk1, dv1, o1, keep_ref, send_ref,
):
    core = where_ref[0]
    cols = dq0.shape[1]
    for group, ys in enumerate(((dq0, dk0, dv0, o0), (dq1, dk1, dv1, o1))):
        for number, (left, right) in enumerate(((a_ref, ys[0]), (wide_ref, ys[1]), (wide_ref, ys[2]), (e_ref, ys[3]))):
            columns = slice(number * cols, (number + 1) * cols)

            def target(ref):
                def put(first, count, value):
                    ref[group, first : first + count, columns] = value

                return put

            store_parts(dot_tn(left[...], right[...]), target(keep_ref), target(send_ref), core, parts)


def attention_grads(core, parts, wide, a, e, own, other):
    width = a.shape[1]
    cols = own[0].shape[1]
    whole = pl.BlockSpec(memory_space=pltpu.VMEM)
    out = shape((2, width // 2, 4 * cols), BF16)
    return call(
        partial(attention_grads_kernel, parts),
        (out, out),
        flops=4 * width * cols * (2 * a.shape[0] + 2 * wide.shape[0]),
        bytes_accessed=12e6,
        in_specs=[pl.BlockSpec(memory_space=pltpu.SMEM)] + [whole] * 11,
    )(core, wide, a, e, *own, *other)


def feed_grads_kernel(parts, half, where_ref, a0, a1, e_ref, du0, du1, h0, h1, keep_ref, send_ref):
    step = pl.program_id(0)
    core = where_ref[0]
    rows = a0.shape[0]

    def target(ref):
        def put(first, count, value):
            ref[first : first + count, :] = value

        return put

    @pl.when(step < half)
    def _():
        product = dot_tn(a0[...], du0[...]) + dot_tn(a1[...], du1[...])
        store_parts(product, target(keep_ref), target(send_ref), core, parts)

    @pl.when(step >= half)
    def _():
        mine = pl.ds(pl.multiple_of(where_ref[1] * rows, rows), rows)
        theirs = pl.ds(pl.multiple_of((1 - where_ref[1]) * rows, rows), rows)
        product = dot_tn(e_ref[mine, :], h0[...]) + dot_tn(e_ref[theirs, :], h1[...])
        store_parts(product, target(keep_ref), target(send_ref), core, parts)


def feed_grads(where, parts, a0, a1, e, du0, du1, h0, h1, chunk=512):
    rows, width = a0.shape
    hidden = du0.shape[1]
    half = hidden // chunk
    out = shape((width // 2, 2 * hidden), BF16)
    first = pl.BlockSpec((rows, chunk), lambda i, w: (0, jnp.minimum(i, half - 1)))
    second = pl.BlockSpec((rows, chunk), lambda i, w: (0, jnp.maximum(i - half, 0)))
    return call(
        partial(feed_grads_kernel, parts, half),
        (out, out),
        flops=8 * rows * width * hidden,
        bytes_accessed=16e6,
        scalars=1,
        grid=(2 * half,),
        in_specs=[full_spec((rows, width))] * 2 + [full_spec((2 * rows, width))] + [first] * 2 + [second] * 2,
        out_specs=(pl.BlockSpec((width // 2, chunk), lambda i, w: (0, i)),) * 2,
    )(where, a0, a1, e, du0, du1, h0, h1)


def swap_tensor(value):
    return lax.ppermute(value, "tensor", [(0, 1), (1, 0)])


def swap_dp(value, bit):
    count = lax.axis_size("dp")
    return lax.ppermute(value, "dp", [(number, number ^ (1 << bit)) for number in range(count)])


def fetch_group(tensors, place):
    part = place % 4
    first = swap_tensor(lax.select_n(part, *tensors))
    second = swap_dp(first, 1)
    third = swap_dp(first, 0)
    fourth = swap_dp(second, 0)
    pieces = (first, third, second, fourth)
    return tuple(lax.select_n(part ^ number, *pieces) for number in range(4))


def halve(value, bit, place, axis):
    length = value.shape[axis] // 2
    mine = (place >> bit) & 1
    sent = lax.dynamic_slice_in_dim(value, (1 - mine) * length, length, axis)
    kept = lax.dynamic_slice_in_dim(value, mine * length, length, axis)
    return add(kept, swap_dp(sent, bit))


def add(left, right):
    return (left.astype(F32) + right.astype(F32)).astype(BF16)


def shards(
    target_tokens, memory_tokens, output_grad, target_segments, memory_segments,
    norm1_gain, norm1_shift, self_query, self_key, self_value, self_out,
    norm2_gain, norm2_shift, cross_query, cross_key, cross_value, cross_out,
    norm3_gain, norm3_shift, ffn_up, ffn_down,
):
    _, length, width = target_tokens.shape
    share = length // 2
    cols = self_query.shape[1]
    parts = lax.axis_size("dp")
    bits = parts.bit_length() - 1
    place = lax.axis_index("dp")
    side = lax.axis_index("tensor")
    core = place & 1
    x = target_tokens[0]
    memory = memory_tokens[0]
    e3 = output_grad[0]
    vectors = [v.reshape(1, width) for v in (norm1_gain, norm1_shift, norm2_gain, norm2_shift, norm3_gain, norm3_shift)]
    g1, b1, g2, b2, g3, b3 = vectors

    def folded(weight):
        return jnp.concatenate([weight[:, :cols], weight[:, cols:]], axis=0)

    self_own = (self_query, self_key, self_value, folded(self_out))
    cross_own = (cross_query, cross_key, cross_value, folded(cross_out))
    self_other = fetch_group(self_own, place)
    cross_other = fetch_group(cross_own, place)

    numbers = jnp.arange(DOCS + 1)[:, None]
    target_starts = jnp.sum(target_segments < numbers, 1).astype(jnp.int32)
    memory_starts = jnp.sum(memory_segments < numbers, 1).astype(jnp.int32)
    self_starts = jnp.stack([target_starts, target_starts])
    cross_starts = jnp.stack([target_starts, memory_starts])
    lane = jnp.arange(128) % 64
    hot = target_segments[0][:, None] == lane[None, :]
    doc_rows = jnp.where(hot, LOW, 0.0).astype(BF16)
    doc_target = jnp.where((lane < DOCS)[None, :] & ~hot, 1.0, 0.0).astype(BF16)
    doc_memory = jnp.where(
        (lane < DOCS)[None, :] & (memory_segments[0][:, None] != lane[None, :]), 1.0, 0.0
    ).astype(BF16)
    own_blocks = share // BLOCK
    block_at = (side * own_blocks).astype(jnp.int32)
    where_self = jnp.stack([block_at, block_at])
    where_cross = jnp.stack([block_at, jnp.zeros((), jnp.int32)])
    where_block = block_at.reshape(1)

    a1, q_own, k_own, v_own = norm_project(x, g1, b1, *self_own[:3])
    o1_own, qa1_own = attend(where_self, self_starts, q_own, k_own, v_own, doc_rows, doc_target, share, True)
    k2_own, v2_own = (dot(memory, w).astype(BF16) for w in cross_own[1:3])
    q_oth, k_oth, v_oth = (dot(a1, w).astype(BF16) for w in self_other[:3])
    o1_oth, qa1_oth = attend(where_self, self_starts, q_oth, k_oth, v_oth, doc_rows, doc_target, share, True)
    stream1, a2, q2_own, q2_oth = after_self(
        where_block, x, o1_own, o1_oth, self_own[3], self_other[3], g2, b2, cross_own[0], cross_other[0]
    )
    o2_own, qa2_own = attend(where_cross, cross_starts, q2_own, k2_own, v2_own, doc_rows, doc_memory, share, False)
    k2_oth, v2_oth = (dot(memory, w).astype(BF16) for w in cross_other[1:3])
    o2_oth, qa2_oth = attend(where_cross, cross_starts, q2_oth, k2_oth, v2_oth, doc_rows, doc_memory, share, False)
    stream2, a3 = after_cross(stream1, o2_own, o2_oth, cross_own[3], cross_other[3], g3, b3)

    a3_oth = swap_tensor(a3)
    side_one = side.astype(jnp.int32).reshape(1)
    h_own, du_own, out_own, r3_own = feed(side_one, a3, e3, ffn_up, ffn_down, F32)
    h_oth, du_oth, out_oth, r3_oth = feed(1 - side_one, a3_oth, e3, ffn_up, ffn_down, BF16)
    r3_recv = swap_tensor(r3_oth)
    out_recv = swap_tensor(out_oth)
    aligned = (width // parts) % 16 == 0
    static_parts = parts if aligned else 2
    core_side = jnp.stack([core, side]).astype(jnp.int32)
    keep_f, send_f = feed_grads(core_side, static_parts, a3, a3_oth, e3, du_own, du_oth, h_own, h_oth)
    layer_output = (stream2 + out_own + out_recv.astype(F32)).astype(BF16)

    def reordered(keep, send):
        if aligned:
            return keep, send
        whole = jnp.where(core == 0, jnp.stack([keep, send]), jnp.stack([send, keep]))
        axis = whole.ndim - 2
        rows = width // parts
        flat = jnp.moveaxis(whole, 0, axis - 1)
        flat = flat.reshape(flat.shape[: axis - 1] + (parts, rows, flat.shape[-1]))
        order = [bit_reversed(number, bits) for number in range(parts)]
        flat = jnp.take(flat, jnp.array(order), axis=axis - 1)
        flat = flat.reshape(flat.shape[: axis - 1] + (2, width // 2, flat.shape[-1]))
        pick = lambda index: lax.dynamic_index_in_dim(flat, index, axis - 1, False)
        return pick(core), pick(1 - core)

    def reduce_core(keep, send):
        keep, send = reordered(keep, send)
        return add(keep, swap_dp(send, 0))

    sum_f = reduce_core(keep_f, send_f)
    for bit in range(1, bits):
        sum_f = halve(sum_f, bit, place, 0)

    grad2, e2, do2_own, do2_oth, dg3, db3 = after_feed(
        where_block, stream2, r3_own, r3_recv, e3, g3, cross_own[3], cross_other[3]
    )
    dq2_own, dk2_own, dv2_own = attend_back(
        where_cross, cross_starts, qa2_own, k2_own, v2_own, do2_own, o2_own, doc_memory, False
    )
    dq2_oth, dk2_oth, dv2_oth = attend_back(
        where_cross, cross_starts, qa2_oth, k2_oth, v2_oth, do2_oth, o2_oth, doc_memory, False
    )
    grad1, e1, do1_own, do1_oth, dg2, db2 = after_cross_back(
        stream1, grad2, dq2_own, dq2_oth, cross_own[0], cross_other[0], g2, self_own[3], self_other[3]
    )
    core_one = core.astype(jnp.int32).reshape(1)
    keep_c, send_c = attention_grads(
        core_one, static_parts, memory, a2, e2,
        (dq2_own, dk2_own, dv2_own, o2_own), (dq2_oth, dk2_oth, dv2_oth, o2_oth),
    )
    sum_c = reduce_core(keep_c, send_c)
    sum_c = add(sum_c[0], swap_tensor(sum_c[1]))
    for bit in range(1, bits):
        sum_c = halve(sum_c, bit, place, 0)
    send_m, keep_m = key_value_back(
        where_block, dk2_own, dv2_own, dk2_oth, dv2_oth, cross_own[1], cross_own[2], cross_other[1], cross_other[2]
    )
    grad_memory = keep_m + swap_tensor(send_m).astype(F32)

    dq1_own, dk1_own, dv1_own = attend_back(
        where_self, self_starts, qa1_own, k_own, v_own, do1_own, o1_own, doc_target, True
    )
    dq1_oth, dk1_oth, dv1_oth = attend_back(
        where_self, self_starts, qa1_oth, k_oth, v_oth, do1_oth, o1_oth, doc_target, True
    )
    send_r, keep_r, dg1, db1 = key_value_back(
        where_block, dk1_own, dv1_own, dk1_oth, dv1_oth, self_own[1], self_own[2], self_other[1], self_other[2],
        (dq1_own, dq1_oth, self_own[0], self_other[0], x),
    )
    recv_r = swap_tensor(send_r)
    a1_mine = lax.dynamic_slice_in_dim(a1, side * share, share, 0)
    keep_s, send_s = attention_grads(
        core_one, static_parts, a1, a1_mine, e1,
        (dq1_own, dk1_own, dv1_own, o1_own), (dq1_oth, dk1_oth, dv1_oth, o1_oth),
    )
    sum_s = reduce_core(keep_s, send_s)
    sum_s = halve(sum_s, 1, place, 1)
    sum_s = add(sum_s[0], swap_tensor(sum_s[1]))
    for bit in range(2, bits):
        sum_s = halve(sum_s, bit, place, 0)
    grad_x = input_grad(where_block, x, grad1, keep_r, recv_r, g1)

    norms = jnp.concatenate([dg1, db1, dg2, db2, dg3, db3], axis=0)
    norms = norms + swap_tensor(norms)
    for bit in range(bits):
        norms = norms + swap_dp(norms, bit)

    def four(total):
        pieces = [total[:, number * cols : (number + 1) * cols].astype(F32) for number in range(4)]
        return tuple(pieces[:3]) + (pieces[3].T,)

    hidden = ffn_up.shape[1]
    return (
        (layer_output[None], grad_x[None], grad_memory[None])
        + four(sum_s)
        + four(sum_c)
        + (sum_f[:, :hidden].astype(F32), sum_f[:, hidden:].astype(F32).T)
        + tuple(norms[number] for number in range(6))
    )


def solution(mesh):
    tokens = P("dp", None, None)
    columns = P(None, "tensor")
    rows = P("tensor", None)
    block = (P(), P(), columns, columns, columns, rows)
    in_specs = (tokens,) * 3 + (P("dp", None),) * 2 + block + block + (P(), P(), columns, rows)
    out_rows = P("dp", "tensor")
    out_cols = P("tensor", "dp")
    four = (out_rows, out_rows, out_rows, out_cols)
    out_specs = (P("dp", "tensor", None),) * 3 + four + four + (out_rows, out_cols) + (P(),) * 6
    return jax.shard_map(shards, mesh=mesh, in_specs=in_specs, out_specs=out_specs, check_vma=False)
```

```python
from functools import partial

import jax
import jax.numpy as jnp
from jax import lax
from jax.experimental import pallas as pl
from jax.experimental.pallas import tpu as pltpu
from jax.sharding import PartitionSpec as P

HEAD_DIM = 64
DOCS = 4
BLOCK = 256
LOW = -1e30
F32 = jnp.float32
BF16 = jnp.bfloat16
MIB = 1024 * 1024


def dot(left, right):
    return jnp.dot(left, right, preferred_element_type=F32)


def dot_nt(left, right):
    return lax.dot_general(left, right, (((1,), (1,)), ((), ())), preferred_element_type=F32)


def dot_tn(left, right):
    return lax.dot_general(left, right, (((0,), (0,)), ((), ())), preferred_element_type=F32)


def normalise(values):
    centered = values - jnp.mean(values, -1, keepdims=True)
    rstd = lax.rsqrt(jnp.mean(centered * centered, -1, keepdims=True) + 1e-05)
    return centered * rstd, rstd


def norm_backward(unit, rstd, gain, cotangent):
    scaled = cotangent * gain
    return rstd * (
        scaled
        - jnp.mean(scaled, -1, keepdims=True)
        - unit * jnp.mean(scaled * unit, -1, keepdims=True)
    )


def call(kernel, out_shape, *, flops, bytes_accessed, limit=16, scratch=(), scalars=1):
    def run(*operands):
        whole = pl.BlockSpec(memory_space=pltpu.VMEM)
        small = pl.BlockSpec(memory_space=pltpu.SMEM)
        return pl.pallas_call(
            kernel,
            out_shape=out_shape,
            in_specs=[small] * scalars + [whole] * (len(operands) - scalars),
            out_specs=jax.tree.map(lambda _: whole, out_shape),
            scratch_shapes=scratch,
            compiler_params=pltpu.CompilerParams(vmem_limit_bytes=limit * MIB),
            cost_estimate=pl.CostEstimate(
                flops=int(flops), bytes_accessed=int(bytes_accessed), transcendentals=0
            ),
        )(*operands)

    return run


def shape(dims, dtype):
    return jax.ShapeDtypeStruct(dims, dtype)


def full_spec(dims):
    return pl.BlockSpec(dims, lambda *_: (0,) * len(dims))


def row_blocks(rows):
    return [slice(first, first + BLOCK) for first in range(0, rows, BLOCK)]


def own_half(side, rows, first=0, count=None):
    count = rows if count is None else count
    return pl.ds(pl.multiple_of(side * rows + first, BLOCK), count)


def vector(ref, number):
    return ref[number : number + 1, :]


def norm_project_kernel(where_ref, x_ref, norms_ref, wq_ref, wkv_ref, a_ref, q_ref, kv_ref):
    for at in row_blocks(x_ref.shape[0]):
        unit, _ = normalise(x_ref[at].astype(F32))
        a_ref[at] = (unit * vector(norms_ref, 0) + vector(norms_ref, 1)).astype(BF16)
    rows = q_ref.shape[0]
    q_ref[...] = dot(a_ref[own_half(where_ref[0], rows), :], wq_ref[...]).astype(BF16)
    for at in row_blocks(x_ref.shape[0]):
        kv_ref[at] = dot(a_ref[at], wkv_ref[...]).astype(BF16)


def norm_project(side, x, norms, wq, wkv):
    rows, width = x.shape
    cols = wq.shape[1]
    return call(
        norm_project_kernel,
        (shape((rows, width), BF16), shape((rows // 2, cols), BF16), shape((rows, 2 * cols), BF16)),
        flops=5 * rows * width * cols,
        bytes_accessed=4 * rows * width,
    )(side, x, norms, wq, wkv)


def project_kernel(where_ref, a_ref, wq_ref, wkv_ref, q_ref, kv_ref):
    q_ref[...] = dot(a_ref[own_half(where_ref[0], q_ref.shape[0]), :], wq_ref[...]).astype(BF16)
    for at in row_blocks(a_ref.shape[0]):
        kv_ref[at] = dot(a_ref[at], wkv_ref[...]).astype(BF16)


def project(side, a, wq, wkv):
    rows, width = a.shape
    cols = wq.shape[1]
    return call(
        project_kernel,
        (shape((rows // 2, cols), BF16), shape((rows, 2 * cols), BF16)),
        flops=5 * rows * width * cols,
        bytes_accessed=4 * rows * width,
    )(side, a, wq, wkv)


def project_memory_kernel(a_ref, wkv_ref, kv_ref):
    for at in row_blocks(a_ref.shape[0]):
        kv_ref[at] = dot(a_ref[at], wkv_ref[...]).astype(BF16)


def project_memory(memory, wkv):
    rows, width = memory.shape
    return call(
        project_memory_kernel,
        shape((rows, wkv.shape[1]), BF16),
        flops=2 * rows * width * wkv.shape[1],
        bytes_accessed=4 * rows * width,
        scalars=0,
    )(memory, wkv)


def first_doc(starts_ref, row):
    doc = 0
    for number in range(1, DOCS):
        doc = doc + (starts_ref[0, number] <= row).astype(jnp.int32)
    return doc


def key_range(starts_ref, block_number, causal):
    first = block_number * BLOCK
    low = starts_ref[1, first_doc(starts_ref, first)]
    if causal:
        return low // BLOCK, block_number
    high = starts_ref[1, first_doc(starts_ref, first + BLOCK - 1) + 1]
    return low // BLOCK, (high + BLOCK - 1) // BLOCK


def lanes(rows):
    return lax.broadcasted_iota(jnp.int32, (rows, 128), 1)


def causal_mask():
    keys = lax.broadcasted_iota(jnp.int32, (BLOCK, BLOCK), 0)
    rows = lax.broadcasted_iota(jnp.int32, (BLOCK, BLOCK), 1)
    return keys <= rows


def pair_of(ref, pair, rows=slice(None)):
    return ref[rows, pair * 128 : (pair + 1) * 128]


def half_of(head):
    return slice(64 * (head % 2), 64 * (head % 2) + 64)


def in_three(value, place, otherwise):
    high = value.astype(BF16)
    rest = value - high.astype(F32)
    middle = rest.astype(BF16)
    low = (rest - middle.astype(F32)).astype(BF16)
    return jnp.where(place == 4, high, jnp.where(place == 5, middle, jnp.where(place == 6, low, otherwise)))


def walk_keys(starts_ref, block_number, causal, one_block):
    low, high = key_range(starts_ref, block_number, causal)
    if causal:
        one_block(block_number, causal_mask())
    lax.fori_loop(low, high, lambda number, _: (one_block(number, None), 0)[1], 0)


def attend_kernel(
    causal, heads, group, where_ref, starts_ref, q_ref, kv_ref, docs_ref, dock_ref, o_ref, qa_ref,
    ka_ref, vt_ref, qs_ref, acc_ref, max_ref,
):
    keys = kv_ref.shape[0]
    pairs = heads // 2
    left = lanes(keys) < 64
    for pair in range(pairs):
        turned = pair_of(kv_ref, pairs + pair).T
        for head in (2 * pair, 2 * pair + 1):
            mine = left if head % 2 == 0 else ~left
            ka_ref[head] = jnp.where(mine, pair_of(kv_ref, pair), dock_ref[...])
            vt_ref[head, :64] = turned[half_of(head)]
            vt_ref[head, 64:] = jnp.ones((16, keys), BF16)
    left = lanes(BLOCK) < 64
    place = lanes(BLOCK) % 64

    def one_step(step, _):
        at_rows = pl.ds(pl.multiple_of(step * BLOCK, BLOCK), BLOCK)
        block_number = where_ref[0] * (q_ref.shape[0] // BLOCK) + step
        docs = docs_ref[pl.ds(pl.multiple_of(block_number * BLOCK, BLOCK), BLOCK), :]
        for head in range(heads):
            mine = left if head % 2 == 0 else ~left
            scaled = pair_of(q_ref, head // 2, at_rows) * jnp.array(HEAD_DIM**-0.5, BF16)
            qs_ref[head] = jnp.where(mine, scaled, docs)
        max_ref[...] = jnp.full_like(max_ref, LOW)
        acc_ref[...] = jnp.zeros_like(acc_ref)

        def one_block(number, mask):
            at = pl.ds(pl.multiple_of(number * BLOCK, BLOCK), BLOCK)
            for first in range(0, heads, group):
                some = range(first, first + group)
                scores = [dot_nt(ka_ref[head, at, :], qs_ref[head]) for head in some]
                if mask is not None:
                    scores = [jnp.where(mask, score, LOW) for score in scores]
                old = [max_ref[head, 0:1] for head in some]
                new = [jnp.maximum(m, jnp.max(score, 0, keepdims=True)) for m, score in zip(old, scores)]
                weights = [jnp.exp(score - m).astype(BF16) for score, m in zip(scores, new)]
                mixed = [dot(vt_ref[head, :, at], weight) for head, weight in zip(some, weights)]
                shrink = [jnp.exp(m - n) for m, n in zip(old, new)]
                for number_in, head in enumerate(some):
                    acc_ref[head] = acc_ref[head] * shrink[number_in] + mixed[number_in]
                    max_ref[head, 0:1] = new[number_in]

        walk_keys(starts_ref, block_number, causal, one_block)
        for pair in range(pairs):
            both = []
            for head in (2 * pair, 2 * pair + 1):
                mine = left if head % 2 == 0 else ~left
                acc = acc_ref[head]
                total = acc[64:65]
                both.append(acc[:64] / total)
                lse = max_ref[head, 0:1] + jnp.log(total)
                column = jnp.broadcast_to(-lse, (128, BLOCK)).T
                qa_ref[head, at_rows, :] = jnp.where(mine, qs_ref[head], in_three(column, place, docs))
            o_ref[at_rows, pair * 128 : (pair + 1) * 128] = jnp.concatenate(both, 0).T.astype(BF16)
        return 0

    lax.fori_loop(0, q_ref.shape[0] // BLOCK, one_step, 0)


def attend(side, starts, q, kv, doc_rows, doc_keys, causal):
    rows, cols = q.shape
    heads = cols // HEAD_DIM
    keys = kv.shape[0]
    return call(
        partial(attend_kernel, causal, heads, heads),
        (shape((rows, cols), BF16), shape((heads, rows, 128), BF16)),
        flops=16 * rows * keys * cols,
        bytes_accessed=8 * keys * cols,
        scalars=2,
        limit=20,
        scratch=[
            pltpu.VMEM((heads, keys, 128), BF16),
            pltpu.VMEM((heads, 80, keys), BF16),
            pltpu.VMEM((heads, BLOCK, 128), BF16),
            pltpu.VMEM((heads, 80, BLOCK), F32),
            pltpu.VMEM((heads, 8, BLOCK), F32),
        ],
    )(side, starts, q, kv, doc_rows, doc_keys)


def attend_back_kernel(
    causal, heads, group, where_ref, starts_ref, qa_ref, kv_ref, do_ref, o_ref, dock_ref, dq_ref, dkv_ref,
    ka_ref, va_ref, da_ref, dqa_ref, dka_ref, dva_ref, kt_ref, qt_ref, dt_ref,
):
    keys = kv_ref.shape[0]
    pairs = heads // 2
    left = lanes(keys) < 64
    place = lanes(keys) % 64
    ones = jnp.where((place >= 4) & (place < 7), 1.0, 0.0).astype(BF16)
    for head in range(heads):
        mine = left if head % 2 == 0 else ~left
        ka_ref[head] = jnp.where(mine, pair_of(kv_ref, head // 2), dock_ref[...] + ones)
        va_ref[head] = jnp.where(mine, pair_of(kv_ref, pairs + head // 2), ones)
    for pair in range(pairs):
        kt_ref[pair] = pair_of(kv_ref, pair).T
    dka_ref[...] = jnp.zeros_like(dka_ref)
    dva_ref[...] = jnp.zeros_like(dva_ref)
    left = lanes(BLOCK) < 64
    place = lanes(BLOCK) % 64

    def one_step(step, _):
        at_rows = pl.ds(pl.multiple_of(step * BLOCK, BLOCK), BLOCK)
        block_number = where_ref[0] * (do_ref.shape[0] // BLOCK) + step
        for pair in range(pairs):
            grad = pair_of(do_ref, pair, at_rows)
            dt_ref[pair] = grad.T
            product = grad.astype(F32) * pair_of(o_ref, pair, at_rows).astype(F32)
            for head in (2 * pair, 2 * pair + 1):
                mine = left if head % 2 == 0 else ~left
                delta = -jnp.sum(jnp.where(mine, product, 0.0), -1, keepdims=True)
                delta = jnp.broadcast_to(delta, (BLOCK, 128))
                da_ref[head] = jnp.where(mine, grad, in_three(delta, place, jnp.zeros((), BF16)))
            qt_ref[pair] = jnp.where(left, qa_ref[2 * pair, at_rows, :], qa_ref[2 * pair + 1, at_rows, :]).T
        dqa_ref[...] = jnp.zeros_like(dqa_ref)

        def one_block(number, mask):
            at = pl.ds(pl.multiple_of(number * BLOCK, BLOCK), BLOCK)
            for first in range(0, heads, group):
                some = range(first, first + group)
                scores = [dot_nt(ka_ref[head, at, :], qa_ref[head, at_rows, :]) for head in some]
                grads = [dot_nt(va_ref[head, at, :], da_ref[head]) for head in some]
                if mask is not None:
                    scores = [jnp.where(mask, score, LOW) for score in scores]
                weights = [jnp.exp(score) for score in scores]
                grads = [(weight * grad).astype(BF16) for weight, grad in zip(weights, grads)]
                weights = [weight.astype(BF16) for weight in weights]
                values = [dot_nt(dt_ref[head // 2, half_of(head)], weight) for head, weight in zip(some, weights)]
                kept = [dot_nt(qt_ref[head // 2, half_of(head)], grad) for head, grad in zip(some, grads)]
                asked = [dot(kt_ref[head // 2, half_of(head), at], grad) for head, grad in zip(some, grads)]
                for number_in, head in enumerate(some):
                    dva_ref[head // 2, half_of(head), at] += values[number_in]
                    dka_ref[head // 2, half_of(head), at] += kept[number_in]
                    dqa_ref[head // 2, half_of(head)] += asked[number_in]

        walk_keys(starts_ref, block_number, causal, one_block)
        for pair in range(pairs):
            dq_ref[at_rows, pair * 128 : (pair + 1) * 128] = (dqa_ref[pair].T * HEAD_DIM**-0.5).astype(BF16)
        return 0

    lax.fori_loop(0, do_ref.shape[0] // BLOCK, one_step, 0)
    for pair in range(pairs):
        dkv_ref[:, pair * 128 : (pair + 1) * 128] = dka_ref[pair].astype(BF16).T
        dkv_ref[:, (pairs + pair) * 128 : (pairs + pair + 1) * 128] = dva_ref[pair].astype(BF16).T


def attend_back(side, starts, qa, kv, do, o, doc_keys, causal):
    rows, cols = do.shape
    heads = cols // HEAD_DIM
    keys = kv.shape[0]
    return call(
        partial(attend_back_kernel, causal, heads, heads // 2),
        (shape((rows, cols), BF16), shape((keys, 2 * cols), BF16)),
        flops=40 * rows * keys * cols,
        bytes_accessed=12 * keys * cols,
        scalars=2,
        limit=24,
        scratch=[
            pltpu.VMEM((heads, keys, 128), BF16),
            pltpu.VMEM((heads, keys, 128), BF16),
            pltpu.VMEM((heads, BLOCK, 128), BF16),
            pltpu.VMEM((heads // 2, 128, BLOCK), F32),
            pltpu.VMEM((heads // 2, 128, keys), F32),
            pltpu.VMEM((heads // 2, 128, keys), F32),
            pltpu.VMEM((heads // 2, 128, keys), BF16),
            pltpu.VMEM((heads // 2, 128, BLOCK), BF16),
            pltpu.VMEM((heads // 2, 128, BLOCK), BF16),
        ],
    )(side, starts, qa, kv, do, o, doc_keys)


def out_project(own, other, own_ref, other_ref):
    half = own_ref.shape[1]
    left = dot(own, own_ref[:half]) + dot(other, other_ref[:half])
    right = dot(own, own_ref[half:]) + dot(other, other_ref[half:])
    return jnp.concatenate([left, right], axis=1)


def after_self_kernel(where_ref, x_ref, own_ref, other_ref, wo_ref, wp_ref, norms_ref, wq_ref, wr_ref, s_ref, a_ref, q_ref, r_ref):
    rows = s_ref.shape[0]
    for at in row_blocks(rows):
        start = x_ref[own_half(where_ref[0], rows, at.start, BLOCK), :].astype(F32)
        stream = start + out_project(own_ref[at], other_ref[at], wo_ref, wp_ref)
        s_ref[at] = stream
        unit, _ = normalise(stream)
        a_ref[at] = (unit * vector(norms_ref, 2) + vector(norms_ref, 3)).astype(BF16)
    q_ref[...] = dot(a_ref[...], wq_ref[...]).astype(BF16)
    r_ref[...] = dot(a_ref[...], wr_ref[...]).astype(BF16)


def after_self(side, x, own, other, wo, wp, norms, wq, wr):
    rows, cols = own.shape
    width = x.shape[1]
    return call(
        after_self_kernel,
        (shape((rows, width), F32), shape((rows, width), BF16)) + (shape((rows, cols), BF16),) * 2,
        flops=8 * rows * width * cols,
        bytes_accessed=12 * rows * width,
    )(side, x, own, other, wo, wp, norms, wq, wr)


def after_cross_kernel(s_ref, own_ref, other_ref, wo_ref, wp_ref, norms_ref, t_ref, a_ref):
    for at in row_blocks(s_ref.shape[0]):
        stream = s_ref[at] + out_project(own_ref[at], other_ref[at], wo_ref, wp_ref)
        t_ref[at] = stream
        unit, _ = normalise(stream)
        a_ref[at] = (unit * vector(norms_ref, 4) + vector(norms_ref, 5)).astype(BF16)


def after_cross(stream, own, other, wo, wp, norms):
    rows, cols = own.shape
    width = stream.shape[1]
    return call(
        after_cross_kernel,
        (shape((rows, width), F32), shape((rows, width), BF16)),
        flops=4 * rows * width * cols,
        bytes_accessed=12 * rows * width,
        scalars=0,
    )(stream, own, other, wo, wp, norms)


def feed_kernel(where_ref, a_ref, e_ref, up_ref, down_ref, h_ref, du_ref, out_ref, r_ref, out_acc, r_acc):
    step = pl.program_id(0)

    @pl.when(step == 0)
    def _():
        out_acc[...] = jnp.zeros_like(out_acc)
        r_acc[...] = jnp.zeros_like(r_acc)

    rows = a_ref.shape[0]
    for at in row_blocks(rows):
        u = dot(a_ref[at], up_ref[...])
        dh = dot_nt(e_ref[own_half(where_ref[0], rows, at.start, BLOCK), :], down_ref[...])
        square = u * u
        curve = jnp.tanh(u * (0.7978845608028654 + 0.035677408136300125 * square))
        half = 0.5 + 0.5 * curve
        slope = half + (0.5 * u) * (1.0 - curve * curve) * (0.7978845608028654 + 0.10703222440890037 * square)
        h_ref[at] = (u * half).astype(BF16)
        du_ref[at] = (dh * slope).astype(BF16)
    out_acc[...] += dot(h_ref[...], down_ref[...])
    r_acc[...] += dot_nt(du_ref[...], up_ref[...])

    @pl.when(step == pl.num_programs(0) - 1)
    def _():
        out_ref[...] = out_acc[...].astype(out_ref.dtype)
        r_ref[...] = r_acc[...].astype(r_ref.dtype)


def feed(where, a, e, up, down, dtype, chunk=512):
    rows, width = a.shape
    hidden = up.shape[1]
    whole = full_spec((rows, width))
    return pl.pallas_call(
        feed_kernel,
        out_shape=(shape((rows, hidden), BF16),) * 2 + (shape((rows, width), dtype),) * 2,
        grid=(hidden // chunk,),
        in_specs=[
            pl.BlockSpec(memory_space=pltpu.SMEM), whole, full_spec(e.shape),
            pl.BlockSpec((width, chunk), lambda i: (0, i)), pl.BlockSpec((chunk, width), lambda i: (i, 0)),
        ],
        out_specs=(pl.BlockSpec((rows, chunk), lambda i: (0, i)),) * 2 + (whole,) * 2,
        scratch_shapes=[pltpu.VMEM((rows, width), F32)] * 2,
        compiler_params=pltpu.CompilerParams(vmem_limit_bytes=28 * MIB),
        cost_estimate=pl.CostEstimate(
            flops=8 * rows * width * hidden, bytes_accessed=4 * hidden * width, transcendentals=0
        ),
    )(where, a, e, up, down)


def grad_into_heads(e, weight_ref):
    half = weight_ref.shape[1]
    return (dot_nt(e[:, :half], weight_ref[:half]) + dot_nt(e[:, half:], weight_ref[half:])).astype(BF16)


def add_rows(ref, number, value):
    ref[number : number + 1, :] += jnp.sum(value, 0, keepdims=True)


def after_feed_kernel(where_ref, s_ref, r_ref, recv_ref, e_ref, norms_ref, wo_ref, wp_ref, g_ref, eb_ref, own_ref, other_ref, d_ref):
    rows = s_ref.shape[0]
    d_ref[...] = jnp.zeros_like(d_ref)
    for at in row_blocks(rows):
        unit, rstd = normalise(s_ref[at])
        cotangent = r_ref[at] + recv_ref[at].astype(F32)
        add_rows(d_ref, 0, cotangent * unit)
        add_rows(d_ref, 1, cotangent)
        top = e_ref[own_half(where_ref[0], rows, at.start, BLOCK), :].astype(F32)
        grad = top + norm_backward(unit, rstd, vector(norms_ref, 4), cotangent)
        g_ref[at] = grad
        eb_ref[at] = grad.astype(BF16)
    own_ref[...] = grad_into_heads(eb_ref[...], wo_ref)
    other_ref[...] = grad_into_heads(eb_ref[...], wp_ref)


def after_feed(side, stream, kept, received, e, norms, wo, wp):
    rows, width = stream.shape
    cols = wo.shape[1]
    return call(
        after_feed_kernel,
        (shape((rows, width), F32), shape((rows, width), BF16)) + (shape((rows, cols), BF16),) * 2
        + (shape((2, width), F32),),
        flops=4 * rows * width * cols,
        bytes_accessed=16 * rows * width,
        limit=20,
    )(side, stream, kept, received, e, norms, wo, wp)


def after_cross_back_kernel(
    s_ref, g_ref, dq_ref, dr_ref, wq_ref, wr_ref, norms_ref, wo_ref, wp_ref, out_ref, eb_ref, own_ref, other_ref, d_ref
):
    d_ref[...] = jnp.zeros_like(d_ref)
    for at in row_blocks(s_ref.shape[0]):
        unit, rstd = normalise(s_ref[at])
        cotangent = dot_nt(dq_ref[at], wq_ref[...]) + dot_nt(dr_ref[at], wr_ref[...])
        add_rows(d_ref, 0, cotangent * unit)
        add_rows(d_ref, 1, cotangent)
        grad = g_ref[at] + norm_backward(unit, rstd, vector(norms_ref, 2), cotangent)
        out_ref[at] = grad
        eb_ref[at] = grad.astype(BF16)
    own_ref[...] = grad_into_heads(eb_ref[...], wo_ref)
    other_ref[...] = grad_into_heads(eb_ref[...], wp_ref)


def after_cross_back(stream, grad, dq, dr, wq, wr, norms, wo, wp):
    rows, width = stream.shape
    cols = wo.shape[1]
    return call(
        after_cross_back_kernel,
        (shape((rows, width), F32), shape((rows, width), BF16)) + (shape((rows, cols), BF16),) * 2
        + (shape((2, width), F32),),
        flops=8 * rows * width * cols,
        bytes_accessed=16 * rows * width,
        scalars=0,
        limit=20,
    )(stream, grad, dq, dr, wq, wr, norms, wo, wp)


def key_value_back_kernel(with_queries, where_ref, own_ref, other_ref, wkv_ref, wlw_ref, *refs):
    if with_queries:
        dq_ref, dr_ref, wq_ref, wr_ref, x_ref, send_ref, keep_ref, d_ref = refs
        d_ref[...] = jnp.zeros_like(d_ref)
    else:
        send_ref, keep_ref = refs
    rows = send_ref.shape[0]
    side = where_ref[0]
    for half, target in ((1 - side, send_ref), (side, keep_ref)):
        for at in row_blocks(rows):
            place = own_half(half, rows, at.start, BLOCK)
            total = dot_nt(own_ref[place, :], wkv_ref[...]) + dot_nt(other_ref[place, :], wlw_ref[...])
            if with_queries:
                if target is keep_ref:
                    total += dot_nt(dq_ref[at], wq_ref[...]) + dot_nt(dr_ref[at], wr_ref[...])
                unit, _ = normalise(x_ref[place, :].astype(F32))
                add_rows(d_ref, 0, total * unit)
                add_rows(d_ref, 1, total)
            target[at] = total.astype(target.dtype)


def key_value_back(side, own, other, wkv, wlw, queries=()):
    rows = own.shape[0] // 2
    width = wkv.shape[0]
    cols = wkv.shape[1] // 2
    outs = (shape((rows, width), BF16), shape((rows, width), F32))
    if queries:
        outs += (shape((2, width), F32),)
    return call(
        partial(key_value_back_kernel, len(queries) > 0),
        outs,
        flops=18 * rows * width * cols,
        bytes_accessed=12 * rows * width,
        limit=20,
    )(side, own, other, wkv, wlw, *queries)


def input_grad_kernel(where_ref, x_ref, g_ref, keep_ref, recv_ref, norms_ref, out_ref):
    rows = g_ref.shape[0]
    for at in row_blocks(rows):
        unit, rstd = normalise(x_ref[own_half(where_ref[0], rows, at.start, BLOCK), :].astype(F32))
        cotangent = keep_ref[at] + recv_ref[at].astype(F32)
        out_ref[at] = g_ref[at] + norm_backward(unit, rstd, vector(norms_ref, 0), cotangent)


def input_grad(side, x, grad, kept, received, norms):
    rows, width = grad.shape
    return call(
        input_grad_kernel,
        shape((rows, width), F32),
        flops=rows * width * 20,
        bytes_accessed=16 * rows * width,
    )(side, x, grad, kept, received, norms)


def bit_reversed(number, bits):
    turned = 0
    for bit in range(bits):
        turned |= ((number >> bit) & 1) << (bits - 1 - bit)
    return turned


def store_parts(product, keep, send, core, parts):
    bits = parts.bit_length() - 1
    rows = product.shape[0] // parts
    product = product.astype(BF16)

    def write(target, wanted):
        for number in range(parts // 2):
            block = bit_reversed(number, bits - 1) * 2 + wanted
            target(number * rows, rows, product[block * rows : (block + 1) * rows])

    for value in (0, 1):
        @pl.when(core == value)
        def _():
            write(keep, value)
            write(send, 1 - value)


def put_columns(ref, columns):
    def put(first, count, value):
        ref[first : first + count, columns] = value

    return put


def attention_grads_kernel(parts, where_ref, wide_ref, a_ref, e_ref, dq_ref, dkv_ref, o_ref, keep_ref, send_ref):
    core = where_ref[0]
    cols = dq_ref.shape[1]
    narrow = a_ref[own_half(where_ref[1], dq_ref.shape[0]), :] if a_ref.shape[0] != dq_ref.shape[0] else a_ref[...]
    first = 0
    for left, right in ((narrow, dq_ref), (wide_ref[...], dkv_ref), (e_ref[...], o_ref)):
        columns = slice(first, first + right.shape[1])
        first += right.shape[1]
        product = dot_tn(left, right[...])
        store_parts(product, put_columns(keep_ref, columns), put_columns(send_ref, columns), core, parts)


def attention_grads(core_side, parts, wide, a, e, dq, dkv, o):
    rows, width = e.shape
    cols = dq.shape[1]
    out = shape((width // 2, 4 * cols), BF16)
    return call(
        partial(attention_grads_kernel, parts),
        (out, out),
        flops=2 * width * cols * (2 * rows + 2 * wide.shape[0]),
        bytes_accessed=6e6,
        limit=20,
    )(core_side, wide, a, e, dq, dkv, o)


def feed_grads_kernel(parts, half, where_ref, a0, a1, e_ref, du0, du1, h0, h1, keep_ref, send_ref):
    step = pl.program_id(0)
    core = where_ref[0]
    rows = a0.shape[0]
    put_keep = put_columns(keep_ref, slice(None))
    put_send = put_columns(send_ref, slice(None))

    @pl.when(step < half)
    def _():
        product = dot_tn(a0[...], du0[...]) + dot_tn(a1[...], du1[...])
        store_parts(product, put_keep, put_send, core, parts)

    @pl.when(step >= half)
    def _():
        mine = e_ref[own_half(where_ref[1], rows), :]
        theirs = e_ref[own_half(1 - where_ref[1], rows), :]
        product = dot_tn(mine, h0[...]) + dot_tn(theirs, h1[...])
        store_parts(product, put_keep, put_send, core, parts)


def feed_grads(where, parts, a0, a1, e, du0, du1, h0, h1, chunk=768):
    rows, width = a0.shape
    hidden = du0.shape[1]
    half = hidden // chunk
    out = shape((width // 2, 2 * hidden), BF16)
    first = pl.BlockSpec((rows, chunk), lambda i: (0, jnp.minimum(i, half - 1)))
    second = pl.BlockSpec((rows, chunk), lambda i: (0, jnp.maximum(i - half, 0)))
    return pl.pallas_call(
        partial(feed_grads_kernel, parts, half),
        out_shape=(out, out),
        grid=(2 * half,),
        in_specs=[pl.BlockSpec(memory_space=pltpu.SMEM)] + [full_spec((rows, width))] * 2 + [full_spec((2 * rows, width))]
        + [first] * 2 + [second] * 2,
        out_specs=(pl.BlockSpec((width // 2, chunk), lambda i: (0, i)),) * 2,
        compiler_params=pltpu.CompilerParams(vmem_limit_bytes=28 * MIB),
        cost_estimate=pl.CostEstimate(
            flops=8 * rows * width * hidden, bytes_accessed=16 * MIB, transcendentals=0
        ),
    )(where, a0, a1, e, du0, du1, h0, h1)


def swap_tensor(value):
    return lax.ppermute(value, "tensor", [(0, 1), (1, 0)])


def swap_dp(value, bit):
    count = lax.axis_size("dp")
    return lax.ppermute(value, "dp", [(number, number ^ (1 << bit)) for number in range(count)])


def after(value, *others):
    return lax.optimization_barrier((value,) + others)[0]


def share_group(first, part):
    second = swap_dp(first, 1)
    third = swap_dp(first, 0)
    fourth = swap_dp(second, 0)
    pieces = (first, third, second, fourth)
    q, k, v, o = (lax.select_n(part ^ number, *pieces) for number in range(4))
    return q, jnp.concatenate([k, v], axis=1), o


def halve(value, bit, place, axis=0):
    length = value.shape[axis] // 2
    mine = (place >> bit) & 1
    sent = lax.dynamic_slice_in_dim(value, (1 - mine) * length, length, axis)
    kept = lax.dynamic_slice_in_dim(value, mine * length, length, axis)
    return add(kept, swap_dp(sent, bit))


def add(left, right):
    return (left.astype(F32) + right.astype(F32)).astype(BF16)


def shards(
    target_tokens, memory_tokens, output_grad, target_segments, memory_segments,
    norm1_gain, norm1_shift, self_query, self_key, self_value, self_out,
    norm2_gain, norm2_shift, cross_query, cross_key, cross_value, cross_out,
    norm3_gain, norm3_shift, ffn_up, ffn_down,
):
    _, length, width = target_tokens.shape
    cols = self_query.shape[1]
    parts = lax.axis_size("dp")
    bits = parts.bit_length() - 1
    place = lax.axis_index("dp")
    side = lax.axis_index("tensor")
    core = place & 1
    x = target_tokens[0]
    memory = memory_tokens[0]
    e3 = output_grad[0]
    norms = jnp.stack([norm1_gain, norm1_shift, norm2_gain, norm2_shift, norm3_gain, norm3_shift])
    side_one = side.astype(jnp.int32).reshape(1)
    core_side = jnp.stack([core, side]).astype(jnp.int32)

    def folded(weight):
        return jnp.concatenate([weight[:, :cols], weight[:, cols:]], axis=0)

    part = place % 4
    self_wo = folded(self_out)
    cross_wo = folded(cross_out)
    self_first = swap_tensor(lax.select_n(part, self_query, self_key, self_value, self_wo))
    cross_sent = lax.select_n(part, cross_query, cross_key, cross_value, cross_wo)
    cross_first = swap_tensor(after(cross_sent, self_first))
    self_wq2, self_wkv2, self_wo2 = share_group(self_first, part)
    self_wkv = jnp.concatenate([self_key, self_value], axis=1)
    cross_wkv = jnp.concatenate([cross_key, cross_value], axis=1)

    numbers = jnp.arange(DOCS + 1)[:, None]
    target_starts = jnp.sum(target_segments < numbers, 1).astype(jnp.int32)
    memory_starts = jnp.sum(memory_segments < numbers, 1).astype(jnp.int32)
    self_starts = jnp.stack([target_starts, target_starts])
    cross_starts = jnp.stack([target_starts, memory_starts])
    lane = jnp.arange(128) % 64
    hot = target_segments[0][:, None] == lane[None, :]
    doc_rows = jnp.where(hot, LOW, 0.0).astype(BF16)
    doc_target = jnp.where((lane < DOCS)[None, :] & ~hot, 1.0, 0.0).astype(BF16)
    doc_memory = jnp.where(
        (lane < DOCS)[None, :] & (memory_segments[0][:, None] != lane[None, :]), 1.0, 0.0
    ).astype(BF16)

    a1, q_own, kv_own = norm_project(side_one, x, norms, self_query, self_wkv)
    o1_own, qa1_own = attend(side_one, self_starts, q_own, kv_own, doc_rows, doc_target, True)
    kv2_own = project_memory(memory, cross_wkv)
    q_oth, kv_oth = project(side_one, after(a1, o1_own, kv2_own), self_wq2, self_wkv2)
    o1_oth, qa1_oth = attend(side_one, self_starts, q_oth, kv_oth, doc_rows, doc_target, True)
    cross_wq2, cross_wkv2, cross_wo2 = share_group(after(cross_first, q_oth), part)
    stream1, a2, q2_own, q2_oth = after_self(
        side_one, x, o1_own, o1_oth, self_wo, self_wo2, norms, cross_query, cross_wq2
    )
    o2_own, qa2_own = attend(side_one, cross_starts, q2_own, kv2_own, doc_rows, doc_memory, False)
    kv2_oth = project_memory(memory, cross_wkv2)
    o2_oth, qa2_oth = attend(side_one, cross_starts, q2_oth, kv2_oth, doc_rows, doc_memory, False)
    stream2, a3 = after_cross(stream1, o2_own, o2_oth, cross_wo, cross_wo2, norms)

    a3_oth = swap_tensor(a3)
    h_own, du_own, out_own, r3_own = feed(side_one, a3, e3, ffn_up, ffn_down, F32)
    a3_oth = after(a3_oth, r3_own)
    h_oth, du_oth, out_oth, r3_oth = feed(1 - side_one, a3_oth, e3, ffn_up, ffn_down, BF16)
    r3_recv = swap_tensor(r3_oth)
    aligned = (width // parts) % 16 == 0
    static_parts = parts if aligned else 2
    keep_f, send_f = feed_grads(core_side, static_parts, a3, a3_oth, e3, du_own, du_oth, h_own, h_oth)
    r3_recv = after(r3_recv, keep_f)
    out_recv = swap_tensor(after(out_oth, r3_recv))

    def reordered(keep, send):
        if aligned:
            return keep, send
        whole = jnp.where(core == 0, jnp.concatenate([keep, send]), jnp.concatenate([send, keep]))
        order = [bit_reversed(number, bits) for number in range(parts)]
        whole = jnp.take(whole.reshape(parts, width // parts, -1), jnp.array(order), axis=0)
        whole = whole.reshape(2, width // 2, -1)
        pick = lambda index: lax.dynamic_index_in_dim(whole, index, 0, False)
        return pick(core), pick(1 - core)

    def reduce_core(keep, send):
        keep, send = reordered(keep, send)
        return add(keep, swap_dp(send, 0))

    sum_f = reduce_core(keep_f, send_f)
    grad2, e2, do2_own, do2_oth, d3 = after_feed(side_one, stream2, r3_own, r3_recv, e3, norms, cross_wo, cross_wo2)
    do2_own = after(do2_own, sum_f)
    sum_f = halve(sum_f, 1, place)
    dq2_own, dkv2_own = attend_back(side_one, cross_starts, qa2_own, kv2_own, do2_own, o2_own, doc_memory, False)
    do2_oth = after(do2_oth, dq2_own)
    dq2_oth, dkv2_oth = attend_back(side_one, cross_starts, qa2_oth, kv2_oth, do2_oth, o2_oth, doc_memory, False)
    keep_c, send_c = attention_grads(core_side, static_parts, memory, a2, e2, dq2_own, dkv2_own, o2_own)
    keep_d, send_d = attention_grads(core_side, static_parts, memory, a2, e2, dq2_oth, dkv2_oth, o2_oth)
    dq2_oth = after(dq2_oth, sum_f, keep_c, keep_d)
    if bits > 2:
        sum_f = halve(sum_f, 2, place)
    sum_c = reduce_core(keep_c, send_c)
    sum_d = reduce_core(keep_d, send_d)
    grad1, e1, do1_own, do1_oth, d2 = after_cross_back(
        stream1, grad2, dq2_own, dq2_oth, cross_query, cross_wq2, norms, self_wo, self_wo2
    )
    send_m, keep_m = key_value_back(side_one, dkv2_own, after(dkv2_oth, grad1), cross_wkv, cross_wkv2)
    grad_memory = keep_m + swap_tensor(send_m).astype(F32)
    layer_output = (stream2 + out_own + after(out_recv, grad1).astype(F32)).astype(BF16)

    do1_own = after(do1_own, sum_f, sum_c, sum_d, send_m, layer_output)
    for bit in range(3, bits):
        sum_f = halve(sum_f, bit, place)
    sum_cd = halve(jnp.stack([sum_c, sum_d]), 1, place, 1)
    dq1_own, dkv1_own = attend_back(side_one, self_starts, qa1_own, kv_own, do1_own, o1_own, doc_target, True)
    keep_s, send_s = attention_grads(core_side, static_parts, a1, a1, e1, dq1_own, dkv1_own, o1_own)
    sum_s = reduce_core(keep_s, send_s)
    do1_oth = after(do1_oth, keep_s, sum_f)
    dq1_oth, dkv1_oth = attend_back(side_one, self_starts, qa1_oth, kv_oth, do1_oth, o1_oth, doc_target, True)
    dq1_oth = after(dq1_oth, sum_s, sum_cd)
    sum_s = halve(sum_s, 1, place)
    send_r, keep_r, d1 = key_value_back(
        side_one, dkv1_own, dkv1_oth, self_wkv, self_wkv2, (dq1_own, dq1_oth, self_query, self_wq2, x)
    )
    recv_r = swap_tensor(send_r)
    keep_t, send_t = attention_grads(core_side, static_parts, a1, a1, e1, after(dq1_oth, send_r), dkv1_oth, o1_oth)
    sum_t = reduce_core(keep_t, send_t)
    grad_x = input_grad(side_one, x, grad1, keep_r, recv_r, norms)
    sum_c = add(sum_cd[0], swap_tensor(after(sum_cd[1], recv_r)))
    sum_t = halve(sum_t, 1, place)
    sum_s = add(sum_s, swap_tensor(sum_t))
    for bit in range(2, bits):
        sum_c = halve(sum_c, bit, place)
        sum_s = halve(sum_s, bit, place)

    small = jnp.concatenate([d1, d2, d3], axis=0)
    small = small + swap_tensor(small)
    for bit in range(bits):
        small = small + swap_dp(small, bit)

    def four(total):
        pieces = [total[:, number * cols : (number + 1) * cols].astype(F32) for number in range(4)]
        return tuple(pieces[:3]) + (pieces[3].T,)

    hidden = ffn_up.shape[1]
    return (
        (layer_output[None], grad_x[None], grad_memory[None])
        + four(sum_s)
        + four(sum_c)
        + (sum_f[:, :hidden].astype(F32), sum_f[:, hidden:].astype(F32).T)
        + tuple(small[number] for number in range(6))
    )


def solution(mesh):
    tokens = P("dp", None, None)
    columns = P(None, "tensor")
    rows = P("tensor", None)
    block = (P(), P(), columns, columns, columns, rows)
    in_specs = (tokens,) * 3 + (P("dp", None),) * 2 + block + block + (P(), P(), columns, rows)
    out_rows = P("dp", "tensor")
    out_cols = P("tensor", "dp")
    four = (out_rows, out_rows, out_rows, out_cols)
    out_specs = (P("dp", "tensor", None),) * 3 + four + four + (out_rows, out_cols) + (P(),) * 6
    return jax.shard_map(shards, mesh=mesh, in_specs=in_specs, out_specs=out_specs, check_vma=False)
```

```python
from functools import partial

import jax
import jax.numpy as jnp
from jax import lax
from jax.experimental import pallas as pl
from jax.experimental.pallas import tpu as pltpu
from jax.sharding import PartitionSpec as P

HEAD_DIM = 64
DOCS = 4
BLOCK = 256
LOW = -1e30
NORM_ROWS = 16
SPARE = 12
COST = 0.02
F32 = jnp.float32
BF16 = jnp.bfloat16
MIB = 1024 * 1024


def dot(left, right):
    return jnp.dot(left, right, preferred_element_type=F32)


def dot_nt(left, right):
    return lax.dot_general(left, right, (((1,), (1,)), ((), ())), preferred_element_type=F32)


def dot_tn(left, right):
    return lax.dot_general(left, right, (((0,), (0,)), ((), ())), preferred_element_type=F32)


def normalise(values):
    centered = values - jnp.mean(values, -1, keepdims=True)
    rstd = lax.rsqrt(jnp.mean(centered * centered, -1, keepdims=True) + 1e-05)
    return centered * rstd, rstd


def norm_backward(unit, rstd, gain, cotangent):
    scaled = cotangent * gain
    return rstd * (
        scaled
        - jnp.mean(scaled, -1, keepdims=True)
        - unit * jnp.mean(scaled * unit, -1, keepdims=True)
    )


PARTS = {"Q": (0, 1), "K": (1, 2), "O": (3, 1)}


class Staged:
    def __init__(self, arriving, leaving, spare):
        self.arriving, self.leaving, self.spare, self.sent = arriving, leaving, list(spare), []

    def need(self, *refs):
        for number, (ref, copy) in enumerate(self.arriving):
            if copy is not None and any(ref is wanted for wanted in refs):
                copy.wait()
                self.arriving[number] = (ref, None)

    def fetch(self, *refs):
        for ref, copy in self.arriving:
            if any(ref is wanted for wanted in refs):
                copy.start()

    def send(self, *refs):
        for number, (ref, target, sem) in enumerate(self.leaving):
            if target is not None and any(ref is wanted for wanted in refs):
                self.sent.append(pltpu.make_async_copy(ref, target, sem))
                self.sent[-1].start()
                self.leaving[number] = (ref, None, sem)

    def send_columns(self, refs, columns, last):
        for number, (ref, target, sem) in enumerate(self.leaving):
            if target is not None and any(ref is wanted for wanted in refs):
                if not last:
                    sem = self.spare.pop()
                self.sent.append(pltpu.make_async_copy(ref.at[:, columns], target.at[:, columns], sem))
                self.sent[-1].start()
                if last:
                    self.leaving[number] = (ref, None, sem)

    def finish(self):
        self.need(*(ref for ref, _ in self.arriving))
        self.send(*(ref for ref, _, _ in self.leaving))
        for copy in self.sent:
            copy.wait()


def call(kernel, out_shape, *, far="", far_out="", flops=0, limit=36, scratch=(), scalars=1):
    single = not isinstance(out_shape, tuple)
    shapes = (out_shape,) if single else out_shape

    def run(*operands):
        vmem = pl.BlockSpec(memory_space=pltpu.VMEM)
        hbm = pl.BlockSpec(memory_space=pltpu.HBM)
        small = pl.BlockSpec(memory_space=pltpu.SMEM)
        arrays = operands[scalars:]
        marks = far.ljust(len(arrays), "N")
        out_marks = far_out.ljust(len(shapes), "N")
        assert len(marks) == len(arrays) and len(out_marks) == len(shapes), (len(arrays), len(shapes))
        also = [number for number, mark in enumerate(out_marks) if mark == "B"]
        buffers, out_buffers = [], []
        for mark, array in zip(marks, arrays):
            dims = array.shape
            if mark == "H":
                dims = (dims[0] // 2,) + dims[1:]
            elif mark == "R":
                dims = (shapes[0].shape[0],) + dims[1:]
            elif mark in PARTS:
                dims = (dims[0], dims[1] // 4 * PARTS[mark][1])
            buffers.append(pltpu.VMEM(dims, array.dtype) if mark != "N" else None)
        for mark, item in zip(out_marks, shapes):
            out_buffers.append(pltpu.VMEM(item.shape, item.dtype) if mark == "F" else None)
        extra = [item for item in buffers + out_buffers if item is not None]
        copies = len(extra) + len(also)
        extra.append(pltpu.SemaphoreType.DMA((copies + SPARE,)))

        def wrapped(*refs):
            heads, refs = refs[:scalars], refs[scalars:]
            ins, refs = list(refs[: len(arrays)]), refs[len(arrays) :]
            outs, refs = list(refs[: len(shapes)]), refs[len(shapes) :]
            seconds, refs = refs[: len(also)], refs[len(also) :]
            own, refs = refs[: len(scratch)], refs[len(scratch) :]
            held, sems = list(refs[:-1]), refs[-1]
            arriving, leaving, place = [], [], 0
            for number, mark in enumerate(marks):
                if mark != "N":
                    source = ins[number]
                    if mark == "H":
                        rows = source.shape[0] // 2
                        source = source.at[pl.ds(pl.multiple_of(heads[0][0] * rows, BLOCK), rows)]
                    elif mark == "R":
                        source = source.at[pl.ds(pl.multiple_of(heads[0][0] * BLOCK, BLOCK), shapes[0].shape[0])]
                    elif mark in PARTS:
                        quarter = source.shape[1] // 4
                        source = source.at[:, pl.ds(PARTS[mark][0] * quarter, PARTS[mark][1] * quarter)]
                    ins[number] = held.pop(0)
                    copy = pltpu.make_async_copy(source, ins[number], sems.at[place])
                    if mark != "L":
                        copy.start()
                    arriving.append((ins[number], copy))
                    place += 1
            for number, mark in enumerate(out_marks):
                if mark == "F":
                    target, outs[number] = outs[number], held.pop(0)
                    leaving.append((outs[number], target, sems.at[place]))
                    place += 1
            for number, second in zip(also, seconds):
                leaving.append((outs[number], second, sems.at[place]))
                place += 1
            stage = Staged(arriving, leaving, [sems.at[copies + number] for number in range(SPARE)])
            kernel(stage, *heads, *ins, *outs, *own)
            stage.finish()

        kept = [pltpu.HBM(item.shape, item.dtype) if mark == "F" else item for item, mark in zip(shapes, out_marks)]
        kept += [pltpu.HBM(shapes[number].shape, shapes[number].dtype) for number in also]
        pinned = [
            pltpu.with_memory_space_constraint(array, pltpu.HBM) if mark != "N" else array
            for array, mark in zip(arrays, marks)
        ]
        results = pl.pallas_call(
            wrapped,
            out_shape=tuple(kept),
            in_specs=[small] * scalars + [vmem if mark == "N" else hbm for mark in marks],
            out_specs=tuple(hbm if mark == "F" else vmem for mark in out_marks) + (hbm,) * len(also),
            scratch_shapes=list(scratch) + extra,
            compiler_params=pltpu.CompilerParams(vmem_limit_bytes=limit * MIB),
            cost_estimate=pl.CostEstimate(flops=int(COST * flops), bytes_accessed=4096, transcendentals=0),
        )(*operands[:scalars], *pinned)
        return results[0] if len(results) == 1 else results

    return run


def shape(dims, dtype):
    return jax.ShapeDtypeStruct(dims, dtype)


def row_blocks(rows):
    return [slice(first, first + BLOCK) for first in range(0, rows, BLOCK)]


def own_half(side, rows, first=0, count=None):
    count = rows if count is None else count
    return pl.ds(pl.multiple_of(side * rows + first, BLOCK), count)


def vector(ref, number):
    return ref[number : number + 1, :]


def norm_project_kernel(stage, where_ref, x_ref, norms_ref, wq_ref, wkv_ref, a_ref, q_ref, kv_ref):
    stage.need(x_ref)
    for at in row_blocks(x_ref.shape[0]):
        unit, _ = normalise(x_ref[at].astype(F32))
        a_ref[at] = (unit * vector(norms_ref, 0) + vector(norms_ref, 1)).astype(BF16)
    stage.send(a_ref)
    rows = q_ref.shape[0]
    stage.need(wkv_ref)
    for at in row_blocks(x_ref.shape[0]):
        kv_ref[at] = dot(a_ref[at], wkv_ref[...]).astype(BF16)
    stage.send(kv_ref)
    stage.need(wq_ref)
    q_ref[...] = dot(a_ref[own_half(where_ref[0], rows), :], wq_ref[...]).astype(BF16)


def project_kernel(stage, where_ref, a_ref, wq_ref, wkv_ref, q_ref, kv_ref):
    stage.need(a_ref, wkv_ref)
    for at in row_blocks(a_ref.shape[0]):
        kv_ref[at] = dot(a_ref[at], wkv_ref[...]).astype(BF16)
    stage.send(kv_ref)
    stage.need(wq_ref)
    q_ref[...] = dot(a_ref[own_half(where_ref[0], q_ref.shape[0]), :], wq_ref[...]).astype(BF16)


def project_memory_kernel(stage, memory_ref, wkv_ref, kv_ref):
    stage.need(memory_ref, wkv_ref)
    for at in row_blocks(memory_ref.shape[0]):
        kv_ref[at] = dot(memory_ref[at], wkv_ref[...]).astype(BF16)
    stage.send(kv_ref)


def project_both_kernel(stage, memory_ref, wkv_ref, a_ref, wq_ref, q_ref, kv_ref):
    project_memory_kernel(stage, memory_ref, wkv_ref, kv_ref)
    stage.need(a_ref, wq_ref)
    q_ref[...] = dot(a_ref[...], wq_ref[...]).astype(BF16)


def first_doc(starts_ref, row):
    doc = 0
    for number in range(1, DOCS):
        doc = doc + (starts_ref[0, number] <= row).astype(jnp.int32)
    return doc


def key_range(starts_ref, block_number, causal):
    first = block_number * BLOCK
    low = starts_ref[1, first_doc(starts_ref, first)]
    if causal:
        low = low // BLOCK
        return low * BLOCK, block_number - low
    high = starts_ref[1, first_doc(starts_ref, first + BLOCK - 1) + 1]
    low = low // 128 * 128
    count = (high - low + BLOCK - 1) // BLOCK
    return jnp.minimum(low, starts_ref[1, DOCS] - count * BLOCK), count


def lanes(rows):
    return lax.broadcasted_iota(jnp.int32, (rows, 128), 1)


def causal_mask():
    keys = lax.broadcasted_iota(jnp.int32, (BLOCK, BLOCK), 0)
    rows = lax.broadcasted_iota(jnp.int32, (BLOCK, BLOCK), 1)
    return keys <= rows


def pair_of(ref, pair, rows=slice(None)):
    return ref[rows, pair * 128 : (pair + 1) * 128]


def half_of(head):
    return slice(64 * (head % 2), 64 * (head % 2) + 64)


def in_three(value, place, otherwise):
    high = value.astype(BF16)
    rest = value - high.astype(F32)
    middle = rest.astype(BF16)
    low = (rest - middle.astype(F32)).astype(BF16)
    return jnp.where(place == 4, high, jnp.where(place == 5, middle, jnp.where(place == 6, low, otherwise)))


def walk_keys(starts_ref, block_number, causal, one_block):
    first, count = key_range(starts_ref, block_number, causal)
    if causal:
        one_block(block_number * BLOCK, causal_mask())
    lax.fori_loop(0, count, lambda number, _: (one_block(first + number * BLOCK, None), 0)[1], 0)


def attend_kernel(
    causal, heads, group, stage, where_ref, starts_ref, q_ref, kv_ref, docs_ref, dock_ref, o_ref, qa_ref,
    ka_ref, vt_ref, qs_ref, acc_ref, max_ref,
):
    keys = kv_ref.shape[0]
    pairs = heads // 2
    stage.need(kv_ref, dock_ref)
    left = lanes(keys) < 64
    for pair in range(pairs):
        turned = pair_of(kv_ref, pairs + pair).T
        for head in (2 * pair, 2 * pair + 1):
            mine = left if head % 2 == 0 else ~left
            ka_ref[head] = jnp.where(mine, pair_of(kv_ref, pair), dock_ref[...])
            vt_ref[head, :64] = turned[half_of(head)]
            vt_ref[head, 64:] = jnp.ones((16, keys), BF16)
    left = lanes(BLOCK) < 64
    place = lanes(BLOCK) % 64
    stage.need(q_ref, docs_ref)

    def one_step(step, _):
        at_rows = pl.ds(pl.multiple_of(step * BLOCK, BLOCK), BLOCK)
        block_number = where_ref[0] * (q_ref.shape[0] // BLOCK) + step
        docs = docs_ref[pl.ds(pl.multiple_of(block_number * BLOCK, BLOCK), BLOCK), :]
        for head in range(heads):
            mine = left if head % 2 == 0 else ~left
            scaled = pair_of(q_ref, head // 2, at_rows) * jnp.array(HEAD_DIM**-0.5, BF16)
            qs_ref[head] = jnp.where(mine, scaled, docs)
        max_ref[...] = jnp.full_like(max_ref, LOW)
        acc_ref[...] = jnp.zeros_like(acc_ref)

        def one_block(first_key, mask):
            at = pl.ds(pl.multiple_of(first_key, 128), BLOCK)
            for first in range(0, heads, group):
                some = range(first, first + group)
                scores = [dot_nt(ka_ref[head, at, :], qs_ref[head]) for head in some]
                if mask is not None:
                    scores = [jnp.where(mask, score, LOW) for score in scores]
                old = [max_ref[head, 0:1] for head in some]
                new = [jnp.maximum(m, jnp.max(score, 0, keepdims=True)) for m, score in zip(old, scores)]
                weights = [jnp.exp(score - m).astype(BF16) for score, m in zip(scores, new)]
                mixed = [dot(vt_ref[head, :, at], weight) for head, weight in zip(some, weights)]
                shrink = [jnp.exp(m - n) for m, n in zip(old, new)]
                for number_in, head in enumerate(some):
                    acc_ref[head] = acc_ref[head] * shrink[number_in] + mixed[number_in]
                    max_ref[head, 0:1] = new[number_in]

        walk_keys(starts_ref, block_number, causal, one_block)
        for pair in range(pairs):
            both = []
            for head in (2 * pair, 2 * pair + 1):
                mine = left if head % 2 == 0 else ~left
                acc = acc_ref[head]
                total = acc[64:65]
                both.append(acc[:64] / total)
                lse = max_ref[head, 0:1] + jnp.log(total)
                column = jnp.broadcast_to(-lse, (128, BLOCK)).T
                qa_ref[head, at_rows, :] = jnp.where(mine, qs_ref[head], in_three(column, place, docs))
            o_ref[at_rows, pair * 128 : (pair + 1) * 128] = jnp.concatenate(both, 0).T.astype(BF16)
        return 0

    lax.fori_loop(0, q_ref.shape[0] // BLOCK, one_step, 0)
    stage.send(o_ref, qa_ref)


def attend_back_kernel(
    causal, heads, group, stage, where_ref, starts_ref, qa_ref, kv_ref, do_ref, o_ref, dock_ref, dq_ref, dkv_ref,
    ka_ref, va_ref, da_ref, dqa_ref, dka_ref, dva_ref, kt_ref, qt_ref, dt_ref,
):
    keys = kv_ref.shape[0]
    pairs = heads // 2
    stage.need(kv_ref, dock_ref)
    left = lanes(keys) < 64
    place = lanes(keys) % 64
    ones = jnp.where((place >= 4) & (place < 7), 1.0, 0.0).astype(BF16)
    for head in range(heads):
        mine = left if head % 2 == 0 else ~left
        ka_ref[head] = jnp.where(mine, pair_of(kv_ref, head // 2), dock_ref[...] + ones)
        va_ref[head] = jnp.where(mine, pair_of(kv_ref, pairs + head // 2), ones)
    for pair in range(pairs):
        kt_ref[pair] = pair_of(kv_ref, pair).T
    dka_ref[...] = jnp.zeros_like(dka_ref)
    dva_ref[...] = jnp.zeros_like(dva_ref)
    stage.need(qa_ref, o_ref, do_ref)
    left = lanes(BLOCK) < 64
    place = lanes(BLOCK) % 64

    def one_step(step, _):
        at_rows = pl.ds(pl.multiple_of(step * BLOCK, BLOCK), BLOCK)
        block_number = where_ref[0] * (do_ref.shape[0] // BLOCK) + step
        for pair in range(pairs):
            grad = pair_of(do_ref, pair, at_rows)
            dt_ref[pair] = grad.T
            product = grad.astype(F32) * pair_of(o_ref, pair, at_rows).astype(F32)
            for head in (2 * pair, 2 * pair + 1):
                mine = left if head % 2 == 0 else ~left
                delta = -jnp.sum(jnp.where(mine, product, 0.0), -1, keepdims=True)
                delta = jnp.broadcast_to(delta, (BLOCK, 128))
                da_ref[head] = jnp.where(mine, grad, in_three(delta, place, jnp.zeros((), BF16)))
            qt_ref[pair] = jnp.where(left, qa_ref[2 * pair, at_rows, :], qa_ref[2 * pair + 1, at_rows, :]).T
        dqa_ref[...] = jnp.zeros_like(dqa_ref)

        def one_block(first_key, mask):
            at = pl.ds(pl.multiple_of(first_key, 128), BLOCK)
            for first in range(0, heads, group):
                some = range(first, first + group)
                scores = [dot_nt(ka_ref[head, at, :], qa_ref[head, at_rows, :]) for head in some]
                grads = [dot_nt(va_ref[head, at, :], da_ref[head]) for head in some]
                if mask is not None:
                    scores = [jnp.where(mask, score, LOW) for score in scores]
                weights = [jnp.exp(score) for score in scores]
                grads = [(weight * grad).astype(BF16) for weight, grad in zip(weights, grads)]
                weights = [weight.astype(BF16) for weight in weights]
                values = [dot_nt(dt_ref[head // 2, half_of(head)], weight) for head, weight in zip(some, weights)]
                kept = [dot_nt(qt_ref[head // 2, half_of(head)], grad) for head, grad in zip(some, grads)]
                asked = [dot(kt_ref[head // 2, half_of(head), at], grad) for head, grad in zip(some, grads)]
                for number_in, head in enumerate(some):
                    dva_ref[head // 2, half_of(head), at] += values[number_in]
                    dka_ref[head // 2, half_of(head), at] += kept[number_in]
                    dqa_ref[head // 2, half_of(head)] += asked[number_in]

        walk_keys(starts_ref, block_number, causal, one_block)
        for pair in range(pairs):
            dq_ref[at_rows, pair * 128 : (pair + 1) * 128] = (dqa_ref[pair].T * HEAD_DIM**-0.5).astype(BF16)
        return 0

    lax.fori_loop(0, do_ref.shape[0] // BLOCK, one_step, 0)
    for pair in range(pairs):
        dkv_ref[:, pair * 128 : (pair + 1) * 128] = dka_ref[pair].astype(BF16).T
        dkv_ref[:, (pairs + pair) * 128 : (pairs + pair + 1) * 128] = dva_ref[pair].astype(BF16).T


def out_project(own, other, own_ref, other_ref):
    half = own_ref.shape[1]
    left = dot(own, own_ref[:half]) + dot(other, other_ref[:half])
    right = dot(own, own_ref[half:]) + dot(other, other_ref[half:])
    return jnp.concatenate([left, right], axis=1)


def after_self_kernel(stage, x_ref, own_ref, other_ref, wo_ref, wp_ref, norms_ref, wq_ref, s_ref, a_ref, q_ref):
    stage.need(x_ref, own_ref, wo_ref, wp_ref)
    rows = s_ref.shape[0]
    for at in row_blocks(rows):
        stream = x_ref[at].astype(F32) + out_project(own_ref[at], other_ref[at], wo_ref, wp_ref)
        s_ref[at] = stream
        unit, _ = normalise(stream)
        a_ref[at] = (unit * vector(norms_ref, 2) + vector(norms_ref, 3)).astype(BF16)
    stage.send(s_ref, a_ref)
    stage.need(wq_ref)
    q_ref[...] = dot(a_ref[...], wq_ref[...]).astype(BF16)


def after_cross_kernel(stage, s_ref, own_ref, other_ref, wo_ref, wp_ref, norms_ref, t_ref, a_ref, *parts):
    stage.need(s_ref, own_ref, wo_ref, wp_ref)
    for at in row_blocks(s_ref.shape[0]):
        stream = s_ref[at] + out_project(own_ref[at], other_ref[at], wo_ref, wp_ref)
        t_ref[at] = stream
        unit, _ = normalise(stream)
        a_ref[at] = (unit * vector(norms_ref, 4) + vector(norms_ref, 5)).astype(BF16)
        parts[at.start // BLOCK][...] = a_ref[at]


def prepare_kernel(stage, e_ref, down_ref, memory_ref, wkv_ref, dh_ref, kv_ref):
    stage.need(e_ref, down_ref)
    for at in row_blocks(e_ref.shape[0]):
        dh_ref[at] = dot_nt(e_ref[at], down_ref[...]).astype(BF16)
    stage.send(dh_ref)
    project_memory_kernel(stage, memory_ref, wkv_ref, kv_ref)


def prepare(e, down, memory, wkv):
    rows, width = e.shape
    hidden = down.shape[0]
    return call(
        prepare_kernel,
        (shape((rows, hidden), BF16), shape((memory.shape[0], wkv.shape[1]), BF16)),
        far="FFFF",
        far_out="FF",
        flops=2 * rows * width * hidden,
        scalars=0,
    )(e, down, memory, wkv)


def attend_scratch(heads, keys):
    return [
        pltpu.VMEM((heads, keys, 128), BF16),
        pltpu.VMEM((heads, 80, keys), BF16),
        pltpu.VMEM((heads, BLOCK, 128), BF16),
        pltpu.VMEM((heads, 80, BLOCK), F32),
        pltpu.VMEM((heads, 8, BLOCK), F32),
    ]


def self_own_kernel(heads, stage, side_ref, starts_ref, x, norms, wq, wkv, docs, dock, o, qa, a, kv, q, *scratch):
    norm_project_kernel(stage, side_ref, x, norms, wq, wkv, a, q, kv)
    attend_kernel(True, heads, heads, stage, side_ref, starts_ref, q, kv, docs, dock, o, qa, *scratch)


def self_own(side, starts, x, norms, wq, wkv, docs, dock):
    keys, width = x.shape
    rows, cols = keys // 2, wq.shape[1]
    heads = cols // HEAD_DIM
    return call(
        partial(self_own_kernel, heads),
        (shape((rows, cols), BF16), shape((heads, rows, 128), BF16), shape((keys, width), BF16), shape((keys, 2 * cols), BF16)),
        far="FNFFFF",
        far_out="BFFF",
        flops=5 * keys * width * cols + 16 * rows * keys * cols,
        scalars=2,
        scratch=[pltpu.VMEM((rows, cols), BF16)] + attend_scratch(heads, keys),
    )(side, starts, x, norms, wq, wkv, docs, dock)


def self_other_kernel(
    heads, stage, side_ref, starts_ref, a, wq, wkv, docs, dock, x, own, wo, wp, norms, wc, o, qa, kv, stream, a2, q2, q, *scratch
):
    project_kernel(stage, side_ref, a, wq, wkv, q, kv)
    attend_kernel(True, heads, heads, stage, side_ref, starts_ref, q, kv, docs, dock, o, qa, *scratch)
    after_self_kernel(stage, x, own, o, wo, wp, norms, wc, stream, a2, q2)


def self_other(side, starts, a, wq, wkv, docs, dock, x, own, wo, wp, norms, wc):
    keys, width = a.shape
    rows, cols = own.shape
    heads = cols // HEAD_DIM
    return call(
        partial(self_other_kernel, heads),
        (
            shape((rows, cols), BF16), shape((heads, rows, 128), BF16), shape((keys, 2 * cols), BF16),
            shape((rows, width), F32), shape((rows, width), BF16), shape((rows, cols), BF16),
        ),
        far="FQKFFHNFONF",
        far_out="FFFFFN",
        flops=5 * keys * width * cols + 16 * rows * keys * cols,
        scalars=2,
        scratch=[pltpu.VMEM((rows, cols), BF16)] + attend_scratch(heads, keys),
    )(side, starts, a, wq, wkv, docs, dock, x, own, wo, wp, norms, wc)


def cross_own_kernel(heads, stage, side_ref, starts_ref, kv, q, docs, dock, o, qa, *scratch):
    attend_kernel(False, heads, heads, stage, side_ref, starts_ref, q, kv, docs, dock, o, qa, *scratch)


def cross_own(side, starts, kv, q, docs, dock):
    keys = kv.shape[0]
    rows, cols = q.shape
    heads = cols // HEAD_DIM
    return call(
        partial(cross_own_kernel, heads),
        (shape((rows, cols), BF16), shape((heads, rows, 128), BF16)),
        far="FNFF",
        far_out="BF",
        flops=16 * rows * keys * cols,
        scalars=2,
        scratch=attend_scratch(heads, keys),
    )(side, starts, kv, q, docs, dock)


def cross_other_kernel(
    heads, stage, side_ref, starts_ref, memory, wkv, a, wq, docs, dock, stream, own, wo, wp, norms, o, qa, kv, after, a3, first, second, q, *scratch
):
    project_both_kernel(stage, memory, wkv, a, wq, q, kv)
    attend_kernel(False, heads, heads, stage, side_ref, starts_ref, q, kv, docs, dock, o, qa, *scratch)
    after_cross_kernel(stage, stream, own, o, wo, wp, norms, after, a3, first, second)


def cross_other(side, starts, memory, wkv, a, wq, docs, dock, stream, own, wo, wp, norms):
    keys, width = memory.shape
    rows, cols = own.shape
    heads = cols // HEAD_DIM
    return call(
        partial(cross_other_kernel, heads),
        (
            shape((rows, cols), BF16), shape((heads, rows, 128), BF16), shape((keys, 2 * cols), BF16),
            shape((rows, width), F32), shape((rows, width), BF16), shape((BLOCK, width), BF16), shape((BLOCK, width), BF16),
        ),
        far="FKFQFFFNFON",
        far_out="FFFFNNN",
        flops=5 * keys * width * cols + 16 * rows * keys * cols,
        scalars=2,
        scratch=[pltpu.VMEM((rows, cols), BF16)] + attend_scratch(heads, keys),
    )(side, starts, memory, wkv, a, wq, docs, dock, stream, own, wo, wp, norms)


def feed_kernel(chunk, stage, where_ref, a_ref, dh_ref, up_ref, down_ref, h_ref, du_ref, out_ref, r_ref, *sums):
    rows = a_ref.shape[0]
    out_acc, r_acc = sums if sums else (out_ref, r_ref)
    stage.need(a_ref, up_ref)
    chunks = [slice(first, first + chunk) for first in range(0, up_ref.shape[1], chunk)]
    for some in chunks:
        for at in row_blocks(rows):
            u = dot(a_ref[at], up_ref[:, some])
            if some.start == 0 and at.start == 0:
                stage.need(dh_ref, down_ref)
            square = u * u
            curve = jnp.tanh(u * (0.7978845608028654 + 0.035677408136300125 * square))
            half = 0.5 + 0.5 * curve
            slope = half + (0.5 * u) * (1.0 - curve * curve) * (0.7978845608028654 + 0.10703222440890037 * square)
            h_ref[at, some] = (u * half).astype(BF16)
            du_ref[at, some] = (dh_ref[at, some].astype(F32) * slope).astype(BF16)
        stage.send_columns((h_ref, du_ref), some, some is chunks[-1])
        out_part = dot(h_ref[:, some], down_ref[some])
        if some.start == 0:
            out_acc[...] = out_part
        elif some is chunks[-1]:
            out_ref[...] = (out_acc[...] + out_part).astype(out_ref.dtype)
            stage.send(out_ref)
        else:
            out_acc[...] += out_part
        r_part = dot_nt(du_ref[:, some], up_ref[:, some])
        if some.start == 0:
            r_acc[...] = r_part
        elif some is chunks[-1]:
            r_ref[...] = (r_acc[...] + r_part).astype(r_ref.dtype)
        else:
            r_acc[...] += r_part


def feed(where, a, dh, up, down, dtype, chunk=512):
    rows, width = a.shape
    hidden = up.shape[1]
    return call(
        partial(feed_kernel, chunk),
        (shape((rows, hidden), BF16),) * 2 + (shape((rows, width), dtype),) * 2,
        far="NRFF",
        far_out="FFFN" if dtype == F32 else "FFNN",
        flops=6 * rows * width * hidden,
        limit=24,
        scratch=[] if dtype == F32 else [pltpu.VMEM((rows, width), F32)] * 2,
    )(where, a, dh, up, down)


def grad_into_heads(e, weight_ref):
    half = weight_ref.shape[1]
    return (dot_nt(e[:, :half], weight_ref[:half]) + dot_nt(e[:, half:], weight_ref[half:])).astype(BF16)


def add_rows(ref, number, value):
    ref[number : number + 1, :] += jnp.sum(value, 0, keepdims=True)


def after_feed_kernel(stage, s_ref, r_ref, recv0_ref, recv1_ref, e_ref, norms_ref, wo_ref, wp_ref, g_ref, eb_ref, own_ref, other_ref, d_ref):
    d_ref[...] = jnp.zeros_like(d_ref)
    stage.need(s_ref, r_ref, recv0_ref, recv1_ref, e_ref)
    for at in row_blocks(s_ref.shape[0]):
        unit, rstd = normalise(s_ref[at])
        cotangent = r_ref[at] + (recv0_ref if at.start == 0 else recv1_ref)[...].astype(F32)
        add_rows(d_ref, 0, cotangent * unit)
        add_rows(d_ref, 1, cotangent)
        grad = e_ref[at].astype(F32) + norm_backward(unit, rstd, vector(norms_ref, 4), cotangent)
        g_ref[at] = grad
        eb_ref[at] = grad.astype(BF16)
    stage.send(g_ref, eb_ref)
    stage.need(wo_ref, wp_ref)
    own_ref[...] = grad_into_heads(eb_ref[...], wo_ref)
    other_ref[...] = grad_into_heads(eb_ref[...], wp_ref)


def after_cross_back_kernel(
    stage, s_ref, g_ref, dq_ref, dr_ref, wq_ref, wr_ref, norms_ref, wo_ref, wp_ref, out_ref, eb_ref, own_ref, other_ref, d_ref
):
    d_ref[...] = jnp.zeros_like(d_ref)
    stage.need(s_ref, g_ref, dr_ref, wq_ref, wr_ref)
    for at in row_blocks(s_ref.shape[0]):
        unit, rstd = normalise(s_ref[at])
        cotangent = dot_nt(dq_ref[at], wq_ref[...]) + dot_nt(dr_ref[at], wr_ref[...])
        add_rows(d_ref, 0, cotangent * unit)
        add_rows(d_ref, 1, cotangent)
        grad = g_ref[at] + norm_backward(unit, rstd, vector(norms_ref, 2), cotangent)
        out_ref[at] = grad
        eb_ref[at] = grad.astype(BF16)
    stage.send(out_ref, eb_ref)
    stage.need(wo_ref, wp_ref)
    own_ref[...] = grad_into_heads(eb_ref[...], wo_ref)
    other_ref[...] = grad_into_heads(eb_ref[...], wp_ref)


def key_value_back_kernel(with_queries, stage, where_ref, own_ref, other_ref, wkv_ref, wlw_ref, *refs):
    if with_queries:
        dq_ref, dr_ref, wq_ref, wr_ref, x_ref, send_ref, keep_ref, d_ref = refs
        d_ref[...] = jnp.zeros_like(d_ref)
    else:
        send_ref, keep_ref = refs
    stage.need(own_ref, other_ref, wkv_ref, wlw_ref)
    if with_queries:
        stage.need(x_ref)
    rows = send_ref.shape[0]
    side = where_ref[0]
    for half, target in ((1 - side, send_ref), (side, keep_ref)):
        if with_queries and target is keep_ref:
            stage.need(dq_ref, dr_ref, wq_ref, wr_ref)
        for at in row_blocks(rows):
            place = own_half(half, rows, at.start, BLOCK)
            total = dot_nt(own_ref[place, :], wkv_ref[...]) + dot_nt(other_ref[place, :], wlw_ref[...])
            if with_queries:
                if target is keep_ref:
                    total += dot_nt(dq_ref[at], wq_ref[...]) + dot_nt(dr_ref[at], wr_ref[...])
                unit, _ = normalise(x_ref[place, :].astype(F32))
                add_rows(d_ref, 0, total * unit)
                add_rows(d_ref, 1, total)
            target[at] = total.astype(target.dtype)


def key_value_back(side, own, other, wkv, wlw, queries=()):
    rows = own.shape[0] // 2
    width = wkv.shape[0]
    cols = wkv.shape[1] // 2
    outs = (shape((rows, width), BF16), shape((rows, width), F32))
    if queries:
        outs += (shape((2, width), F32),)
    return call(
        partial(key_value_back_kernel, len(queries) > 0),
        outs,
        far="FFFK",
        far_out="NF",
        flops=18 * rows * width * cols,
    )(side, own, other, wkv, wlw, *queries)


def input_grad_kernel(stage, where_ref, x_ref, g_ref, keep_ref, recv_ref, norms_ref, out_ref):
    stage.need(x_ref, g_ref, keep_ref, recv_ref)
    for at in row_blocks(g_ref.shape[0]):
        unit, rstd = normalise(x_ref[at].astype(F32))
        cotangent = keep_ref[at] + recv_ref[at].astype(F32)
        out_ref[at] = g_ref[at] + norm_backward(unit, rstd, vector(norms_ref, 0), cotangent)


def input_grad(side, x, grad, kept, received, norms):
    rows, width = grad.shape
    return call(
        input_grad_kernel,
        shape((rows, width), F32),
        far="HFF",
        flops=rows * width * 20,
    )(side, x, grad, kept, received, norms)


def bit_reversed(number, bits):
    turned = 0
    for bit in range(bits):
        turned |= ((number >> bit) & 1) << (bits - 1 - bit)
    return turned


def store_parts(product, keep, send, core, parts):
    bits = parts.bit_length() - 1
    rows = product.shape[0] // parts
    product = product.astype(BF16)

    def write(target, wanted):
        for number in range(parts // 2):
            block = bit_reversed(number, bits - 1) * 2 + wanted
            target(number * rows, rows, product[block * rows : (block + 1) * rows])

    for value in (0, 1):
        @pl.when(core == value)
        def _():
            write(keep, value)
            write(send, 1 - value)


def put_columns(ref, columns):
    def put(first, count, value):
        ref[first : first + count, columns] = value

    return put


def attention_grads_kernel(parts, stage, where_ref, wide_ref, a_ref, e_ref, dq_ref, dkv_ref, o_ref, keep_ref, send_ref):
    core = where_ref[1]
    cols = dq_ref.shape[1]
    half = slice(None) if a_ref.shape == e_ref.shape else own_half(where_ref[0], dq_ref.shape[0])
    stage.need(wide_ref, a_ref, e_ref, o_ref)
    products = ((wide_ref, slice(None), dkv_ref, cols), (a_ref, half, dq_ref, 0), (e_ref, slice(None), o_ref, 3 * cols))
    for left, rows, right, first in products:
        product = dot_tn(left[rows, :], right[...])
        columns = slice(first, first + right.shape[1])
        store_parts(product, put_columns(keep_ref, columns), put_columns(send_ref, columns), core, parts)
    stage.send(keep_ref, send_ref)


def feed_grads_kernel(parts, chunk, stage, where_ref, a0, a1, a2, du0, du1, du2, h0, h1, h2, e_ref, keep_ref, send_ref):
    core = where_ref[1]
    rows, hidden = du0.shape
    stage.need(a0, a1, a2, du0, du1, du2)
    stage.fetch(e_ref, h0, h1, h2)
    places = [own_half(where_ref[0], rows)] + [own_half(1 - where_ref[0], rows, at.start, BLOCK) for at in row_blocks(rows)]
    for base in (0, hidden):
        if base > 0:
            stage.need(e_ref, h0, h1, h2)
        for first in range(0, hidden, chunk):
            some = slice(first, first + chunk)
            if base == 0:
                pairs = [(left[...], right[:, some]) for left, right in ((a0, du0), (a1, du1), (a2, du2))]
            else:
                pairs = [(e_ref[place, :], right[:, some]) for place, right in zip(places, (h0, h1, h2))]
            product = dot_tn(*pairs[0]) + dot_tn(*pairs[1]) + dot_tn(*pairs[2])
            columns = slice(base + first, base + first + chunk)
            store_parts(product, put_columns(keep_ref, columns), put_columns(send_ref, columns), core, parts)
            stage.send_columns((keep_ref, send_ref), columns, columns.stop == 2 * hidden)


def attend_back_scratch(heads, keys):
    pairs = heads // 2
    return [
        pltpu.VMEM((heads, keys, 128), BF16),
        pltpu.VMEM((heads, keys, 128), BF16),
        pltpu.VMEM((heads, BLOCK, 128), BF16),
        pltpu.VMEM((pairs, 128, BLOCK), F32),
        pltpu.VMEM((pairs, 128, keys), F32),
        pltpu.VMEM((pairs, 128, keys), F32),
        pltpu.VMEM((pairs, 128, keys), BF16),
        pltpu.VMEM((pairs, 128, BLOCK), BF16),
        pltpu.VMEM((pairs, 128, BLOCK), BF16),
    ]


def after_feed(side, stream, kept, first, second, e3, norms, wo, wp):
    rows, width = stream.shape
    cols = wo.shape[1]
    return call(
        after_feed_kernel_of_side,
        (shape((rows, width), F32), shape((rows, width), BF16), shape((rows, cols), BF16), shape((rows, cols), BF16), shape((2, width), F32)),
        far="FNNNHNFO",
        flops=4 * rows * width * cols,
    )(side, stream, kept, first, second, e3, norms, wo, wp)


def after_feed_kernel_of_side(stage, side_ref, *refs):
    after_feed_kernel(stage, *refs)


def cross_back_kernel(
    parts, heads, stage, where_ref, starts_ref, doo, don, qao, kvo, oo, qan, kvn, on, dock, memory, a2, e2, stream, grad,
    wq, wr, norms, wo, wp,
    keep_d, send_d, keep_c, send_c, dkvo, dkvn, out, e1, own, other, d, dqo, dqn, *scratch
):
    attend_back_kernel(False, heads, heads // 2, stage, where_ref, starts_ref, qao, kvo, doo, oo, dock, dqo, dkvo, *scratch)
    stage.send(dkvo)
    attention_grads_kernel(parts, stage, where_ref, memory, a2, e2, dqo, dkvo, oo, keep_d, send_d)
    attend_back_kernel(False, heads, heads // 2, stage, where_ref, starts_ref, qan, kvn, don, on, dock, dqn, dkvn, *scratch)
    stage.send(dkvn)
    attention_grads_kernel(parts, stage, where_ref, memory, a2, e2, dqn, dkvn, on, keep_c, send_c)
    after_cross_back_kernel(stage, stream, grad, dqn, dqo, wq, wr, norms, wo, wp, out, e1, own, other, d)


def cross_back(where, parts, starts, doo, don, qao, kvo, oo, qan, kvn, on, dock, memory, a2, e2, stream, grad, wq, wr, norms, wo, wp):
    rows, width = stream.shape
    keys, cols = kvo.shape[0], wo.shape[1]
    heads = cols // HEAD_DIM
    part = shape((width // 2, 4 * cols), BF16)
    narrow = shape((rows, cols), BF16)
    return call(
        partial(cross_back_kernel, parts, heads),
        (
            part, part, part, part, shape((keys, 2 * cols), BF16), shape((keys, 2 * cols), BF16), shape((rows, width), F32),
            shape((rows, width), BF16), narrow, narrow, shape((2, width), F32),
        ),
        far="NNFFFFFFFFFNFNFQNFO",
        far_out="FFFFFFFFFNN",
        flops=120 * rows * keys * cols,
        scalars=2,
        limit=44,
        scratch=[pltpu.VMEM((rows, cols), BF16)] * 2 + attend_back_scratch(heads, keys),
    )(where, starts, doo, don, qao, kvo, oo, qan, kvn, on, dock, memory, a2, e2, stream, grad, wq, wr, norms, wo, wp)


def self_other_back_kernel(parts, heads, stage, where_ref, starts_ref, do, qa, kv, o, dock, a1, e1, dq, dkv, keep, send, *scratch):
    attend_back_kernel(True, heads, heads // 2, stage, where_ref, starts_ref, qa, kv, do, o, dock, dq, dkv, *scratch)
    stage.send(dq, dkv)
    attention_grads_kernel(parts, stage, where_ref, a1, a1, e1, dq, dkv, o, keep, send)


def self_other_back(where, parts, starts, do, qa, kv, o, dock, a1, e1):
    rows, cols = do.shape
    keys, width = a1.shape
    heads = cols // HEAD_DIM
    part = shape((width // 2, 4 * cols), BF16)
    return call(
        partial(self_other_back_kernel, parts, heads),
        (shape((rows, cols), BF16), shape((keys, 2 * cols), BF16), part, part),
        far="NFFFFFF",
        far_out="FFFF",
        flops=56 * rows * keys * cols,
        scalars=2,
        limit=34,
        scratch=attend_back_scratch(heads, keys),
    )(where, starts, do, qa, kv, o, dock, a1, e1)


def self_own_back_kernel(
    parts, heads, stage, where_ref, starts_ref, do, qa, kv, o, dock, a1, e1, dqo, dkvo, wkv, wlw, wq, wr, x,
    keep_r, send_r, d, keep, send, dq, dkv, *scratch
):
    attend_back_kernel(True, heads, heads // 2, stage, where_ref, starts_ref, qa, kv, do, o, dock, dq, dkv, *scratch)
    attention_grads_kernel(parts, stage, where_ref, a1, a1, e1, dq, dkv, o, keep, send)
    key_value_back_kernel(True, stage, where_ref, dkv, dkvo, wkv, wlw, dq, dqo, wq, wr, x, send_r, keep_r, d)


def self_own_back(where, parts, starts, do, qa, kv, o, dock, a1, e1, dqo, dkvo, wkv, wlw, wq, wr, x):
    rows, cols = do.shape
    keys, width = a1.shape
    heads = cols // HEAD_DIM
    part = shape((width // 2, 4 * cols), BF16)
    return call(
        partial(self_own_back_kernel, parts, heads),
        (shape((rows, width), F32), shape((rows, width), BF16), shape((2, width), F32), part, part),
        far="FFFFFFFFFFKFQF",
        far_out="FNNFF",
        flops=74 * rows * keys * cols,
        scalars=2,
        limit=36,
        scratch=[pltpu.VMEM((rows, cols), BF16), pltpu.VMEM((keys, 2 * cols), BF16)] + attend_back_scratch(heads, keys),
    )(where, starts, do, qa, kv, o, dock, a1, e1, dqo, dkvo, wkv, wlw, wq, wr, x)


def feed_grads(where, parts, e, a, du, h, chunk=768):
    rows, width = a[0].shape
    hidden = du[0].shape[1]
    out = shape((width // 2, 2 * hidden), BF16)
    return call(
        partial(feed_grads_kernel, parts, chunk),
        (out, out),
        far="NNNFFFLLLL",
        far_out="FF",
        flops=8 * rows * width * hidden,
        limit=30,
    )(where, *a, *du, *h, e)


def swap_tensor(value):
    return lax.ppermute(value, "tensor", [(0, 1), (1, 0)])


def swap_dp(value, bit):
    count = lax.axis_size("dp")
    return lax.ppermute(value, "dp", [(number, number ^ (1 << bit)) for number in range(count)])


def after(value, *others):
    return lax.optimization_barrier((value,) + others)[0] if others else value


def quarter_of(query, key, value, out, part):
    width, cols = query.shape
    rows = width // 4
    pieces = [lax.dynamic_slice_in_dim(weight, part * rows, rows, 0) for weight in (query, key, value)]
    pieces.append(lax.dynamic_slice(out, ((part % 2) * rows, (part // 2) * cols), (rows, cols)))
    return jnp.concatenate(pieces, axis=1)


def whole_of(first, second, third, fourth, part):
    pieces = (first, third, second, fourth)
    return jnp.concatenate([lax.select_n(part ^ number, *pieces) for number in range(4)], axis=0)


class Sum:
    def __init__(self, *terms):
        self.terms = [term if isinstance(term, tuple) else (term, 0) for term in terms]
        last, first = self.terms[-1]
        self.rows = last.shape[0]

    def cut(self, first, rows):
        return Sum.of([(array, start + first) for array, start in self.terms], rows)

    @classmethod
    def of(cls, terms, rows):
        made = cls.__new__(cls)
        made.terms, made.rows = terms, rows
        return made

    def plus(self, array):
        return Sum.of(self.terms + [(array, 0)], self.rows)

    def formed(self, dtype=BF16):
        pieces = [
            array.astype(F32) if array.shape[0] == self.rows else lax.dynamic_slice_in_dim(array, start, self.rows, 0).astype(F32)
            for array, start in self.terms
        ]
        return sum(pieces[1:], pieces[0]).astype(dtype)

    def tied(self, *others):
        arrays = [array for array, _ in self.terms]
        made = lax.optimization_barrier((tuple(arrays), others))
        return (Sum.of([(array, start) for array, (_, start) in zip(made[0], self.terms)], self.rows),) + tuple(made[1])


def halve(value, bit, place):
    rows = value.rows // 2
    mine = (place >> bit) & 1
    return value.cut(mine * rows, rows), swap_dp(value.cut((1 - mine) * rows, rows).formed(), bit)


def add(left, right):
    return (left.astype(F32) + right.astype(F32)).astype(BF16)


def shards(
    target_tokens, memory_tokens, output_grad, target_segments, memory_segments,
    norm1_gain, norm1_shift, self_query, self_key, self_value, self_out,
    norm2_gain, norm2_shift, cross_query, cross_key, cross_value, cross_out,
    norm3_gain, norm3_shift, ffn_up, ffn_down,
):
    _, length, width = target_tokens.shape
    cols = self_query.shape[1]
    parts = lax.axis_size("dp")
    bits = parts.bit_length() - 1
    place = lax.axis_index("dp")
    side = lax.axis_index("tensor")
    core = place & 1
    x = target_tokens[0]
    memory = memory_tokens[0]
    e3 = output_grad[0]
    norms = jnp.stack([norm1_gain, norm1_shift, norm2_gain, norm2_shift, norm3_gain, norm3_shift])
    tie = lax.optimization_barrier
    side_one = side.astype(jnp.int32).reshape(1)
    where = jnp.stack([side, core]).astype(jnp.int32)

    def folded(weight):
        return jnp.concatenate([weight[:, :cols], weight[:, cols:]], axis=0)

    part = place % 4
    self_first = swap_tensor(quarter_of(self_query, self_key, self_value, self_out, part))
    cross_quarter = quarter_of(cross_query, cross_key, cross_value, cross_out, part)
    self_wo = folded(self_out)
    cross_wo = folded(cross_out)
    self_wkv = jnp.concatenate([self_key, self_value], axis=1)
    cross_wkv = jnp.concatenate([cross_key, cross_value], axis=1)

    numbers = jnp.arange(DOCS + 1)[:, None]
    target_starts = jnp.sum(target_segments < numbers, 1).astype(jnp.int32)
    memory_starts = jnp.sum(memory_segments < numbers, 1).astype(jnp.int32)
    self_starts = jnp.stack([target_starts, target_starts])
    cross_starts = jnp.stack([target_starts, memory_starts])
    lane = jnp.arange(128) % 64
    hot = target_segments[0][:, None] == lane[None, :]
    doc_rows = jnp.where(hot, LOW, 0.0).astype(BF16)
    doc_target = jnp.where((lane < DOCS)[None, :] & ~hot, 1.0, 0.0).astype(BF16)
    doc_memory = jnp.where(
        (lane < DOCS)[None, :] & (memory_segments[0][:, None] != lane[None, :]), 1.0, 0.0
    ).astype(BF16)

    dh, kv2_own = prepare(e3, ffn_down, memory, cross_wkv)
    (
        self_first, cross_quarter, x_now, dh, kv2_own, doc_rows, doc_target, doc_memory, self_wo, cross_wo, self_wkv, norms
    ) = tie((self_first, cross_quarter, x, dh, kv2_own, doc_rows, doc_target, doc_memory, self_wo, cross_wo, self_wkv, norms))
    self_second = swap_dp(self_first, 1)
    self_third = swap_dp(self_first, 0)
    cross_first = swap_tensor(cross_quarter)
    o1_own, qa1_own, a1, kv_own, o1_own_far = self_own(
        side_one, self_starts, x_now, norms, self_query, self_wkv, doc_rows, doc_target
    )
    self_second, o1_own, cross_first = tie((self_second, o1_own, cross_first))
    self_fourth = swap_dp(self_second, 0)
    self_fourth, self_third = tie((self_fourth, self_third))
    self_two = whole_of(self_first, self_second, self_third, self_fourth, part)
    cross_first, self_two = tie((cross_first, self_two))
    cross_second = swap_dp(cross_first, 1)
    cross_third = swap_dp(cross_first, 0)
    o1_oth, qa1_oth, kv_oth, stream1, a2, q2_own = self_other(
        side_one, self_starts, a1, self_two, self_two, doc_rows, doc_target, x, o1_own, self_wo, self_two, norms, cross_query
    )
    cross_second, q2_own = tie((cross_second, q2_own))
    cross_fourth = swap_dp(cross_second, 0)
    o2_own, qa2_own, o2_own_far = cross_own(side_one, cross_starts, kv2_own, q2_own, doc_rows, doc_memory)
    cross_fourth, cross_third, o2_own = tie((cross_fourth, cross_third, o2_own))
    cross_two = whole_of(cross_first, cross_second, cross_third, cross_fourth, part)
    o2_oth, qa2_oth, kv2_oth, stream2, a3, a3_first, a3_second = cross_other(
        side_one, cross_starts, memory, cross_two, a2, cross_two, doc_rows, doc_memory, stream1, o2_own, cross_wo, cross_two, norms
    )

    first_block = (side * (length // 2 // BLOCK)).astype(jnp.int32).reshape(1)
    other_block = length // 2 // BLOCK - first_block
    a3_first, a3_second = swap_tensor(a3_first), swap_tensor(a3_second)
    h_own, du_own, out_own, r3_own = feed(first_block, a3, dh, ffn_up, ffn_down, F32)
    a3_first, r3_own = tie((a3_first, r3_own))
    h_first, du_first, out_first, r3_first = feed(other_block, a3_first, dh, ffn_up, ffn_down, BF16)
    a3_second, r3_first = tie((a3_second, r3_first))
    r3_first = swap_tensor(r3_first)
    h_second, du_second, out_second, r3_second = feed(other_block + 1, a3_second, dh, ffn_up, ffn_down, BF16)
    r3_second = swap_tensor(r3_second)
    aligned = (width // parts) % 16 == 0
    static_parts = parts if aligned else 2
    keep_f, send_f = feed_grads(
        where, static_parts, e3, (a3, a3_first, a3_second), (du_own, du_first, du_second), (h_own, h_first, h_second)
    )
    r3_first, r3_second, keep_f, send_f = tie((r3_first, r3_second, keep_f, send_f))

    def reordered(keep, send):
        if aligned:
            return keep, send
        whole = jnp.where(core == 0, jnp.concatenate([keep, send]), jnp.concatenate([send, keep]))
        order = [bit_reversed(number, bits) for number in range(parts)]
        whole = jnp.take(whole.reshape(parts, width // parts, -1), jnp.array(order), axis=0)
        whole = whole.reshape(2, width // 2, -1)
        pick = lambda index: lax.dynamic_index_in_dim(whole, index, 0, False)
        return pick(core), pick(1 - core)

    def swap_core(keep, send):
        keep, send = reordered(keep, send)
        return keep, swap_dp(send, 0)

    keep_f, recv_f = swap_core(keep_f, send_f)
    grad2, e2, do2_own, do2_oth, d3 = after_feed(
        side_one, stream2, r3_own, r3_first, r3_second, e3, norms, cross_wo, cross_two
    )
    do2_oth, keep_f, recv_f, out_first, out_second = tie((do2_oth, keep_f, recv_f, out_first, out_second))
    out_first, out_second = swap_tensor(out_first), swap_tensor(out_second)
    sum_f, recv_f = halve(Sum(keep_f, recv_f), 1, place)
    keep_d, send_d, keep_c, send_c, dkv2_oth, dkv2_own, grad1, e1, do1_own, do1_oth, d2 = cross_back(
        where, static_parts, cross_starts, do2_oth, do2_own, qa2_oth, kv2_oth, o2_oth, qa2_own, kv2_own, o2_own_far,
        doc_memory, memory, a2, e2, stream1, grad2, cross_query, cross_two, norms, self_wo, self_two,
    )
    keep_d, send_d, keep_c, send_c, recv_f, out_first, out_second = tie(
        (keep_d, send_d, keep_c, send_c, recv_f, out_first, out_second)
    )
    keep_d, recv_d = swap_core(keep_d, send_d)
    keep_c, recv_c = swap_core(keep_c, send_c)
    sum_f = sum_f.plus(recv_f)
    send_m, keep_m = key_value_back(side_one, dkv2_own, dkv2_oth, cross_wkv, cross_two)

    do1_oth, keep_d, recv_d, keep_c, recv_c, send_m = tie((do1_oth, keep_d, recv_d, keep_c, recv_c, send_m))
    sum_d, recv_d = halve(Sum(keep_d, recv_d), 1, place)
    recv_m = swap_tensor(send_m)
    dq1_oth, dkv1_oth, keep_t, send_t = self_other_back(
        where, static_parts, self_starts, do1_oth, qa1_oth, kv_oth, o1_oth, doc_target, a1, e1
    )
    keep_t, send_t, recv_d, recv_m = tie((keep_t, send_t, recv_d, recv_m))
    keep_t, recv_t = swap_core(keep_t, send_t)
    do1_own, keep_t, recv_t = tie((do1_own, keep_t, recv_t))
    if bits > 2:
        sum_f, recv_f = halve(sum_f, 2, place)
    sum_t, recv_t = halve(Sum(keep_t, recv_t), 1, place)
    sum_c, recv_c = halve(Sum(keep_c, recv_c), 1, place)
    sent_d = swap_tensor(sum_d.plus(recv_d).formed())
    keep_r, send_r, d1, keep_s, send_s = self_own_back(
        where, static_parts, self_starts, do1_own, qa1_own, kv_own, o1_own_far, doc_target, a1, e1,
        dq1_oth, dkv1_oth, self_wkv, self_two, self_query, self_two, x,
    )
    keep_s, send_s, d1, recv_c, sent_d, recv_t, recv_f = tie((keep_s, send_s, d1, recv_c, sent_d, recv_t, recv_f))
    keep_s, recv_s = swap_core(keep_s, send_s)
    sent_t = swap_tensor(sum_t.plus(recv_t).formed())
    sum_c = sum_c.plus(recv_c).plus(sent_d)
    if bits > 2:
        sum_c, recv_c = halve(sum_c, 2, place)
    lines = jnp.concatenate([jnp.concatenate([d[0:1], d[1:2]], axis=1) for d in (d1, d2, d3)], axis=0)
    lines = jnp.pad(lines, ((0, NORM_ROWS - 3), (0, 0))).astype(BF16)
    lines = add(lines, swap_tensor(lines))
    lines = add(lines, swap_dp(lines, 0))
    keep_s, recv_s, send_r, lines, out_first, out_second = tie((keep_s, recv_s, send_r, lines, out_first, out_second))
    recv_r = swap_tensor(send_r)
    layer_output = (stream2 + out_own + jnp.concatenate([out_first, out_second]).astype(F32)).astype(BF16)
    if bits > 2:
        sum_f = sum_f.plus(recv_f)
    if bits > 3:
        sum_f, recv_f = halve(sum_f, 3, place)
    sum_s = Sum(keep_s, recv_s)

    def halve_with_lines(value, lines, bit):
        rows = value.rows // 2
        mine = (place >> bit) & 1
        message = jnp.concatenate([value.cut((1 - mine) * rows, rows).formed(), lines], axis=0)
        received = swap_dp(message, bit)
        return value.cut(mine * rows, rows).plus(received), add(lines, received[rows:])

    sum_s, lines = halve_with_lines(sum_s, lines, 1)
    sum_s, lines, sent_t, recv_c, recv_f, recv_m, layer_output = sum_s.tied(
        lines, sent_t, recv_c, recv_f, recv_m, layer_output
    )
    sum_s = sum_s.plus(sent_t)
    for bit in range(3, bits):
        sum_f = sum_f.plus(recv_f)
        if bit + 1 < bits:
            sum_f, recv_f = halve(sum_f, bit + 1, place)
    if bits > 2:
        sum_c = sum_c.plus(recv_c)
    for bit in range(3, bits):
        sum_c, recv_c = halve(sum_c, bit, place)
        sum_c = sum_c.plus(recv_c)
    for bit in range(2, bits):
        sum_s, lines = halve_with_lines(sum_s, lines, bit)
        if bit == 2:
            recv_r, lines = tie((recv_r, lines))
    grad_x = input_grad(side_one, x, grad1, keep_r, recv_r, norms)
    grad_memory = keep_m + recv_m.astype(F32)
    small = lines.astype(F32)
    sum_s, sum_c, sum_f = (value.formed(F32) for value in (sum_s, sum_c, sum_f))

    def four(total):
        pieces = [total[:, number * cols : (number + 1) * cols] for number in range(4)]
        return tuple(pieces[:3]) + (pieces[3].T,)

    hidden = ffn_up.shape[1]
    return (
        (layer_output[None], grad_x[None], grad_memory[None])
        + four(sum_s)
        + four(sum_c)
        + (sum_f[:, :hidden], sum_f[:, hidden:].T)
        + tuple(small[number // 2, (number % 2) * width : (number % 2 + 1) * width] for number in range(6))
    )


def solution(mesh):
    tokens = P("dp", None, None)
    columns = P(None, "tensor")
    rows = P("tensor", None)
    block = (P(), P(), columns, columns, columns, rows)
    in_specs = (tokens,) * 3 + (P("dp", None),) * 2 + block + block + (P(), P(), columns, rows)
    out_rows = P("dp", "tensor")
    out_cols = P("tensor", "dp")
    four = (out_rows, out_rows, out_rows, out_cols)
    out_specs = (P("dp", "tensor", None),) * 3 + four + four + (out_rows, out_cols) + (P(),) * 6
    return jax.shard_map(shards, mesh=mesh, in_specs=in_specs, out_specs=out_specs, check_vma=False)
```

```python
from functools import partial

import jax
import jax.numpy as jnp
from jax import lax
from jax.experimental import pallas as pl
from jax.experimental.pallas import tpu as pltpu
from jax.sharding import PartitionSpec as P

HEAD_DIM = 64
DOCS = 4
BLOCK = 256
LOW = -1e30
NORM_ROWS = 16
SPARE = 12
COST = 0.02
F32 = jnp.float32
BF16 = jnp.bfloat16
MIB = 1024 * 1024


def dot(left, right):
    return jnp.dot(left, right, preferred_element_type=F32)


def dot_nt(left, right):
    return lax.dot_general(left, right, (((1,), (1,)), ((), ())), preferred_element_type=F32)


def dot_tn(left, right):
    return lax.dot_general(left, right, (((0,), (0,)), ((), ())), preferred_element_type=F32)


def normalise(values):
    centered = values - jnp.mean(values, -1, keepdims=True)
    rstd = lax.rsqrt(jnp.mean(centered * centered, -1, keepdims=True) + 1e-05)
    return centered * rstd, rstd


def norm_backward(unit, rstd, gain, cotangent):
    scaled = cotangent * gain
    return rstd * (
        scaled
        - jnp.mean(scaled, -1, keepdims=True)
        - unit * jnp.mean(scaled * unit, -1, keepdims=True)
    )


PARTS = {"Q": (0, 1), "K": (1, 2), "O": (3, 1)}


class Staged:
    def __init__(self, arriving, leaving, spare):
        self.arriving, self.leaving, self.spare, self.sent = arriving, leaving, list(spare), []

    def need(self, *refs):
        for number, (ref, copy) in enumerate(self.arriving):
            if copy is not None and any(ref is wanted for wanted in refs):
                copy.wait()
                self.arriving[number] = (ref, None)

    def send(self, *refs):
        for number, (ref, target, sem) in enumerate(self.leaving):
            if target is not None and any(ref is wanted for wanted in refs):
                self.sent.append(pltpu.make_async_copy(ref, target, sem))
                self.sent[-1].start()
                self.leaving[number] = (ref, None, sem)

    def send_columns(self, refs, columns, last):
        for number, (ref, target, sem) in enumerate(self.leaving):
            if target is not None and any(ref is wanted for wanted in refs):
                if not last:
                    sem = self.spare.pop()
                self.sent.append(pltpu.make_async_copy(ref.at[:, columns], target.at[:, columns], sem))
                self.sent[-1].start()
                if last:
                    self.leaving[number] = (ref, None, sem)

    def finish(self):
        self.need(*(ref for ref, _ in self.arriving))
        self.send(*(ref for ref, _, _ in self.leaving))
        for copy in self.sent:
            copy.wait()


def call(kernel, out_shape, *, far="", far_out="", flops=0, limit=36, scratch=(), scalars=1):
    shapes = out_shape if isinstance(out_shape, tuple) else (out_shape,)

    def run(*operands, ahead=()):
        vmem = pl.BlockSpec(memory_space=pltpu.VMEM)
        hbm = pl.BlockSpec(memory_space=pltpu.HBM)
        small = pl.BlockSpec(memory_space=pltpu.SMEM)
        arrays = operands[scalars:]
        marks = far.ljust(len(arrays), "N")
        out_marks = far_out.ljust(len(shapes), "N")
        assert len(marks) == len(arrays) and len(out_marks) == len(shapes), (len(arrays), len(shapes))
        also = [number for number, mark in enumerate(out_marks) if mark == "W"]
        copied = [mark not in "NVX" for mark in marks]

        def held(mark, array):
            dims = array.shape
            if mark == "H":
                dims = (dims[0] // 2,) + dims[1:]
            elif mark == "R":
                dims = (shapes[0].shape[0],) + dims[1:]
            elif mark in PARTS:
                dims = (dims[0], dims[1] // 4 * PARTS[mark][1])
            return dims, array.dtype

        def part_of(mark, source, heads):
            if mark == "H":
                rows = source.shape[0] // 2
                return source.at[pl.ds(pl.multiple_of(heads[0][0] * rows, BLOCK), rows)]
            if mark == "R":
                return source.at[pl.ds(pl.multiple_of(heads[0][0] * BLOCK, BLOCK), shapes[0].shape[0])]
            if mark in PARTS:
                quarter = source.shape[1] // 4
                return source.at[:, pl.ds(PARTS[mark][0] * quarter, PARTS[mark][1] * quarter)]
            return source

        extra = [pltpu.VMEM(*held(mark, array)) for mark, array, here in zip(marks, arrays, copied) if here]
        extra += [pltpu.VMEM(item.shape, item.dtype) for mark, item in zip(out_marks, shapes) if mark == "F"]
        copies = len(extra) + len(also) + len(ahead)
        extra.append(pltpu.SemaphoreType.DMA((copies + SPARE,)))

        def wrapped(*refs):
            refs = list(refs)

            def take(count):
                taken = refs[:count]
                del refs[:count]
                return taken

            heads, ins, coming = take(scalars), take(len(arrays)), take(len(ahead))
            outs, seconds, arrived, own = take(len(shapes)), take(len(also)), take(len(ahead)), take(len(scratch))
            buffers, sems = refs[:-1], refs[-1]
            arriving, leaving, place = [], [], 0
            for number, mark in enumerate(marks):
                if copied[number]:
                    source = part_of(mark, ins[number], heads)
                    ins[number] = buffers.pop(0)
                    copy = pltpu.make_async_copy(source, ins[number], sems.at[place])
                    copy.start()
                    arriving.append((ins[number], copy))
                    place += 1
            for (_, mark), source, target in zip(ahead, coming, arrived):
                copy = pltpu.make_async_copy(part_of(mark, source, heads), target, sems.at[place])
                copy.start()
                arriving.append((target, copy))
                place += 1
            for number, mark in enumerate(out_marks):
                if mark == "F":
                    target, outs[number] = outs[number], buffers.pop(0)
                    leaving.append((outs[number], target, sems.at[place]))
                    place += 1
            for number, second in zip(also, seconds):
                leaving.append((outs[number], second, sems.at[place]))
                place += 1
            stage = Staged(arriving, leaving, [sems.at[copies + number] for number in range(SPARE)])
            kernel(stage, *heads, *ins, *outs, *own)
            stage.finish()

        places = {"F": pltpu.HBM}
        kept = [places[mark](item.shape, item.dtype) if mark in places else item for item, mark in zip(shapes, out_marks)]
        kept += [pltpu.HBM(shapes[number].shape, shapes[number].dtype) for number in also]
        kept += [shape(*held(mark, array)) for array, mark in ahead]
        pinned = [
            array if mark in "NV" else pltpu.with_memory_space_constraint(array, pltpu.HBM)
            for array, mark in zip(arrays, marks)
        ]
        pinned += [pltpu.with_memory_space_constraint(array, pltpu.HBM) for array, _ in ahead]
        results = pl.pallas_call(
            wrapped,
            out_shape=tuple(kept),
            in_specs=[small] * scalars + [vmem if mark in "NV" else hbm for mark in marks] + [hbm] * len(ahead),
            out_specs=tuple(hbm if mark == "F" else vmem for mark in out_marks) + (hbm,) * len(also) + (vmem,) * len(ahead),
            scratch_shapes=list(scratch) + extra,
            compiler_params=pltpu.CompilerParams(vmem_limit_bytes=limit * MIB),
            cost_estimate=pl.CostEstimate(flops=int(COST * flops), bytes_accessed=4096, transcendentals=0),
        )(*operands[:scalars], *pinned)
        return results[0] if len(results) == 1 else results

    return run


def shape(dims, dtype):
    return jax.ShapeDtypeStruct(dims, dtype)


def row_blocks(rows):
    return [slice(first, first + BLOCK) for first in range(0, rows, BLOCK)]


def own_half(side, rows, first=0, count=None):
    count = rows if count is None else count
    return pl.ds(pl.multiple_of(side * rows + first, BLOCK), count)


def vector(ref, number):
    return ref[number : number + 1, :]


def norm_project_kernel(stage, where_ref, x_ref, norms_ref, wq_ref, wkv_ref, a_ref, q_ref, kv_ref):
    stage.need(x_ref)
    for at in row_blocks(x_ref.shape[0]):
        unit, _ = normalise(x_ref[at].astype(F32))
        a_ref[at] = (unit * vector(norms_ref, 0) + vector(norms_ref, 1)).astype(BF16)
    stage.send(a_ref)
    rows = q_ref.shape[0]
    stage.need(wkv_ref)
    for at in row_blocks(x_ref.shape[0]):
        kv_ref[at] = dot(a_ref[at], wkv_ref[...]).astype(BF16)
    stage.send(kv_ref)
    stage.need(wq_ref)
    q_ref[...] = dot(a_ref[own_half(where_ref[0], rows), :], wq_ref[...]).astype(BF16)


def project_kernel(stage, where_ref, a_ref, wq_ref, wkv_ref, q_ref, kv_ref):
    stage.need(a_ref, wkv_ref)
    for at in row_blocks(a_ref.shape[0]):
        kv_ref[at] = dot(a_ref[at], wkv_ref[...]).astype(BF16)
    stage.send(kv_ref)
    stage.need(wq_ref)
    q_ref[...] = dot(a_ref[own_half(where_ref[0], q_ref.shape[0]), :], wq_ref[...]).astype(BF16)


def project_memory_kernel(stage, memory_ref, wkv_ref, kv_ref):
    stage.need(memory_ref, wkv_ref)
    for at in row_blocks(memory_ref.shape[0]):
        kv_ref[at] = dot(memory_ref[at], wkv_ref[...]).astype(BF16)
    stage.send(kv_ref)


def project_both_kernel(stage, memory_ref, wkv_ref, a_ref, wq_ref, q_ref, kv_ref):
    project_memory_kernel(stage, memory_ref, wkv_ref, kv_ref)
    stage.need(a_ref, wq_ref)
    q_ref[...] = dot(a_ref[...], wq_ref[...]).astype(BF16)


def first_doc(starts_ref, row):
    doc = 0
    for number in range(1, DOCS):
        doc = doc + (starts_ref[0, number] <= row).astype(jnp.int32)
    return doc


def key_range(starts_ref, block_number, causal):
    first = block_number * BLOCK
    low = starts_ref[1, first_doc(starts_ref, first)]
    if causal:
        low = low // BLOCK
        return low * BLOCK, block_number - low
    high = starts_ref[1, first_doc(starts_ref, first + BLOCK - 1) + 1]
    low = low // 128 * 128
    count = (high - low + BLOCK - 1) // BLOCK
    return jnp.minimum(low, starts_ref[1, DOCS] - count * BLOCK), count


def lanes(rows):
    return lax.broadcasted_iota(jnp.int32, (rows, 128), 1)


def causal_mask():
    keys = lax.broadcasted_iota(jnp.int32, (BLOCK, BLOCK), 0)
    rows = lax.broadcasted_iota(jnp.int32, (BLOCK, BLOCK), 1)
    return keys <= rows


def pair_of(ref, pair, rows=slice(None)):
    return ref[rows, pair * 128 : (pair + 1) * 128]


def half_of(head):
    return slice(64 * (head % 2), 64 * (head % 2) + 64)


def in_three(value, place, otherwise):
    high = value.astype(BF16)
    rest = value - high.astype(F32)
    middle = rest.astype(BF16)
    low = (rest - middle.astype(F32)).astype(BF16)
    return jnp.where(place == 4, high, jnp.where(place == 5, middle, jnp.where(place == 6, low, otherwise)))


def walk_keys(starts_ref, block_number, causal, one_block):
    first, count = key_range(starts_ref, block_number, causal)
    if causal:
        one_block(block_number * BLOCK, causal_mask())
    lax.fori_loop(0, count, lambda number, _: (one_block(first + number * BLOCK, None), 0)[1], 0)


def attend_kernel(
    causal, heads, group, stage, where_ref, starts_ref, q_ref, kv_ref, docs_ref, dock_ref, o_ref, qa_ref,
    ka_ref, vt_ref, qs_ref, acc_ref, max_ref,
):
    keys = kv_ref.shape[0]
    pairs = heads // 2
    stage.need(kv_ref, dock_ref)
    left = lanes(keys) < 64
    for pair in range(pairs):
        turned = pair_of(kv_ref, pairs + pair).T
        for head in (2 * pair, 2 * pair + 1):
            mine = left if head % 2 == 0 else ~left
            ka_ref[head] = jnp.where(mine, pair_of(kv_ref, pair), dock_ref[...])
            vt_ref[head, :64] = turned[half_of(head)]
            vt_ref[head, 64:] = jnp.ones((16, keys), BF16)
    left = lanes(BLOCK) < 64
    place = lanes(BLOCK) % 64
    stage.need(q_ref, docs_ref)

    def one_step(step, _):
        at_rows = pl.ds(pl.multiple_of(step * BLOCK, BLOCK), BLOCK)
        block_number = where_ref[0] * (q_ref.shape[0] // BLOCK) + step
        docs = docs_ref[pl.ds(pl.multiple_of(block_number * BLOCK, BLOCK), BLOCK), :]
        for head in range(heads):
            mine = left if head % 2 == 0 else ~left
            scaled = pair_of(q_ref, head // 2, at_rows) * jnp.array(HEAD_DIM**-0.5, BF16)
            qs_ref[head] = jnp.where(mine, scaled, docs)
        max_ref[...] = jnp.full_like(max_ref, LOW)
        acc_ref[...] = jnp.zeros_like(acc_ref)

        def one_block(first_key, mask):
            at = pl.ds(pl.multiple_of(first_key, 128), BLOCK)
            for first in range(0, heads, group):
                some = range(first, first + group)
                scores = [dot_nt(ka_ref[head, at, :], qs_ref[head]) for head in some]
                if mask is not None:
                    scores = [jnp.where(mask, score, LOW) for score in scores]
                old = [max_ref[head, 0:1] for head in some]
                new = [jnp.maximum(m, jnp.max(score, 0, keepdims=True)) for m, score in zip(old, scores)]
                weights = [jnp.exp(score - m).astype(BF16) for score, m in zip(scores, new)]
                mixed = [dot(vt_ref[head, :, at], weight) for head, weight in zip(some, weights)]
                shrink = [jnp.exp(m - n) for m, n in zip(old, new)]
                for number_in, head in enumerate(some):
                    acc_ref[head] = acc_ref[head] * shrink[number_in] + mixed[number_in]
                    max_ref[head, 0:1] = new[number_in]

        walk_keys(starts_ref, block_number, causal, one_block)
        for pair in range(pairs):
            both = []
            for head in (2 * pair, 2 * pair + 1):
                mine = left if head % 2 == 0 else ~left
                acc = acc_ref[head]
                total = acc[64:65]
                both.append(acc[:64] / total)
                lse = max_ref[head, 0:1] + jnp.log(total)
                column = jnp.broadcast_to(-lse, (128, BLOCK)).T
                qa_ref[head, at_rows, :] = jnp.where(mine, qs_ref[head], in_three(column, place, docs))
            o_ref[at_rows, pair * 128 : (pair + 1) * 128] = jnp.concatenate(both, 0).T.astype(BF16)
        return 0

    lax.fori_loop(0, q_ref.shape[0] // BLOCK, one_step, 0)
    stage.send(o_ref, qa_ref)


def attend_back_kernel(
    causal, heads, group, stage, where_ref, starts_ref, qa_ref, kv_ref, do_ref, o_ref, dock_ref, dq_ref, dkv_ref,
    ka_ref, va_ref, da_ref, dqa_ref, dka_ref, dva_ref, kt_ref, qt_ref, dt_ref,
):
    keys = kv_ref.shape[0]
    pairs = heads // 2
    stage.need(kv_ref, dock_ref)
    left = lanes(keys) < 64
    place = lanes(keys) % 64
    ones = jnp.where((place >= 4) & (place < 7), 1.0, 0.0).astype(BF16)
    for head in range(heads):
        mine = left if head % 2 == 0 else ~left
        ka_ref[head] = jnp.where(mine, pair_of(kv_ref, head // 2), dock_ref[...] + ones)
        va_ref[head] = jnp.where(mine, pair_of(kv_ref, pairs + head // 2), ones)
    for pair in range(pairs):
        kt_ref[pair] = pair_of(kv_ref, pair).T
    dka_ref[...] = jnp.zeros_like(dka_ref)
    dva_ref[...] = jnp.zeros_like(dva_ref)
    stage.need(qa_ref, o_ref, do_ref)
    left = lanes(BLOCK) < 64
    place = lanes(BLOCK) % 64

    def one_step(step, _):
        at_rows = pl.ds(pl.multiple_of(step * BLOCK, BLOCK), BLOCK)
        block_number = where_ref[0] * (do_ref.shape[0] // BLOCK) + step
        for pair in range(pairs):
            grad = pair_of(do_ref, pair, at_rows)
            dt_ref[pair] = grad.T
            product = grad.astype(F32) * pair_of(o_ref, pair, at_rows).astype(F32)
            for head in (2 * pair, 2 * pair + 1):
                mine = left if head % 2 == 0 else ~left
                delta = -jnp.sum(jnp.where(mine, product, 0.0), -1, keepdims=True)
                delta = jnp.broadcast_to(delta, (BLOCK, 128))
                da_ref[head] = jnp.where(mine, grad, in_three(delta, place, jnp.zeros((), BF16)))
            qt_ref[pair] = jnp.where(left, qa_ref[2 * pair, at_rows, :], qa_ref[2 * pair + 1, at_rows, :]).T
        dqa_ref[...] = jnp.zeros_like(dqa_ref)

        def one_block(first_key, mask):
            at = pl.ds(pl.multiple_of(first_key, 128), BLOCK)
            for first in range(0, heads, group):
                some = range(first, first + group)
                scores = [dot_nt(ka_ref[head, at, :], qa_ref[head, at_rows, :]) for head in some]
                grads = [dot_nt(va_ref[head, at, :], da_ref[head]) for head in some]
                if mask is not None:
                    scores = [jnp.where(mask, score, LOW) for score in scores]
                weights = [jnp.exp(score) for score in scores]
                grads = [(weight * grad).astype(BF16) for weight, grad in zip(weights, grads)]
                weights = [weight.astype(BF16) for weight in weights]
                values = [dot_nt(dt_ref[head // 2, half_of(head)], weight) for head, weight in zip(some, weights)]
                kept = [dot_nt(qt_ref[head // 2, half_of(head)], grad) for head, grad in zip(some, grads)]
                asked = [dot(kt_ref[head // 2, half_of(head), at], grad) for head, grad in zip(some, grads)]
                for number_in, head in enumerate(some):
                    dva_ref[head // 2, half_of(head), at] += values[number_in]
                    dka_ref[head // 2, half_of(head), at] += kept[number_in]
                    dqa_ref[head // 2, half_of(head)] += asked[number_in]

        walk_keys(starts_ref, block_number, causal, one_block)
        for pair in range(pairs):
            dq_ref[at_rows, pair * 128 : (pair + 1) * 128] = (dqa_ref[pair].T * HEAD_DIM**-0.5).astype(BF16)
        return 0

    lax.fori_loop(0, do_ref.shape[0] // BLOCK, one_step, 0)
    for pair in range(pairs):
        dkv_ref[:, pair * 128 : (pair + 1) * 128] = dka_ref[pair].astype(BF16).T
        dkv_ref[:, (pairs + pair) * 128 : (pairs + pair + 1) * 128] = dva_ref[pair].astype(BF16).T


def out_project(own, other, own_ref, other_ref):
    half = other_ref.shape[1]
    folded = [dot(other, other_ref[:half]), dot(other, other_ref[half:])]
    return dot(own, own_ref[...]) + jnp.concatenate(folded, axis=1)


def after_self_kernel(stage, x_ref, own_ref, other_ref, wo_ref, wp_ref, norms_ref, wq_ref, s_ref, a_ref, q_ref):
    stage.need(x_ref, own_ref, wo_ref, wp_ref)
    rows = s_ref.shape[0]
    for at in row_blocks(rows):
        stream = x_ref[at].astype(F32) + out_project(own_ref[at], other_ref[at], wo_ref, wp_ref)
        s_ref[at] = stream
        unit, _ = normalise(stream)
        a_ref[at] = (unit * vector(norms_ref, 2) + vector(norms_ref, 3)).astype(BF16)
    stage.send(s_ref, a_ref)
    stage.need(wq_ref)
    q_ref[...] = dot(a_ref[...], wq_ref[...]).astype(BF16)


def after_cross_kernel(stage, s_ref, own_ref, other_ref, wo_ref, wp_ref, norms_ref, t_ref, a_ref, *parts):
    stage.need(s_ref, own_ref, wo_ref, wp_ref)
    for at in row_blocks(s_ref.shape[0]):
        stream = s_ref[at] + out_project(own_ref[at], other_ref[at], wo_ref, wp_ref)
        t_ref[at] = stream
        unit, _ = normalise(stream)
        a_ref[at] = (unit * vector(norms_ref, 4) + vector(norms_ref, 5)).astype(BF16)
        parts[at.start // BLOCK][...] = a_ref[at]


def prepare_kernel(stage, e_ref, down_ref, memory_ref, wkv_ref, dh_ref, kv_ref):
    stage.need(e_ref, down_ref)
    for at in row_blocks(e_ref.shape[0]):
        dh_ref[at] = dot_nt(e_ref[at], down_ref[...]).astype(BF16)
    stage.send(dh_ref)
    project_memory_kernel(stage, memory_ref, wkv_ref, kv_ref)


def prepare(e, down, memory, wkv, ahead=()):
    rows, width = e.shape
    hidden = down.shape[0]
    return call(
        prepare_kernel,
        (shape((rows, hidden), BF16), shape((memory.shape[0], wkv.shape[1]), BF16)),
        far="FFFF",
        far_out="FF",
        flops=2 * rows * width * hidden,
        scalars=0,
    )(e, down, memory, wkv, ahead=ahead)


def attend_scratch(heads, keys):
    return [
        pltpu.VMEM((heads, keys, 128), BF16),
        pltpu.VMEM((heads, 80, keys), BF16),
        pltpu.VMEM((heads, BLOCK, 128), BF16),
        pltpu.VMEM((heads, 80, BLOCK), F32),
        pltpu.VMEM((heads, 8, BLOCK), F32),
    ]


def self_own_kernel(heads, stage, side_ref, starts_ref, x, norms, wq, wkv, docs, dock, o, qa, a, kv, q, *scratch):
    norm_project_kernel(stage, side_ref, x, norms, wq, wkv, a, q, kv)
    attend_kernel(True, heads, heads, stage, side_ref, starts_ref, q, kv, docs, dock, o, qa, *scratch)


def self_own(side, starts, x, norms, wq, wkv, docs, dock, ahead=()):
    keys, width = x.shape
    rows, cols = keys // 2, wq.shape[1]
    heads = cols // HEAD_DIM
    return call(
        partial(self_own_kernel, heads),
        (shape((rows, cols), BF16), shape((heads, rows, 128), BF16), shape((keys, width), BF16), shape((keys, 2 * cols), BF16)),
        far="FNFFFF",
        far_out="WFFF",
        flops=5 * keys * width * cols + 16 * rows * keys * cols,
        scalars=2,
        scratch=[pltpu.VMEM((rows, cols), BF16)] + attend_scratch(heads, keys),
    )(side, starts, x, norms, wq, wkv, docs, dock, ahead=ahead)


def gather(where_ref, pieces, whole, sems):
    rows = pieces[0].shape[0]
    targets = [whole.at[pl.ds(number * rows, rows)] for number in range(4)]
    for number in range(4):
        for place in range(4):
            @pl.when((where_ref[1] ^ number) == place)
            def _():
                pltpu.make_async_copy(pieces[place], targets[number], sems.at[number]).start()

    return [pltpu.make_async_copy(pieces[0], targets[number], sems.at[number]) for number in range(4)]


def split_weights(whole):
    cols = whole.shape[1] // 4
    return whole.at[:, pl.ds(0, cols)], whole.at[:, pl.ds(cols, 2 * cols)], whole.at[:, pl.ds(3 * cols, cols)]


def self_other_kernel(
    heads, stage, side_ref, starts_ref, a, p0, p1, p2, p3, docs, dock, x, own, wo, norms, wc,
    o, qa, kv, stream, a2, q2, whole, q, sems, *scratch
):
    waits = gather(side_ref, (p0, p1, p2, p3), whole, sems)
    stage.need(a)
    for copy in waits:
        copy.wait()
    stage.send(whole)
    wq, wkv, wp = split_weights(whole)
    project_kernel(stage, side_ref, a, wq, wkv, q, kv)
    attend_kernel(True, heads, heads, stage, side_ref, starts_ref, q, kv, docs, dock, o, qa, *scratch)
    after_self_kernel(stage, x, own, o, wo, wp, norms, wc, stream, a2, q2)


def self_other(where, starts, a, pieces, docs, dock, x, own, wo, norms, wc, ahead=()):
    keys, width = a.shape
    rows, cols = own.shape
    heads = cols // HEAD_DIM
    return call(
        partial(self_other_kernel, heads),
        (
            shape((rows, cols), BF16), shape((heads, rows, 128), BF16), shape((keys, 2 * cols), BF16),
            shape((rows, width), F32), shape((rows, width), BF16), shape((rows, cols), BF16), shape((width, 4 * cols), BF16),
        ),
        far="FXXXXFFHNFNF",
        far_out="FFFFFNF",
        flops=5 * keys * width * cols + 16 * rows * keys * cols,
        scalars=2,
        scratch=[pltpu.VMEM((rows, cols), BF16), pltpu.SemaphoreType.DMA((4,))] + attend_scratch(heads, keys),
    )(where, starts, a, *pieces, docs, dock, x, own, wo, norms, wc, ahead=ahead)


def cross_own_kernel(heads, stage, side_ref, starts_ref, kv, q, docs, dock, o, qa, *scratch):
    attend_kernel(False, heads, heads, stage, side_ref, starts_ref, q, kv, docs, dock, o, qa, *scratch)


def cross_own(side, starts, kv, q, docs, dock, ahead=()):
    keys = kv.shape[0]
    rows, cols = q.shape
    heads = cols // HEAD_DIM
    return call(
        partial(cross_own_kernel, heads),
        (shape((rows, cols), BF16), shape((heads, rows, 128), BF16)),
        far="VNFV",
        far_out="WF",
        flops=16 * rows * keys * cols,
        scalars=2,
        scratch=attend_scratch(heads, keys),
    )(side, starts, kv, q, docs, dock, ahead=ahead)


def cross_other_kernel(
    heads, stage, side_ref, starts_ref, memory, p0, p1, p2, p3, a, docs, dock, stream, own, wo, norms,
    o, qa, kv, after, a3, first, second, whole, q, sems, *scratch
):
    waits = gather(side_ref, (p0, p1, p2, p3), whole, sems)
    stage.need(memory)
    for copy in waits:
        copy.wait()
    stage.send(whole)
    wq, wkv, wp = split_weights(whole)
    project_both_kernel(stage, memory, wkv, a, wq, q, kv)
    attend_kernel(False, heads, heads, stage, side_ref, starts_ref, q, kv, docs, dock, o, qa, *scratch)
    after_cross_kernel(stage, stream, own, o, wo, wp, norms, after, a3, first, second)


def cross_other(where, starts, memory, pieces, a, docs, dock, stream, own, wo, norms, ahead=()):
    keys, width = memory.shape
    rows, cols = own.shape
    heads = cols // HEAD_DIM
    half = shape((BLOCK, width), BF16)
    return call(
        partial(cross_other_kernel, heads),
        (
            shape((rows, cols), BF16), shape((heads, rows, 128), BF16), shape((keys, 2 * cols), BF16),
            shape((rows, width), F32), shape((rows, width), BF16), half, half, shape((width, 4 * cols), BF16),
        ),
        far="FXXXXFFFFNFN",
        far_out="FFFFNNNF",
        flops=5 * keys * width * cols + 16 * rows * keys * cols,
        scalars=2,
        scratch=[pltpu.VMEM((rows, cols), BF16), pltpu.SemaphoreType.DMA((4,))] + attend_scratch(heads, keys),
    )(where, starts, memory, *pieces, a, docs, dock, stream, own, wo, norms, ahead=ahead)


def feed_kernel(chunk, joined, stage, where_ref, a_ref, dh_ref, up_ref, down_ref, *refs):
    if joined:
        before_ref, refs = refs[0], refs[1:]
    h_ref, du_ref, out_ref, r_ref, *sums = refs
    rows = a_ref.shape[0]
    if joined:
        out_ref[:rows] = before_ref[...]
        out_ref = out_ref.at[pl.ds(rows, rows)]
    out_acc, r_acc = sums if sums else (out_ref, r_ref)
    stage.need(a_ref, up_ref)
    chunks = [slice(first, first + chunk) for first in range(0, up_ref.shape[1], chunk)]
    for some in chunks:
        for at in row_blocks(rows):
            u = dot(a_ref[at], up_ref[:, some])
            if some.start == 0 and at.start == 0:
                stage.need(dh_ref, down_ref)
            square = u * u
            curve = jnp.tanh(u * (0.7978845608028654 + 0.035677408136300125 * square))
            half = 0.5 + 0.5 * curve
            slope = half + (0.5 * u) * (1.0 - curve * curve) * (0.7978845608028654 + 0.10703222440890037 * square)
            h_ref[at, some] = (u * half).astype(BF16)
            du_ref[at, some] = (dh_ref[at, some].astype(F32) * slope).astype(BF16)
        stage.send_columns((h_ref, du_ref), some, some is chunks[-1])
        out_part = dot(h_ref[:, some], down_ref[some])
        if some.start == 0:
            out_acc[...] = out_part
        elif some is chunks[-1]:
            out_ref[...] = (out_acc[...] + out_part).astype(out_ref.dtype)
            stage.send(out_ref)
        else:
            out_acc[...] += out_part
        r_part = dot_nt(du_ref[:, some], up_ref[:, some])
        if some.start == 0:
            r_acc[...] = r_part
        elif some is chunks[-1]:
            r_ref[...] = (r_acc[...] + r_part).astype(r_ref.dtype)
        else:
            r_acc[...] += r_part


def feed(where, a, dh, up, down, dtype, *before, chunk=512, ahead=()):
    rows, width = a.shape
    hidden = up.shape[1]
    return call(
        partial(feed_kernel, chunk, len(before) > 0),
        (shape((rows, hidden), BF16),) * 2 + (shape(((1 + len(before)) * rows, width), dtype), shape((rows, width), dtype)),
        far="NRFF",
        far_out="FFFF" if dtype == F32 else "FFNN",
        flops=6 * rows * width * hidden,
        limit=24,
        scratch=[] if dtype == F32 else [pltpu.VMEM((rows, width), F32)] * 2,
    )(where, a, dh, up, down, *before, ahead=ahead)


def grad_into_heads(e, weight_ref):
    half = weight_ref.shape[1]
    if half == e.shape[1]:
        return dot_nt(e, weight_ref[...]).astype(BF16)
    return (dot_nt(e[:, :half], weight_ref[:half]) + dot_nt(e[:, half:], weight_ref[half:])).astype(BF16)


def add_rows(ref, number, value):
    ref[number : number + 1, :] += jnp.sum(value, 0, keepdims=True)


def after_feed_kernel(stage, s_ref, r_ref, recv0_ref, recv1_ref, e_ref, norms_ref, wo_ref, wp_ref, g_ref, eb_ref, own_ref, other_ref, d_ref):
    d_ref[...] = jnp.zeros_like(d_ref)
    stage.need(s_ref, r_ref, recv0_ref, recv1_ref, e_ref)
    for at in row_blocks(s_ref.shape[0]):
        unit, rstd = normalise(s_ref[at])
        cotangent = r_ref[at] + (recv0_ref if at.start == 0 else recv1_ref)[...].astype(F32)
        add_rows(d_ref, 0, cotangent * unit)
        add_rows(d_ref, 1, cotangent)
        grad = e_ref[at].astype(F32) + norm_backward(unit, rstd, vector(norms_ref, 4), cotangent)
        g_ref[at] = grad
        eb_ref[at] = grad.astype(BF16)
    stage.send(g_ref, eb_ref)
    stage.need(wo_ref, wp_ref)
    own_ref[...] = grad_into_heads(eb_ref[...], wo_ref)
    other_ref[...] = grad_into_heads(eb_ref[...], wp_ref)


def after_cross_back_kernel(
    stage, s_ref, g_ref, dq_ref, dr_ref, wq_ref, wr_ref, norms_ref, wo_ref, wp_ref, out_ref, eb_ref, own_ref, other_ref, d_ref
):
    d_ref[...] = jnp.zeros_like(d_ref)
    stage.need(s_ref, g_ref, dr_ref, wq_ref, wr_ref)
    for at in row_blocks(s_ref.shape[0]):
        unit, rstd = normalise(s_ref[at])
        cotangent = dot_nt(dq_ref[at], wq_ref[...]) + dot_nt(dr_ref[at], wr_ref[...])
        add_rows(d_ref, 0, cotangent * unit)
        add_rows(d_ref, 1, cotangent)
        grad = g_ref[at] + norm_backward(unit, rstd, vector(norms_ref, 2), cotangent)
        out_ref[at] = grad
        eb_ref[at] = grad.astype(BF16)
    stage.send(out_ref, eb_ref)
    stage.need(wo_ref, wp_ref)
    own_ref[...] = grad_into_heads(eb_ref[...], wo_ref)
    other_ref[...] = grad_into_heads(eb_ref[...], wp_ref)


def key_value_back_kernel(with_queries, stage, where_ref, own_ref, other_ref, wkv_ref, wlw_ref, *refs):
    if with_queries:
        dq_ref, dr_ref, wq_ref, wr_ref, x_ref, send_ref, keep_ref, d_ref = refs
        d_ref[...] = jnp.zeros_like(d_ref)
    else:
        send_ref, keep_ref = refs
    stage.need(own_ref, other_ref, wkv_ref, wlw_ref)
    if with_queries:
        stage.need(x_ref)
    rows = send_ref.shape[0]
    side = where_ref[0]
    for half, target in ((1 - side, send_ref), (side, keep_ref)):
        if with_queries and target is keep_ref:
            stage.need(dq_ref, dr_ref, wq_ref, wr_ref)
        for at in row_blocks(rows):
            place = own_half(half, rows, at.start, BLOCK)
            total = dot_nt(own_ref[place, :], wkv_ref[...]) + dot_nt(other_ref[place, :], wlw_ref[...])
            if with_queries:
                if target is keep_ref:
                    total += dot_nt(dq_ref[at], wq_ref[...]) + dot_nt(dr_ref[at], wr_ref[...])
                unit, _ = normalise(x_ref[place, :].astype(F32))
                add_rows(d_ref, 0, total * unit)
                add_rows(d_ref, 1, total)
            target[at] = total.astype(target.dtype)


def key_value_back(side, own, other, wkv, wlw, queries=(), ahead=()):
    rows = own.shape[0] // 2
    width = wkv.shape[0]
    cols = wkv.shape[1] // 2
    outs = (shape((rows, width), BF16), shape((rows, width), F32))
    if queries:
        outs += (shape((2, width), F32),)
    return call(
        partial(key_value_back_kernel, len(queries) > 0),
        outs,
        far="VVVV",
        far_out="NF",
        flops=18 * rows * width * cols,
    )(side, own, other, wkv, wlw, *queries, ahead=ahead)


def input_grad_kernel(stage, where_ref, x_ref, g_ref, keep_ref, recv_ref, norms_ref, out_ref):
    stage.need(x_ref, g_ref, keep_ref, recv_ref)
    for at in row_blocks(g_ref.shape[0]):
        unit, rstd = normalise(x_ref[at].astype(F32))
        cotangent = keep_ref[at] + recv_ref[at].astype(F32)
        out_ref[at] = g_ref[at] + norm_backward(unit, rstd, vector(norms_ref, 0), cotangent)


def input_grad(side, x, grad, kept, received, norms):
    rows, width = grad.shape
    return call(
        input_grad_kernel,
        shape((rows, width), F32),
        far="VVFN",
        flops=rows * width * 20,
    )(side, x, grad, kept, received, norms)


def bit_reversed(number, bits):
    turned = 0
    for bit in range(bits):
        turned |= ((number >> bit) & 1) << (bits - 1 - bit)
    return turned


def store_parts(product, keep, send, core, parts):
    bits = parts.bit_length() - 1
    rows = product.shape[0] // parts
    product = product.astype(BF16)

    def write(target, wanted):
        for number in range(parts // 2):
            block = bit_reversed(number, bits - 1) * 2 + wanted
            target(number * rows, rows, product[block * rows : (block + 1) * rows])

    for value in (0, 1):
        @pl.when(core == value)
        def _():
            write(keep, value)
            write(send, 1 - value)


def put_columns(ref, columns):
    def put(first, count, value):
        ref[first : first + count, columns] = value

    return put


def attention_grads_kernel(parts, stage, where_ref, wide_ref, a_ref, e_ref, dq_ref, dkv_ref, o_ref, keep_ref, send_ref):
    core = where_ref[1]
    cols = dq_ref.shape[1]
    half = slice(None) if a_ref.shape == e_ref.shape else own_half(where_ref[0], dq_ref.shape[0])
    stage.need(wide_ref, a_ref, e_ref, o_ref)
    products = ((wide_ref, slice(None), dkv_ref, cols), (a_ref, half, dq_ref, 0), (e_ref, slice(None), o_ref, 3 * cols))
    for left, rows, right, first in products:
        product = dot_tn(left[rows, :], right[...])
        columns = slice(first, first + right.shape[1])
        store_parts(product, put_columns(keep_ref, columns), put_columns(send_ref, columns), core, parts)
    stage.send(keep_ref, send_ref)


def feed_grads_kernel(
    parts, chunk, stage, where_ref, a0, a1, a2, du0, du1, du2, h0, h1, h2, e_ref, keep_ref, send_ref, a_all, left, right, sems
):
    core = where_ref[1]
    rows, width = a0.shape
    hidden = du0.shape[1]
    places = [(0, rows)] + [(rows + at.start, BLOCK) for at in row_blocks(rows)]

    def fill(sources, number):
        copies = []
        for place, (source, (first, count)) in enumerate(zip(sources, places)):
            copies.append(
                pltpu.make_async_copy(source, left.at[number, pl.ds(first, count)], sems.at[3 * number + place])
            )
            copies[-1].start()
        return copies

    first_copies = fill((du0, du1, du2), 0)
    second_copies = fill((h0, h1, h2), 1)
    for place, half in enumerate((where_ref[0], 1 - where_ref[0])):
        second_copies.append(
            pltpu.make_async_copy(e_ref.at[own_half(half, rows), :], right.at[pl.ds(place * rows, rows)], sems.at[6 + place])
        )
        second_copies[-1].start()
    for source, (first, count) in zip((a0, a1, a2), places):
        a_all[first : first + count] = source[...]
    for base, copies, others in ((0, first_copies, a_all), (hidden, second_copies, right)):
        for copy in copies:
            copy.wait()
        for first in range(0, hidden, chunk):
            product = dot_tn(others[...], left[1 if base else 0, :, first : first + chunk])
            columns = slice(base + first, base + first + chunk)
            store_parts(product, put_columns(keep_ref, columns), put_columns(send_ref, columns), core, parts)
            stage.send_columns((keep_ref, send_ref), columns, columns.stop == 2 * hidden)


def attend_back_scratch(heads, keys):
    pairs = heads // 2
    return [
        pltpu.VMEM((heads, keys, 128), BF16),
        pltpu.VMEM((heads, keys, 128), BF16),
        pltpu.VMEM((heads, BLOCK, 128), BF16),
        pltpu.VMEM((pairs, 128, BLOCK), F32),
        pltpu.VMEM((pairs, 128, keys), F32),
        pltpu.VMEM((pairs, 128, keys), F32),
        pltpu.VMEM((pairs, 128, keys), BF16),
        pltpu.VMEM((pairs, 128, BLOCK), BF16),
        pltpu.VMEM((pairs, 128, BLOCK), BF16),
    ]


def after_feed(side, stream, kept, first, second, e3, norms, wo, wp, ahead=()):
    rows, width = stream.shape
    cols = wo.shape[0]
    return call(
        after_feed_kernel_of_side,
        (shape((rows, width), F32), shape((rows, width), BF16), shape((rows, cols), BF16), shape((rows, cols), BF16), shape((2, width), F32)),
        far="FFFFHNFO",
        flops=4 * rows * width * cols,
    )(side, stream, kept, first, second, e3, norms, wo, wp, ahead=ahead)


def after_feed_kernel_of_side(stage, side_ref, *refs):
    after_feed_kernel(stage, *refs)


def cross_back_kernel(
    parts, heads, stage, where_ref, starts_ref, doo, don, qao, kvo, oo, qan, kvn, on, dock, memory, a2, e2, stream, grad,
    wq, wr, norms, wo, wp,
    keep_d, send_d, keep_c, send_c, dkvo, dkvn, out, e1, own, other, d, dqo, dqn, *scratch
):
    attend_back_kernel(False, heads, heads // 2, stage, where_ref, starts_ref, qao, kvo, doo, oo, dock, dqo, dkvo, *scratch)
    stage.send(dkvo)
    attention_grads_kernel(parts, stage, where_ref, memory, a2, e2, dqo, dkvo, oo, keep_d, send_d)
    attend_back_kernel(False, heads, heads // 2, stage, where_ref, starts_ref, qan, kvn, don, on, dock, dqn, dkvn, *scratch)
    stage.send(dkvn)
    attention_grads_kernel(parts, stage, where_ref, memory, a2, e2, dqn, dkvn, on, keep_c, send_c)
    after_cross_back_kernel(stage, stream, grad, dqn, dqo, wq, wr, norms, wo, wp, out, e1, own, other, d)


def cross_back(where, parts, starts, doo, don, qao, kvo, oo, qan, kvn, on, dock, memory, a2, e2, stream, grad, wq, wr, norms, wo, wp, ahead=()):
    rows, width = stream.shape
    keys, cols = kvo.shape[0], wo.shape[0]
    heads = cols // HEAD_DIM
    part = shape((width // 2, 4 * cols), BF16)
    narrow = shape((rows, cols), BF16)
    return call(
        partial(cross_back_kernel, parts, heads),
        (
            part, part, part, part, shape((keys, 2 * cols), BF16), shape((keys, 2 * cols), BF16), shape((rows, width), F32),
            shape((rows, width), BF16), narrow, narrow, shape((2, width), F32),
        ),
        far="NNVVVFFFVFFNFNFQNFO",
        far_out="FFFFVVFFFNN",
        flops=120 * rows * keys * cols,
        scalars=2,
        limit=36,
        scratch=[pltpu.VMEM((rows, cols), BF16)] * 2 + attend_back_scratch(heads, keys),
    )(where, starts, doo, don, qao, kvo, oo, qan, kvn, on, dock, memory, a2, e2, stream, grad, wq, wr, norms, wo, wp, ahead=ahead)


def self_other_back_kernel(parts, heads, stage, where_ref, starts_ref, do, qa, kv, o, dock, a1, e1, dq, dkv, keep, send, *scratch):
    attend_back_kernel(True, heads, heads // 2, stage, where_ref, starts_ref, qa, kv, do, o, dock, dq, dkv, *scratch)
    stage.send(dq, dkv)
    attention_grads_kernel(parts, stage, where_ref, a1, a1, e1, dq, dkv, o, keep, send)


def self_other_back(where, parts, starts, do, qa, kv, o, dock, a1, e1, ahead=()):
    rows, cols = do.shape
    keys, width = a1.shape
    heads = cols // HEAD_DIM
    part = shape((width // 2, 4 * cols), BF16)
    return call(
        partial(self_other_back_kernel, parts, heads),
        (shape((rows, cols), BF16), shape((keys, 2 * cols), BF16), part, part),
        far="NVVVVFF",
        far_out="FFFF",
        flops=56 * rows * keys * cols,
        scalars=2,
        scratch=attend_back_scratch(heads, keys),
    )(where, starts, do, qa, kv, o, dock, a1, e1, ahead=ahead)


def self_own_back_kernel(
    parts, heads, stage, where_ref, starts_ref, do, qa, kv, o, dock, a1, e1, dqo, dkvo, wkv, wlw, wq, wr, x,
    keep_r, send_r, d, keep, send, dq, dkv, *scratch
):
    attend_back_kernel(True, heads, heads // 2, stage, where_ref, starts_ref, qa, kv, do, o, dock, dq, dkv, *scratch)
    attention_grads_kernel(parts, stage, where_ref, a1, a1, e1, dq, dkv, o, keep, send)
    key_value_back_kernel(True, stage, where_ref, dkv, dkvo, wkv, wlw, dq, dqo, wq, wr, x, send_r, keep_r, d)


def self_own_back(where, parts, starts, do, qa, kv, o, dock, a1, e1, dqo, dkvo, wkv, wlw, wq, wr, x, ahead=()):
    rows, cols = do.shape
    keys, width = a1.shape
    heads = cols // HEAD_DIM
    part = shape((width // 2, 4 * cols), BF16)
    return call(
        partial(self_own_back_kernel, parts, heads),
        (shape((rows, width), F32), shape((rows, width), BF16), shape((2, width), F32), part, part),
        far="FFFFFFFFFFKFQF",
        far_out="FNNFF",
        flops=74 * rows * keys * cols,
        scalars=2,
        limit=36,
        scratch=[pltpu.VMEM((rows, cols), BF16), pltpu.VMEM((keys, 2 * cols), BF16)] + attend_back_scratch(heads, keys),
    )(where, starts, do, qa, kv, o, dock, a1, e1, dqo, dkvo, wkv, wlw, wq, wr, x, ahead=ahead)


def feed_grads(where, parts, e, a, du, h, chunk=768):
    rows, width = a[0].shape
    hidden = du[0].shape[1]
    out = shape((width // 2, 2 * hidden), BF16)
    return call(
        partial(feed_grads_kernel, parts, chunk),
        (out, out),
        far="NNNXXXXXXX",
        far_out="FF",
        flops=8 * rows * width * hidden,
        limit=36,
        scratch=[
            pltpu.VMEM((2 * rows, width), BF16), pltpu.VMEM((2, 2 * rows, hidden), BF16), pltpu.VMEM((2 * rows, width), BF16),
            pltpu.SemaphoreType.DMA((8,)),
        ],
    )(where, *a, *du, *h, e)


def swap_tensor(value):
    return lax.ppermute(value, "tensor", [(0, 1), (1, 0)])


def swap_dp(value, bit):
    count = lax.axis_size("dp")
    return lax.ppermute(value, "dp", [(number, number ^ (1 << bit)) for number in range(count)])


def after(value, *others):
    return lax.optimization_barrier((value,) + others)[0] if others else value


def quarter_of(query, key, value, out, part):
    width, cols = query.shape
    rows = width // 4
    pieces = [lax.dynamic_slice_in_dim(weight, part * rows, rows, 0) for weight in (query, key, value)]
    pieces.append(lax.dynamic_slice(out, ((part % 2) * rows, (part // 2) * cols), (rows, cols)))
    return jnp.concatenate(pieces, axis=1)


class Sum:
    def __init__(self, *terms):
        self.terms = [term if isinstance(term, tuple) else (term, 0) for term in terms]
        last, first = self.terms[-1]
        self.rows = last.shape[0]

    def cut(self, first, rows):
        return Sum.of([(array, start + first) for array, start in self.terms], rows)

    @classmethod
    def of(cls, terms, rows):
        made = cls.__new__(cls)
        made.terms, made.rows = terms, rows
        return made

    def plus(self, array):
        return Sum.of(self.terms + [(array, 0)], self.rows)

    def formed(self, dtype=BF16):
        pieces = [
            array.astype(F32) if array.shape[0] == self.rows else lax.dynamic_slice_in_dim(array, start, self.rows, 0).astype(F32)
            for array, start in self.terms
        ]
        return sum(pieces[1:], pieces[0]).astype(dtype)

    def tied(self, *others):
        arrays = [array for array, _ in self.terms]
        made = lax.optimization_barrier((tuple(arrays), others))
        return (Sum.of([(array, start) for array, (_, start) in zip(made[0], self.terms)], self.rows),) + tuple(made[1])


def halve(value, bit, place):
    rows = value.rows // 2
    mine = (place >> bit) & 1
    return value.cut(mine * rows, rows), swap_dp(value.cut((1 - mine) * rows, rows).formed(), bit)


def add(left, right):
    return (left.astype(F32) + right.astype(F32)).astype(BF16)


def shards(
    target_tokens, memory_tokens, output_grad, target_segments, memory_segments,
    norm1_gain, norm1_shift, self_query, self_key, self_value, self_out,
    norm2_gain, norm2_shift, cross_query, cross_key, cross_value, cross_out,
    norm3_gain, norm3_shift, ffn_up, ffn_down,
):
    _, length, width = target_tokens.shape
    cols = self_query.shape[1]
    parts = lax.axis_size("dp")
    bits = parts.bit_length() - 1
    place = lax.axis_index("dp")
    side = lax.axis_index("tensor")
    core = place & 1
    x = target_tokens[0]
    memory = memory_tokens[0]
    e3 = output_grad[0]
    norms = jnp.stack([norm1_gain, norm1_shift, norm2_gain, norm2_shift, norm3_gain, norm3_shift])
    tie = lax.optimization_barrier
    side_one = side.astype(jnp.int32).reshape(1)
    where = jnp.stack([side, core]).astype(jnp.int32)

    part = place % 4
    self_first = swap_tensor(quarter_of(self_query, self_key, self_value, self_out, part))
    cross_quarter = quarter_of(cross_query, cross_key, cross_value, cross_out, part)
    self_wo, cross_wo = self_out, cross_out
    self_wkv = jnp.concatenate([self_key, self_value], axis=1)
    cross_wkv = jnp.concatenate([cross_key, cross_value], axis=1)

    numbers = jnp.arange(DOCS + 1)[:, None]
    target_starts = jnp.sum(target_segments < numbers, 1).astype(jnp.int32)
    memory_starts = jnp.sum(memory_segments < numbers, 1).astype(jnp.int32)
    self_starts = jnp.stack([target_starts, target_starts])
    cross_starts = jnp.stack([target_starts, memory_starts])
    lane = jnp.arange(128) % 64
    hot = target_segments[0][:, None] == lane[None, :]
    doc_rows = jnp.where(hot, LOW, 0.0).astype(BF16)
    doc_target = jnp.where((lane < DOCS)[None, :] & ~hot, 1.0, 0.0).astype(BF16)
    doc_memory = jnp.where(
        (lane < DOCS)[None, :] & (memory_segments[0][:, None] != lane[None, :]), 1.0, 0.0
    ).astype(BF16)

    dh, kv2_own = prepare(e3, ffn_down, memory, cross_wkv)
    self_first, cross_quarter, x_now, dh, kv2_own, doc_rows, doc_target, doc_memory, self_wkv, norms = tie(
        (self_first, cross_quarter, x, dh, kv2_own, doc_rows, doc_target, doc_memory, self_wkv, norms)
    )
    self_second = swap_dp(self_first, 1)
    self_third = swap_dp(self_first, 0)
    cross_first = swap_tensor(cross_quarter)
    o1_own, qa1_own, a1, kv_own, o1_own_far = self_own(
        side_one, self_starts, x_now, norms, self_query, self_wkv, doc_rows, doc_target
    )
    self_second, o1_own, cross_first = tie((self_second, o1_own, cross_first))
    self_fourth = swap_dp(self_second, 0)
    self_fourth, self_third = tie((self_fourth, self_third))
    self_pieces = (self_first, self_third, self_second, self_fourth)
    cross_first, self_pieces = tie((cross_first, self_pieces))
    side_part = jnp.stack([side, part]).astype(jnp.int32)
    cross_second = swap_dp(cross_first, 1)
    cross_third = swap_dp(cross_first, 0)
    o1_oth, qa1_oth, kv_oth, stream1, a2, q2_own, self_two, kv2_near, memory_docs_near = self_other(
        side_part, self_starts, a1, self_pieces, doc_rows, doc_target, x, o1_own, self_wo, norms, cross_query,
        ahead=((kv2_own, "F"), (doc_memory, "F")),
    )
    cross_second, q2_own = tie((cross_second, q2_own))
    cross_fourth = swap_dp(cross_second, 0)
    o2_own, qa2_own, o2_own_far = cross_own(side_one, cross_starts, kv2_near, q2_own, doc_rows, memory_docs_near)
    cross_fourth, cross_third, o2_own = tie((cross_fourth, cross_third, o2_own))
    cross_pieces = (cross_first, cross_third, cross_second, cross_fourth)
    o2_oth, qa2_oth, kv2_oth, stream2, a3, a3_first, a3_second, cross_two = cross_other(
        side_part, cross_starts, memory, cross_pieces, a2, doc_rows, doc_memory, stream1, o2_own, cross_wo, norms
    )

    first_block = (side * (length // 2 // BLOCK)).astype(jnp.int32).reshape(1)
    other_block = length // 2 // BLOCK - first_block
    a3_first, a3_second = swap_tensor(a3_first), swap_tensor(a3_second)
    h_own, du_own, out_own, r3_own = feed(first_block, a3, dh, ffn_up, ffn_down, F32)
    a3_first, r3_own = tie((a3_first, r3_own))
    h_first, du_first, out_first, r3_first = feed(other_block, a3_first, dh, ffn_up, ffn_down, BF16)
    a3_second, r3_first = tie((a3_second, r3_first))
    r3_first = swap_tensor(r3_first)
    h_second, du_second, out_oth, r3_second = feed(other_block + 1, a3_second, dh, ffn_up, ffn_down, BF16, out_first)
    r3_second = swap_tensor(r3_second)
    aligned = (width // parts) % 16 == 0
    static_parts = parts if aligned else 2
    keep_f, send_f = feed_grads(
        where, static_parts, e3, (a3, a3_first, a3_second), (du_own, du_first, du_second), (h_own, h_first, h_second)
    )
    r3_first, r3_second, keep_f, send_f = tie((r3_first, r3_second, keep_f, send_f))

    def reordered(keep, send):
        if aligned:
            return keep, send
        whole = jnp.where(core == 0, jnp.concatenate([keep, send]), jnp.concatenate([send, keep]))
        order = [bit_reversed(number, bits) for number in range(parts)]
        whole = jnp.take(whole.reshape(parts, width // parts, -1), jnp.array(order), axis=0)
        whole = whole.reshape(2, width // 2, -1)
        pick = lambda index: lax.dynamic_index_in_dim(whole, index, 0, False)
        return pick(core), pick(1 - core)

    def swap_core(keep, send):
        keep, send = reordered(keep, send)
        return keep, swap_dp(send, 0)

    keep_f, recv_f = swap_core(keep_f, send_f)
    grad2, e2, do2_own, do2_oth, d3, qa2_near, kv2_near, o2_near, memory_docs_near = after_feed(
        side_one, stream2, r3_own, r3_first, r3_second, e3, norms, cross_wo, cross_two,
        ahead=((qa2_oth, "F"), (kv2_oth, "F"), (o2_oth, "F"), (doc_memory, "F")),
    )
    do2_oth, keep_f, recv_f, out_oth = tie((do2_oth, keep_f, recv_f, out_oth))
    out_recv = swap_tensor(out_oth)
    sum_f, recv_f = halve(Sum(keep_f, recv_f), 1, place)
    (
        keep_d, send_d, keep_c, send_c, dkv2_oth, dkv2_own, grad1, e1, do1_own, do1_oth, d2, wkv_near, wkv2_near
    ) = cross_back(
        where, static_parts, cross_starts, do2_oth, do2_own, qa2_near, kv2_near, o2_near, qa2_own, kv2_own, o2_own_far,
        memory_docs_near, memory, a2, e2, stream1, grad2, cross_query, cross_two, norms, self_wo, self_two,
        ahead=((cross_wkv, "F"), (cross_two, "K")),
    )
    keep_d, send_d, keep_c, send_c, recv_f, out_recv = tie((keep_d, send_d, keep_c, send_c, recv_f, out_recv))
    keep_d, recv_d = swap_core(keep_d, send_d)
    keep_c, recv_c = swap_core(keep_c, send_c)
    sum_f = sum_f.plus(recv_f)
    if bits > 2:
        sum_f, recv_f = halve(sum_f, 2, place)
    send_m, keep_m, qa1_near, kv_near, o1_near, target_near = key_value_back(
        side_one, dkv2_own, dkv2_oth, wkv_near, wkv2_near,
        ahead=((qa1_oth, "F"), (kv_oth, "F"), (o1_oth, "F"), (doc_target, "F")),
    )

    do1_oth, keep_d, recv_d, keep_c, recv_c, send_m = tie((do1_oth, keep_d, recv_d, keep_c, recv_c, send_m))
    sum_d, recv_d = halve(Sum(keep_d, recv_d), 1, place)
    recv_m = swap_tensor(send_m)
    dq1_oth, dkv1_oth, keep_t, send_t = self_other_back(
        where, static_parts, self_starts, do1_oth, qa1_near, kv_near, o1_near, target_near, a1, e1
    )
    keep_t, send_t, recv_d, recv_m, recv_f = tie((keep_t, send_t, recv_d, recv_m, recv_f))
    keep_t, recv_t = swap_core(keep_t, send_t)
    do1_own, keep_t, recv_t = tie((do1_own, keep_t, recv_t))
    sum_t, recv_t = halve(Sum(keep_t, recv_t), 1, place)
    sum_c, recv_c = halve(Sum(keep_c, recv_c), 1, place)
    sent_d = swap_tensor(sum_d.plus(recv_d).formed())
    keep_r, send_r, d1, keep_s, send_s, half_near, grad1_near = self_own_back(
        where, static_parts, self_starts, do1_own, qa1_own, kv_own, o1_own_far, doc_target, a1, e1,
        dq1_oth, dkv1_oth, self_wkv, self_two, self_query, self_two, x, ahead=((x, "H"), (grad1, "F")),
    )
    keep_s, send_s, d1, recv_c, sent_d, recv_t, recv_f = tie((keep_s, send_s, d1, recv_c, sent_d, recv_t, recv_f))
    keep_s, recv_s = swap_core(keep_s, send_s)
    sent_t = swap_tensor(sum_t.plus(recv_t).formed())
    sum_c = sum_c.plus(recv_c).plus(sent_d)
    if bits > 2:
        sum_c, recv_c = halve(sum_c, 2, place)
    lines = jnp.concatenate([jnp.concatenate([d[0:1], d[1:2]], axis=1) for d in (d1, d2, d3)], axis=0)
    lines = jnp.pad(lines, ((0, NORM_ROWS - 3), (0, 0))).astype(BF16)
    lines = add(lines, swap_tensor(lines))
    lines = add(lines, swap_dp(lines, 0))
    keep_s, recv_s, send_r, lines, out_recv = tie((keep_s, recv_s, send_r, lines, out_recv))
    recv_r = swap_tensor(send_r)
    layer_output = (stream2 + out_own + out_recv.astype(F32)).astype(BF16)
    if bits > 2:
        sum_f = sum_f.plus(recv_f)
    if bits > 3:
        sum_f, recv_f = halve(sum_f, 3, place)
    sum_s = Sum(keep_s, recv_s)

    def halve_with_lines(value, lines, bit):
        rows = value.rows // 2
        mine = (place >> bit) & 1
        message = jnp.concatenate([value.cut((1 - mine) * rows, rows).formed(), lines], axis=0)
        received = swap_dp(message, bit)
        return value.cut(mine * rows, rows).plus(received), add(lines, received[rows:])

    sum_s, lines = halve_with_lines(sum_s, lines, 1)
    sum_s, lines, sent_t, recv_c, recv_m, layer_output = sum_s.tied(lines, sent_t, recv_c, recv_m, layer_output)
    sum_s = sum_s.plus(sent_t)
    if bits > 2:
        sum_c = sum_c.plus(recv_c)
    for bit in range(3, bits):
        sum_c, recv_c = halve(sum_c, bit, place)
        sum_c = sum_c.plus(recv_c)
    for bit in range(2, bits):
        sum_s, lines = halve_with_lines(sum_s, lines, bit)
        if bit == 2:
            recv_r, lines, recv_f = tie((recv_r, lines, recv_f))
    for bit in range(3, bits):
        sum_f = sum_f.plus(recv_f)
        if bit + 1 < bits:
            sum_f, recv_f = halve(sum_f, bit + 1, place)
    grad_x = input_grad(side_one, half_near, grad1_near, keep_r, recv_r, norms)
    grad_memory = keep_m + recv_m.astype(F32)
    small = lines.astype(F32)
    sum_s, sum_c, sum_f = (value.formed(F32) for value in (sum_s, sum_c, sum_f))

    def four(total):
        pieces = [total[:, number * cols : (number + 1) * cols] for number in range(4)]
        return tuple(pieces[:3]) + (pieces[3].T,)

    hidden = ffn_up.shape[1]
    return (
        (layer_output[None], grad_x[None], grad_memory[None])
        + four(sum_s)
        + four(sum_c)
        + (sum_f[:, :hidden], sum_f[:, hidden:].T)
        + tuple(small[number // 2, (number % 2) * width : (number % 2 + 1) * width] for number in range(6))
    )


def solution(mesh):
    tokens = P("dp", None, None)
    columns = P(None, "tensor")
    rows = P("tensor", None)
    block = (P(), P(), columns, columns, columns, rows)
    in_specs = (tokens,) * 3 + (P("dp", None),) * 2 + block + block + (P(), P(), columns, rows)
    out_rows = P("dp", "tensor")
    out_cols = P("tensor", "dp")
    four = (out_rows, out_rows, out_rows, out_cols)
    out_specs = (P("dp", "tensor", None),) * 3 + four + four + (out_rows, out_cols) + (P(),) * 6
    return jax.shard_map(shards, mesh=mesh, in_specs=in_specs, out_specs=out_specs, check_vma=False)
```

```python
from functools import partial

import jax
import jax.numpy as jnp
from jax import lax
from jax.experimental import pallas as pl
from jax.experimental.pallas import tpu as pltpu
from jax.sharding import PartitionSpec as P

HEAD_DIM = 64
DOCS = 4
BLOCK = 256
LOW = -1e30
NORM_ROWS = 16
SPARE = 12
COST = 0.02
F32 = jnp.float32
BF16 = jnp.bfloat16
MIB = 1024 * 1024


def dot(left, right):
    return jnp.dot(left, right, preferred_element_type=F32)


def dot_nt(left, right):
    return lax.dot_general(left, right, (((1,), (1,)), ((), ())), preferred_element_type=F32)


def dot_tn(left, right):
    return lax.dot_general(left, right, (((0,), (0,)), ((), ())), preferred_element_type=F32)


def normalise(values):
    centered = values - jnp.mean(values, -1, keepdims=True)
    rstd = lax.rsqrt(jnp.mean(centered * centered, -1, keepdims=True) + 1e-05)
    return centered * rstd, rstd


def norm_backward(unit, rstd, gain, cotangent):
    scaled = cotangent * gain
    return rstd * (
        scaled
        - jnp.mean(scaled, -1, keepdims=True)
        - unit * jnp.mean(scaled * unit, -1, keepdims=True)
    )


PARTS = {"Q": (0, 1), "K": (1, 2), "O": (3, 1)}


class Staged:
    def __init__(self, arriving, late, leaving, spare):
        self.arriving, self.late, self.leaving, self.spare, self.sent = arriving, late, leaving, list(spare), []

    def fetch(self):
        for copy in self.late:
            copy.start()
        self.late = []

    def need(self, *refs):
        for number, (ref, copy) in enumerate(self.arriving):
            if copy is not None and any(ref is wanted for wanted in refs):
                copy.wait()
                self.arriving[number] = (ref, None)

    def send(self, *refs):
        for number, (ref, target, sem) in enumerate(self.leaving):
            if target is not None and any(ref is wanted for wanted in refs):
                self.sent.append(pltpu.make_async_copy(ref, target, sem))
                self.sent[-1].start()
                self.leaving[number] = (ref, None, sem)

    def send_columns(self, refs, columns, last):
        for number, (ref, target, sem) in enumerate(self.leaving):
            if target is not None and any(ref is wanted for wanted in refs):
                if not last:
                    sem = self.spare.pop()
                self.sent.append(pltpu.make_async_copy(ref.at[:, columns], target.at[:, columns], sem))
                self.sent[-1].start()
                if last:
                    self.leaving[number] = (ref, None, sem)

    def finish(self):
        self.fetch()
        self.need(*(ref for ref, _ in self.arriving))
        self.send(*(ref for ref, _, _ in self.leaving))
        for copy in self.sent:
            copy.wait()


def call(kernel, out_shape, *, far="", far_out="", flops=0, limit=36, scratch=(), scalars=1):
    shapes = out_shape if isinstance(out_shape, tuple) else (out_shape,)

    def run(*operands, ahead=()):
        vmem = pl.BlockSpec(memory_space=pltpu.VMEM)
        hbm = pl.BlockSpec(memory_space=pltpu.HBM)
        small = pl.BlockSpec(memory_space=pltpu.SMEM)
        arrays = operands[scalars:]
        marks = far.ljust(len(arrays), "N")
        out_marks = far_out.ljust(len(shapes), "N")
        assert len(marks) == len(arrays) and len(out_marks) == len(shapes), (len(arrays), len(shapes))
        also = [number for number, mark in enumerate(out_marks) if mark == "W"]
        copied = [mark not in "NVX" for mark in marks]

        def held(mark, array):
            dims = array.shape
            if mark == "H":
                dims = (dims[0] // 2,) + dims[1:]
            elif mark == "R":
                dims = (shapes[0].shape[0],) + dims[1:]
            elif mark in PARTS:
                dims = (dims[0], dims[1] // 4 * PARTS[mark][1])
            return dims, array.dtype

        def part_of(mark, source, heads):
            if mark == "H":
                rows = source.shape[0] // 2
                return source.at[pl.ds(pl.multiple_of(heads[0][0] * rows, BLOCK), rows)]
            if mark == "R":
                return source.at[pl.ds(pl.multiple_of(heads[0][0] * BLOCK, BLOCK), shapes[0].shape[0])]
            if mark in PARTS:
                quarter = source.shape[1] // 4
                return source.at[:, pl.ds(PARTS[mark][0] * quarter, PARTS[mark][1] * quarter)]
            return source

        extra = [pltpu.VMEM(*held(mark, array)) for mark, array, here in zip(marks, arrays, copied) if here]
        extra += [pltpu.VMEM(item.shape, item.dtype) for mark, item in zip(out_marks, shapes) if mark == "F"]
        copies = len(extra) + len(also) + len(ahead)
        extra.append(pltpu.SemaphoreType.DMA((copies + SPARE,)))

        def wrapped(*refs):
            refs = list(refs)

            def take(count):
                taken = refs[:count]
                del refs[:count]
                return taken

            heads, ins, coming = take(scalars), take(len(arrays)), take(len(ahead))
            outs, seconds, arrived, own = take(len(shapes)), take(len(also)), take(len(ahead)), take(len(scratch))
            buffers, sems = refs[:-1], refs[-1]
            arriving, late, leaving, place = [], [], [], 0
            for number, mark in enumerate(marks):
                if copied[number]:
                    source = part_of(mark, ins[number], heads)
                    ins[number] = buffers.pop(0)
                    copy = pltpu.make_async_copy(source, ins[number], sems.at[place])
                    if mark == "L":
                        late.append(copy)
                    else:
                        copy.start()
                    arriving.append((ins[number], copy))
                    place += 1
            for (_, mark), source, target in zip(ahead, coming, arrived):
                copy = pltpu.make_async_copy(part_of(mark, source, heads), target, sems.at[place])
                copy.start()
                arriving.append((target, copy))
                place += 1
            for number, mark in enumerate(out_marks):
                if mark == "F":
                    target, outs[number] = outs[number], buffers.pop(0)
                    leaving.append((outs[number], target, sems.at[place]))
                    place += 1
            for number, second in zip(also, seconds):
                leaving.append((outs[number], second, sems.at[place]))
                place += 1
            stage = Staged(arriving, late, leaving, [sems.at[copies + number] for number in range(SPARE)])
            kernel(stage, *heads, *ins, *outs, *own)
            stage.finish()

        places = {"F": pltpu.HBM}
        kept = [places[mark](item.shape, item.dtype) if mark in places else item for item, mark in zip(shapes, out_marks)]
        kept += [pltpu.HBM(shapes[number].shape, shapes[number].dtype) for number in also]
        kept += [shape(*held(mark, array)) for array, mark in ahead]
        pinned = [
            array if mark in "NV" else pltpu.with_memory_space_constraint(array, pltpu.HBM)
            for array, mark in zip(arrays, marks)
        ]
        pinned += [pltpu.with_memory_space_constraint(array, pltpu.HBM) for array, _ in ahead]
        results = pl.pallas_call(
            wrapped,
            out_shape=tuple(kept),
            in_specs=[small] * scalars + [vmem if mark in "NV" else hbm for mark in marks] + [hbm] * len(ahead),
            out_specs=tuple(hbm if mark == "F" else vmem for mark in out_marks) + (hbm,) * len(also) + (vmem,) * len(ahead),
            scratch_shapes=list(scratch) + extra,
            compiler_params=pltpu.CompilerParams(vmem_limit_bytes=limit * MIB),
            cost_estimate=pl.CostEstimate(flops=int(COST * flops), bytes_accessed=4096, transcendentals=0),
        )(*operands[:scalars], *pinned)
        return results[0] if len(results) == 1 else results

    return run


def shape(dims, dtype):
    return jax.ShapeDtypeStruct(dims, dtype)


def row_blocks(rows):
    return [slice(first, first + BLOCK) for first in range(0, rows, BLOCK)]


def own_half(side, rows, first=0, count=None):
    count = rows if count is None else count
    return pl.ds(pl.multiple_of(side * rows + first, BLOCK), count)


def vector(ref, number):
    return ref[number : number + 1, :]


def norm_project_kernel(stage, where_ref, x_ref, norms_ref, wq_ref, wkv_ref, a_ref, q_ref, kv_ref):
    stage.need(x_ref)
    stage.fetch()
    for at in row_blocks(x_ref.shape[0]):
        unit, _ = normalise(x_ref[at].astype(F32))
        a_ref[at] = (unit * vector(norms_ref, 0) + vector(norms_ref, 1)).astype(BF16)
    stage.send(a_ref)
    rows = q_ref.shape[0]
    stage.need(wkv_ref)
    for at in row_blocks(x_ref.shape[0]):
        kv_ref[at] = dot(a_ref[at], wkv_ref[...]).astype(BF16)
    stage.send(kv_ref)
    stage.need(wq_ref)
    q_ref[...] = dot(a_ref[own_half(where_ref[0], rows), :], wq_ref[...]).astype(BF16)


def project_kernel(stage, where_ref, a_ref, wq_ref, wkv_ref, q_ref, kv_ref):
    stage.need(a_ref, wkv_ref)
    for at in row_blocks(a_ref.shape[0]):
        kv_ref[at] = dot(a_ref[at], wkv_ref[...]).astype(BF16)
    stage.send(kv_ref)
    stage.need(wq_ref)
    q_ref[...] = dot(a_ref[own_half(where_ref[0], q_ref.shape[0]), :], wq_ref[...]).astype(BF16)


def project_memory_kernel(stage, memory_ref, wkv_ref, kv_ref):
    stage.need(memory_ref, wkv_ref)
    for at in row_blocks(memory_ref.shape[0]):
        kv_ref[at] = dot(memory_ref[at], wkv_ref[...]).astype(BF16)
    stage.send(kv_ref)


def project_both_kernel(stage, memory_ref, wkv_ref, a_ref, wq_ref, q_ref, kv_ref):
    project_memory_kernel(stage, memory_ref, wkv_ref, kv_ref)
    stage.need(a_ref, wq_ref)
    q_ref[...] = dot(a_ref[...], wq_ref[...]).astype(BF16)


def first_doc(starts_ref, row):
    doc = 0
    for number in range(1, DOCS):
        doc = doc + (starts_ref[0, number] <= row).astype(jnp.int32)
    return doc


def key_range(starts_ref, block_number, causal):
    first = block_number * BLOCK
    low = starts_ref[1, first_doc(starts_ref, first)]
    if causal:
        low = low // BLOCK
        return low * BLOCK, block_number - low
    high = starts_ref[1, first_doc(starts_ref, first + BLOCK - 1) + 1]
    low = low // 128 * 128
    count = (high - low + BLOCK - 1) // BLOCK
    return jnp.minimum(low, starts_ref[1, DOCS] - count * BLOCK), count


def lanes(rows):
    return lax.broadcasted_iota(jnp.int32, (rows, 128), 1)


def causal_mask():
    keys = lax.broadcasted_iota(jnp.int32, (BLOCK, BLOCK), 0)
    rows = lax.broadcasted_iota(jnp.int32, (BLOCK, BLOCK), 1)
    return keys <= rows


def pair_of(ref, pair, rows=slice(None)):
    return ref[rows, pair * 128 : (pair + 1) * 128]


def half_of(head):
    return slice(64 * (head % 2), 64 * (head % 2) + 64)


def in_three(value, place, otherwise):
    high = value.astype(BF16)
    rest = value - high.astype(F32)
    middle = rest.astype(BF16)
    low = (rest - middle.astype(F32)).astype(BF16)
    return jnp.where(place == 4, high, jnp.where(place == 5, middle, jnp.where(place == 6, low, otherwise)))


def walk_keys(starts_ref, block_number, causal, one_block):
    first, count = key_range(starts_ref, block_number, causal)
    if causal:
        one_block(block_number * BLOCK, causal_mask())
    lax.fori_loop(0, count, lambda number, _: (one_block(first + number * BLOCK, None), 0)[1], 0)


def attend_kernel(
    causal, heads, group, stage, where_ref, starts_ref, q_ref, kv_ref, docs_ref, dock_ref, o_ref, qa_ref,
    ka_ref, vt_ref, qs_ref, acc_ref, max_ref,
):
    keys = kv_ref.shape[0]
    pairs = heads // 2
    stage.need(kv_ref, dock_ref)
    left = lanes(keys) < 64
    for pair in range(pairs):
        turned = pair_of(kv_ref, pairs + pair).T
        for head in (2 * pair, 2 * pair + 1):
            mine = left if head % 2 == 0 else ~left
            ka_ref[head] = jnp.where(mine, pair_of(kv_ref, pair), dock_ref[...])
            vt_ref[head, :64] = turned[half_of(head)]
            vt_ref[head, 64:] = jnp.ones((16, keys), BF16)
    left = lanes(BLOCK) < 64
    place = lanes(BLOCK) % 64
    stage.need(q_ref, docs_ref)

    def one_step(step, _):
        at_rows = pl.ds(pl.multiple_of(step * BLOCK, BLOCK), BLOCK)
        block_number = where_ref[0] * (q_ref.shape[0] // BLOCK) + step
        docs = docs_ref[pl.ds(pl.multiple_of(block_number * BLOCK, BLOCK), BLOCK), :]
        for head in range(heads):
            mine = left if head % 2 == 0 else ~left
            scaled = pair_of(q_ref, head // 2, at_rows) * jnp.array(HEAD_DIM**-0.5, BF16)
            qs_ref[head] = jnp.where(mine, scaled, docs)
        max_ref[...] = jnp.full_like(max_ref, LOW)
        acc_ref[...] = jnp.zeros_like(acc_ref)

        def one_block(first_key, mask):
            at = pl.ds(pl.multiple_of(first_key, 128), BLOCK)
            for first in range(0, heads, group):
                some = range(first, first + group)
                scores = [dot_nt(ka_ref[head, at, :], qs_ref[head]) for head in some]
                if mask is not None:
                    scores = [jnp.where(mask, score, LOW) for score in scores]
                old = [max_ref[head, 0:1] for head in some]
                new = [jnp.maximum(m, jnp.max(score, 0, keepdims=True)) for m, score in zip(old, scores)]
                weights = [jnp.exp(score - m).astype(BF16) for score, m in zip(scores, new)]
                mixed = [dot(vt_ref[head, :, at], weight) for head, weight in zip(some, weights)]
                shrink = [jnp.exp(m - n) for m, n in zip(old, new)]
                for number_in, head in enumerate(some):
                    acc_ref[head] = acc_ref[head] * shrink[number_in] + mixed[number_in]
                    max_ref[head, 0:1] = new[number_in]

        walk_keys(starts_ref, block_number, causal, one_block)
        for pair in range(pairs):
            both = []
            for head in (2 * pair, 2 * pair + 1):
                mine = left if head % 2 == 0 else ~left
                acc = acc_ref[head]
                total = acc[64:65]
                both.append(acc[:64] / total)
                lse = max_ref[head, 0:1] + jnp.log(total)
                column = jnp.broadcast_to(-lse, (128, BLOCK)).T
                qa_ref[head, at_rows, :] = jnp.where(mine, qs_ref[head], in_three(column, place, docs))
            o_ref[at_rows, pair * 128 : (pair + 1) * 128] = jnp.concatenate(both, 0).T.astype(BF16)
        return 0

    lax.fori_loop(0, q_ref.shape[0] // BLOCK, one_step, 0)
    stage.send(o_ref, qa_ref)


def attend_back_kernel(
    causal, heads, group, stage, where_ref, starts_ref, qa_ref, kv_ref, do_ref, o_ref, dock_ref, dq_ref, dkv_ref,
    ka_ref, va_ref, da_ref, dqa_ref, dka_ref, dva_ref, kt_ref, qt_ref, dt_ref,
):
    keys = kv_ref.shape[0]
    pairs = heads // 2
    stage.need(kv_ref, dock_ref)
    left = lanes(keys) < 64
    place = lanes(keys) % 64
    ones = jnp.where((place >= 4) & (place < 7), 1.0, 0.0).astype(BF16)
    for head in range(heads):
        mine = left if head % 2 == 0 else ~left
        ka_ref[head] = jnp.where(mine, pair_of(kv_ref, head // 2), dock_ref[...] + ones)
        va_ref[head] = jnp.where(mine, pair_of(kv_ref, pairs + head // 2), ones)
    for pair in range(pairs):
        kt_ref[pair] = pair_of(kv_ref, pair).T
    dka_ref[...] = jnp.zeros_like(dka_ref)
    dva_ref[...] = jnp.zeros_like(dva_ref)
    stage.need(qa_ref, o_ref, do_ref)
    stage.fetch()
    left = lanes(BLOCK) < 64
    place = lanes(BLOCK) % 64

    def one_step(step, _):
        at_rows = pl.ds(pl.multiple_of(step * BLOCK, BLOCK), BLOCK)
        block_number = where_ref[0] * (do_ref.shape[0] // BLOCK) + step
        for pair in range(pairs):
            grad = pair_of(do_ref, pair, at_rows)
            dt_ref[pair] = grad.T
            product = grad.astype(F32) * pair_of(o_ref, pair, at_rows).astype(F32)
            for head in (2 * pair, 2 * pair + 1):
                mine = left if head % 2 == 0 else ~left
                delta = -jnp.sum(jnp.where(mine, product, 0.0), -1, keepdims=True)
                delta = jnp.broadcast_to(delta, (BLOCK, 128))
                da_ref[head] = jnp.where(mine, grad, in_three(delta, place, jnp.zeros((), BF16)))
            qt_ref[pair] = jnp.where(left, qa_ref[2 * pair, at_rows, :], qa_ref[2 * pair + 1, at_rows, :]).T
        dqa_ref[...] = jnp.zeros_like(dqa_ref)

        def one_block(first_key, mask):
            at = pl.ds(pl.multiple_of(first_key, 128), BLOCK)
            for first in range(0, heads, group):
                some = range(first, first + group)
                scores = [dot_nt(ka_ref[head, at, :], qa_ref[head, at_rows, :]) for head in some]
                grads = [dot_nt(va_ref[head, at, :], da_ref[head]) for head in some]
                if mask is not None:
                    scores = [jnp.where(mask, score, LOW) for score in scores]
                weights = [jnp.exp(score) for score in scores]
                grads = [(weight * grad).astype(BF16) for weight, grad in zip(weights, grads)]
                weights = [weight.astype(BF16) for weight in weights]
                values = [dot_nt(dt_ref[head // 2, half_of(head)], weight) for head, weight in zip(some, weights)]
                kept = [dot_nt(qt_ref[head // 2, half_of(head)], grad) for head, grad in zip(some, grads)]
                asked = [dot(kt_ref[head // 2, half_of(head), at], grad) for head, grad in zip(some, grads)]
                for number_in, head in enumerate(some):
                    dva_ref[head // 2, half_of(head), at] += values[number_in]
                    dka_ref[head // 2, half_of(head), at] += kept[number_in]
                    dqa_ref[head // 2, half_of(head)] += asked[number_in]

        walk_keys(starts_ref, block_number, causal, one_block)
        for pair in range(pairs):
            dq_ref[at_rows, pair * 128 : (pair + 1) * 128] = (dqa_ref[pair].T * HEAD_DIM**-0.5).astype(BF16)
        return 0

    lax.fori_loop(0, do_ref.shape[0] // BLOCK, one_step, 0)
    for pair in range(pairs):
        dkv_ref[:, pair * 128 : (pair + 1) * 128] = dka_ref[pair].astype(BF16).T
        dkv_ref[:, (pairs + pair) * 128 : (pairs + pair + 1) * 128] = dva_ref[pair].astype(BF16).T


def out_project(own, other, own_ref, other_ref):
    half = other_ref.shape[1]
    folded = [dot(other, other_ref[:half]), dot(other, other_ref[half:])]
    return dot(own, own_ref[...]) + jnp.concatenate(folded, axis=1)


def after_self_kernel(stage, x_ref, own_ref, other_ref, wo_ref, wp_ref, norms_ref, wq_ref, s_ref, a_ref, q_ref):
    stage.need(x_ref, own_ref, wo_ref, wp_ref)
    rows = s_ref.shape[0]
    for at in row_blocks(rows):
        stream = x_ref[at].astype(F32) + out_project(own_ref[at], other_ref[at], wo_ref, wp_ref)
        s_ref[at] = stream
        unit, _ = normalise(stream)
        a_ref[at] = (unit * vector(norms_ref, 2) + vector(norms_ref, 3)).astype(BF16)
    stage.send(s_ref, a_ref)
    stage.need(wq_ref)
    q_ref[...] = dot(a_ref[...], wq_ref[...]).astype(BF16)


def after_cross_kernel(stage, s_ref, own_ref, other_ref, wo_ref, wp_ref, norms_ref, t_ref, a_ref, *parts):
    stage.need(s_ref, own_ref, wo_ref, wp_ref)
    for at in row_blocks(s_ref.shape[0]):
        stream = s_ref[at] + out_project(own_ref[at], other_ref[at], wo_ref, wp_ref)
        t_ref[at] = stream
        unit, _ = normalise(stream)
        a_ref[at] = (unit * vector(norms_ref, 4) + vector(norms_ref, 5)).astype(BF16)
        parts[at.start // BLOCK][...] = a_ref[at]


def prepare_kernel(stage, e_ref, down_ref, memory_ref, wkv_ref, dh_ref, kv_ref):
    stage.need(e_ref, down_ref)
    for at in row_blocks(e_ref.shape[0]):
        dh_ref[at] = dot_nt(e_ref[at], down_ref[...]).astype(BF16)
    stage.send(dh_ref)
    project_memory_kernel(stage, memory_ref, wkv_ref, kv_ref)


def prepare(e, down, memory, wkv, ahead=()):
    rows, width = e.shape
    hidden = down.shape[0]
    return call(
        prepare_kernel,
        (shape((rows, hidden), BF16), shape((memory.shape[0], wkv.shape[1]), BF16)),
        far="FFFF",
        far_out="FF",
        flops=2 * rows * width * hidden,
        scalars=0,
    )(e, down, memory, wkv, ahead=ahead)


def attend_scratch(heads, keys):
    return [
        pltpu.VMEM((heads, keys, 128), BF16),
        pltpu.VMEM((heads, 80, keys), BF16),
        pltpu.VMEM((heads, BLOCK, 128), BF16),
        pltpu.VMEM((heads, 80, BLOCK), F32),
        pltpu.VMEM((heads, 8, BLOCK), F32),
    ]


def self_own_kernel(heads, stage, side_ref, starts_ref, x, norms, wq, wkv, docs, dock, o, qa, a, kv, q, *scratch):
    norm_project_kernel(stage, side_ref, x, norms, wq, wkv, a, q, kv)
    attend_kernel(True, heads, heads, stage, side_ref, starts_ref, q, kv, docs, dock, o, qa, *scratch)


def self_own(side, starts, x, norms, wq, wkv, docs, dock, ahead=()):
    keys, width = x.shape
    rows, cols = keys // 2, wq.shape[1]
    heads = cols // HEAD_DIM
    return call(
        partial(self_own_kernel, heads),
        (shape((rows, cols), BF16), shape((heads, rows, 128), BF16), shape((keys, width), BF16), shape((keys, 2 * cols), BF16)),
        far="FNFFFF",
        far_out="WFFF",
        flops=5 * keys * width * cols + 16 * rows * keys * cols,
        scalars=2,
        scratch=[pltpu.VMEM((rows, cols), BF16)] + attend_scratch(heads, keys),
    )(side, starts, x, norms, wq, wkv, docs, dock, ahead=ahead)


def gather(where_ref, pieces, whole, sems):
    rows = pieces[0].shape[0]
    targets = [whole.at[pl.ds(number * rows, rows)] for number in range(4)]
    for number in range(4):
        for place in range(4):
            @pl.when((where_ref[1] ^ number) == place)
            def _():
                pltpu.make_async_copy(pieces[place], targets[number], sems.at[number]).start()

    return [pltpu.make_async_copy(pieces[0], targets[number], sems.at[number]) for number in range(4)]


def split_weights(whole):
    cols = whole.shape[1] // 4
    return whole.at[:, pl.ds(0, cols)], whole.at[:, pl.ds(cols, 2 * cols)], whole.at[:, pl.ds(3 * cols, cols)]


def self_other_kernel(
    heads, stage, side_ref, starts_ref, a, p0, p1, p2, p3, docs, dock, x, own, wo, norms, wc,
    o, qa, kv, stream, a2, q2, whole, q, sems, *scratch
):
    waits = gather(side_ref, (p0, p1, p2, p3), whole, sems)
    stage.need(a)
    for copy in waits:
        copy.wait()
    stage.fetch()
    stage.send(whole)
    wq, wkv, wp = split_weights(whole)
    project_kernel(stage, side_ref, a, wq, wkv, q, kv)
    attend_kernel(True, heads, heads, stage, side_ref, starts_ref, q, kv, docs, dock, o, qa, *scratch)
    after_self_kernel(stage, x, own, o, wo, wp, norms, wc, stream, a2, q2)


def self_other(where, starts, a, pieces, docs, dock, x, own, wo, norms, wc, ahead=()):
    keys, width = a.shape
    rows, cols = own.shape
    heads = cols // HEAD_DIM
    return call(
        partial(self_other_kernel, heads),
        (
            shape((rows, cols), BF16), shape((heads, rows, 128), BF16), shape((keys, 2 * cols), BF16),
            shape((rows, width), F32), shape((rows, width), BF16), shape((rows, cols), BF16), shape((width, 4 * cols), BF16),
        ),
        far="FXXXXLLHNLNL",
        far_out="FFFFFNF",
        flops=5 * keys * width * cols + 16 * rows * keys * cols,
        scalars=2,
        scratch=[pltpu.VMEM((rows, cols), BF16), pltpu.SemaphoreType.DMA((4,))] + attend_scratch(heads, keys),
    )(where, starts, a, *pieces, docs, dock, x, own, wo, norms, wc, ahead=ahead)


def cross_own_kernel(heads, stage, side_ref, starts_ref, kv, q, docs, dock, o, qa, *scratch):
    attend_kernel(False, heads, heads, stage, side_ref, starts_ref, q, kv, docs, dock, o, qa, *scratch)


def cross_own(side, starts, kv, q, docs, dock, ahead=()):
    keys = kv.shape[0]
    rows, cols = q.shape
    heads = cols // HEAD_DIM
    return call(
        partial(cross_own_kernel, heads),
        (shape((rows, cols), BF16), shape((heads, rows, 128), BF16)),
        far="VNFV",
        far_out="WF",
        flops=16 * rows * keys * cols,
        scalars=2,
        scratch=attend_scratch(heads, keys),
    )(side, starts, kv, q, docs, dock, ahead=ahead)


def cross_other_kernel(
    heads, stage, side_ref, starts_ref, memory, p0, p1, p2, p3, a, docs, dock, stream, own, wo, norms,
    o, qa, kv, after, a3, first, second, whole, q, sems, *scratch
):
    waits = gather(side_ref, (p0, p1, p2, p3), whole, sems)
    stage.need(memory)
    for copy in waits:
        copy.wait()
    stage.fetch()
    stage.send(whole)
    wq, wkv, wp = split_weights(whole)
    project_both_kernel(stage, memory, wkv, a, wq, q, kv)
    attend_kernel(False, heads, heads, stage, side_ref, starts_ref, q, kv, docs, dock, o, qa, *scratch)
    after_cross_kernel(stage, stream, own, o, wo, wp, norms, after, a3, first, second)


def cross_other(where, starts, memory, pieces, a, docs, dock, stream, own, wo, norms, ahead=()):
    keys, width = memory.shape
    rows, cols = own.shape
    heads = cols // HEAD_DIM
    half = shape((BLOCK, width), BF16)
    return call(
        partial(cross_other_kernel, heads),
        (
            shape((rows, cols), BF16), shape((heads, rows, 128), BF16), shape((keys, 2 * cols), BF16),
            shape((rows, width), F32), shape((rows, width), BF16), half, half, shape((width, 4 * cols), BF16),
        ),
        far="FXXXXLLLLNLN",
        far_out="FFFFNNNF",
        flops=5 * keys * width * cols + 16 * rows * keys * cols,
        scalars=2,
        scratch=[pltpu.VMEM((rows, cols), BF16), pltpu.SemaphoreType.DMA((4,))] + attend_scratch(heads, keys),
    )(where, starts, memory, *pieces, a, docs, dock, stream, own, wo, norms, ahead=ahead)


def feed_kernel(chunk, joined, stage, where_ref, a_ref, dh_ref, up_ref, down_ref, *refs):
    if joined:
        before_ref, refs = refs[0], refs[1:]
    h_ref, du_ref, out_ref, r_ref, *sums = refs
    rows = a_ref.shape[0]
    if joined:
        out_ref[:rows] = before_ref[...]
        out_ref = out_ref.at[pl.ds(rows, rows)]
    out_acc, r_acc = sums if sums else (out_ref, r_ref)
    stage.need(a_ref, up_ref)
    stage.fetch()
    chunks = [slice(first, first + chunk) for first in range(0, up_ref.shape[1], chunk)]
    for some in chunks:
        for at in row_blocks(rows):
            u = dot(a_ref[at], up_ref[:, some])
            if some.start == 0 and at.start == 0:
                stage.need(dh_ref, down_ref)
            square = u * u
            curve = jnp.tanh(u * (0.7978845608028654 + 0.035677408136300125 * square))
            half = 0.5 + 0.5 * curve
            slope = half + (0.5 * u) * (1.0 - curve * curve) * (0.7978845608028654 + 0.10703222440890037 * square)
            h_ref[at, some] = (u * half).astype(BF16)
            du_ref[at, some] = (dh_ref[at, some].astype(F32) * slope).astype(BF16)
        stage.send_columns((h_ref, du_ref), some, some is chunks[-1])
        out_part = dot(h_ref[:, some], down_ref[some])
        if some.start == 0:
            out_acc[...] = out_part
        elif some is chunks[-1]:
            out_ref[...] = (out_acc[...] + out_part).astype(out_ref.dtype)
            stage.send(out_ref)
        else:
            out_acc[...] += out_part
        r_part = dot_nt(du_ref[:, some], up_ref[:, some])
        if some.start == 0:
            r_acc[...] = r_part
        elif some is chunks[-1]:
            r_ref[...] = (r_acc[...] + r_part).astype(r_ref.dtype)
        else:
            r_acc[...] += r_part


def feed(where, a, dh, up, down, dtype, *before, chunk=512, ahead=()):
    rows, width = a.shape
    hidden = up.shape[1]
    return call(
        partial(feed_kernel, chunk, len(before) > 0),
        (shape((rows, hidden), BF16),) * 2 + (shape(((1 + len(before)) * rows, width), dtype), shape((rows, width), dtype)),
        far="NRFF",
        far_out="FFFF" if dtype == F32 else "FFNN",
        flops=6 * rows * width * hidden,
        limit=24,
        scratch=[] if dtype == F32 else [pltpu.VMEM((rows, width), F32)] * 2,
    )(where, a, dh, up, down, *before, ahead=ahead)


def grad_into_heads(e, weight_ref):
    half = weight_ref.shape[1]
    if half == e.shape[1]:
        return dot_nt(e, weight_ref[...]).astype(BF16)
    return (dot_nt(e[:, :half], weight_ref[:half]) + dot_nt(e[:, half:], weight_ref[half:])).astype(BF16)


def add_rows(ref, number, value):
    ref[number : number + 1, :] += jnp.sum(value, 0, keepdims=True)


def after_feed_kernel(stage, s_ref, r_ref, recv0_ref, recv1_ref, e_ref, norms_ref, wo_ref, wp_ref, g_ref, eb_ref, own_ref, other_ref, d_ref):
    d_ref[...] = jnp.zeros_like(d_ref)
    stage.need(s_ref, r_ref, recv0_ref, recv1_ref, e_ref)
    stage.fetch()
    for at in row_blocks(s_ref.shape[0]):
        unit, rstd = normalise(s_ref[at])
        cotangent = r_ref[at] + (recv0_ref if at.start == 0 else recv1_ref)[...].astype(F32)
        add_rows(d_ref, 0, cotangent * unit)
        add_rows(d_ref, 1, cotangent)
        grad = e_ref[at].astype(F32) + norm_backward(unit, rstd, vector(norms_ref, 4), cotangent)
        g_ref[at] = grad
        eb_ref[at] = grad.astype(BF16)
    stage.send(g_ref, eb_ref)
    stage.need(wo_ref, wp_ref)
    own_ref[...] = grad_into_heads(eb_ref[...], wo_ref)
    other_ref[...] = grad_into_heads(eb_ref[...], wp_ref)


def after_cross_back_kernel(
    stage, s_ref, g_ref, dq_ref, dr_ref, wq_ref, wr_ref, norms_ref, wo_ref, wp_ref, out_ref, eb_ref, own_ref, other_ref, d_ref
):
    d_ref[...] = jnp.zeros_like(d_ref)
    stage.need(s_ref, g_ref, dr_ref, wq_ref, wr_ref)
    for at in row_blocks(s_ref.shape[0]):
        unit, rstd = normalise(s_ref[at])
        cotangent = dot_nt(dq_ref[at], wq_ref[...]) + dot_nt(dr_ref[at], wr_ref[...])
        add_rows(d_ref, 0, cotangent * unit)
        add_rows(d_ref, 1, cotangent)
        grad = g_ref[at] + norm_backward(unit, rstd, vector(norms_ref, 2), cotangent)
        out_ref[at] = grad
        eb_ref[at] = grad.astype(BF16)
    stage.send(out_ref, eb_ref)
    stage.need(wo_ref, wp_ref)
    own_ref[...] = grad_into_heads(eb_ref[...], wo_ref)
    other_ref[...] = grad_into_heads(eb_ref[...], wp_ref)


def key_value_back_kernel(with_queries, stage, where_ref, own_ref, other_ref, wkv_ref, wlw_ref, *refs):
    if with_queries:
        dq_ref, dr_ref, wq_ref, wr_ref, x_ref, send_ref, keep_ref, d_ref = refs
        d_ref[...] = jnp.zeros_like(d_ref)
    else:
        send_ref, keep_ref = refs
    stage.need(own_ref, other_ref, wkv_ref, wlw_ref)
    if with_queries:
        stage.need(x_ref)
    rows = send_ref.shape[0]
    side = where_ref[0]
    for half, target in ((1 - side, send_ref), (side, keep_ref)):
        if with_queries and target is keep_ref:
            stage.need(dq_ref, dr_ref, wq_ref, wr_ref)
        for at in row_blocks(rows):
            place = own_half(half, rows, at.start, BLOCK)
            total = dot_nt(own_ref[place, :], wkv_ref[...]) + dot_nt(other_ref[place, :], wlw_ref[...])
            if with_queries:
                if target is keep_ref:
                    total += dot_nt(dq_ref[at], wq_ref[...]) + dot_nt(dr_ref[at], wr_ref[...])
                unit, _ = normalise(x_ref[place, :].astype(F32))
                add_rows(d_ref, 0, total * unit)
                add_rows(d_ref, 1, total)
            target[at] = total.astype(target.dtype)


def key_value_back(side, own, other, wkv, wlw, queries=(), ahead=()):
    rows = own.shape[0] // 2
    width = wkv.shape[0]
    cols = wkv.shape[1] // 2
    outs = (shape((rows, width), BF16), shape((rows, width), F32))
    if queries:
        outs += (shape((2, width), F32),)
    return call(
        partial(key_value_back_kernel, len(queries) > 0),
        outs,
        far="FFVV",
        far_out="NF",
        flops=18 * rows * width * cols,
    )(side, own, other, wkv, wlw, *queries, ahead=ahead)


def input_grad_kernel(stage, where_ref, x_ref, g_ref, keep_ref, recv_ref, norms_ref, out_ref):
    stage.need(x_ref, g_ref, keep_ref, recv_ref)
    for at in row_blocks(g_ref.shape[0]):
        unit, rstd = normalise(x_ref[at].astype(F32))
        cotangent = keep_ref[at] + recv_ref[at].astype(F32)
        out_ref[at] = g_ref[at] + norm_backward(unit, rstd, vector(norms_ref, 0), cotangent)


def input_grad(side, x, grad, kept, received, norms):
    rows, width = grad.shape
    return call(
        input_grad_kernel,
        shape((rows, width), F32),
        far="VVFN",
        flops=rows * width * 20,
    )(side, x, grad, kept, received, norms)


def bit_reversed(number, bits):
    turned = 0
    for bit in range(bits):
        turned |= ((number >> bit) & 1) << (bits - 1 - bit)
    return turned


def store_parts(product, keep, send, core, parts):
    bits = parts.bit_length() - 1
    rows = product.shape[0] // parts
    product = product.astype(BF16)

    def write(target, wanted):
        for number in range(parts // 2):
            block = bit_reversed(number, bits - 1) * 2 + wanted
            target(number * rows, rows, product[block * rows : (block + 1) * rows])

    for value in (0, 1):
        @pl.when(core == value)
        def _():
            write(keep, value)
            write(send, 1 - value)


def put_columns(ref, columns):
    def put(first, count, value):
        ref[first : first + count, columns] = value

    return put


def attention_grads_kernel(parts, stage, where_ref, wide_ref, a_ref, e_ref, dq_ref, dkv_ref, o_ref, keep_ref, send_ref):
    core = where_ref[1]
    cols = dq_ref.shape[1]
    half = slice(None) if a_ref.shape == e_ref.shape else own_half(where_ref[0], dq_ref.shape[0])
    stage.need(wide_ref, a_ref, e_ref, o_ref)
    products = ((wide_ref, slice(None), dkv_ref, cols), (a_ref, half, dq_ref, 0), (e_ref, slice(None), o_ref, 3 * cols))
    for left, rows, right, first in products:
        product = dot_tn(left[rows, :], right[...])
        columns = slice(first, first + right.shape[1])
        store_parts(product, put_columns(keep_ref, columns), put_columns(send_ref, columns), core, parts)
    stage.send(keep_ref, send_ref)


def feed_grads_kernel(
    parts, chunk, stage, where_ref, a0, a1, a2, du0, du1, du2, h0, h1, h2, e_ref, keep_ref, send_ref, a_all, left, right, sems
):
    core = where_ref[1]
    rows, width = a0.shape
    hidden = du0.shape[1]
    places = [(0, rows)] + [(rows + at.start, BLOCK) for at in row_blocks(rows)]

    def fill(sources, number):
        copies = []
        for place, (source, (first, count)) in enumerate(zip(sources, places)):
            copies.append(
                pltpu.make_async_copy(source, left.at[number, pl.ds(first, count)], sems.at[3 * number + place])
            )
            copies[-1].start()
        return copies

    first_copies = fill((du0, du1, du2), 0)
    second_copies = fill((h0, h1, h2), 1)
    for place, half in enumerate((where_ref[0], 1 - where_ref[0])):
        second_copies.append(
            pltpu.make_async_copy(e_ref.at[own_half(half, rows), :], right.at[pl.ds(place * rows, rows)], sems.at[6 + place])
        )
        second_copies[-1].start()
    for source, (first, count) in zip((a0, a1, a2), places):
        a_all[first : first + count] = source[...]
    for base, copies, others in ((0, first_copies, a_all), (hidden, second_copies, right)):
        for copy in copies:
            copy.wait()
        for first in range(0, hidden, chunk):
            product = dot_tn(others[...], left[1 if base else 0, :, first : first + chunk])
            columns = slice(base + first, base + first + chunk)
            store_parts(product, put_columns(keep_ref, columns), put_columns(send_ref, columns), core, parts)
            stage.send_columns((keep_ref, send_ref), columns, columns.stop == 2 * hidden)


def attend_back_scratch(heads, keys):
    pairs = heads // 2
    return [
        pltpu.VMEM((heads, keys, 128), BF16),
        pltpu.VMEM((heads, keys, 128), BF16),
        pltpu.VMEM((heads, BLOCK, 128), BF16),
        pltpu.VMEM((pairs, 128, BLOCK), F32),
        pltpu.VMEM((pairs, 128, keys), F32),
        pltpu.VMEM((pairs, 128, keys), F32),
        pltpu.VMEM((pairs, 128, keys), BF16),
        pltpu.VMEM((pairs, 128, BLOCK), BF16),
        pltpu.VMEM((pairs, 128, BLOCK), BF16),
    ]


def after_feed(side, stream, kept, first, second, e3, norms, wo, wp, ahead=()):
    rows, width = stream.shape
    cols = wo.shape[0]
    return call(
        after_feed_kernel_of_side,
        (shape((rows, width), F32), shape((rows, width), BF16), shape((rows, cols), BF16), shape((rows, cols), BF16), shape((2, width), F32)),
        far="FFFFHNFO",
        flops=4 * rows * width * cols,
    )(side, stream, kept, first, second, e3, norms, wo, wp, ahead=ahead)


def after_feed_kernel_of_side(stage, side_ref, *refs):
    after_feed_kernel(stage, *refs)


def cross_back_kernel(
    parts, heads, stage, where_ref, starts_ref, doo, don, qao, kvo, oo, qan, kvn, on, dock, memory, a2, e2, stream, grad,
    wq, wr, norms, wo, wp,
    keep_d, send_d, keep_c, send_c, dkvo, dkvn, out, e1, own, other, d, dqo, dqn, *scratch
):
    attend_back_kernel(False, heads, heads // 2, stage, where_ref, starts_ref, qao, kvo, doo, oo, dock, dqo, dkvo, *scratch)
    stage.send(dkvo)
    attention_grads_kernel(parts, stage, where_ref, memory, a2, e2, dqo, dkvo, oo, keep_d, send_d)
    attend_back_kernel(False, heads, heads // 2, stage, where_ref, starts_ref, qan, kvn, don, on, dock, dqn, dkvn, *scratch)
    stage.send(dkvn)
    attention_grads_kernel(parts, stage, where_ref, memory, a2, e2, dqn, dkvn, on, keep_c, send_c)
    after_cross_back_kernel(stage, stream, grad, dqn, dqo, wq, wr, norms, wo, wp, out, e1, own, other, d)


def cross_back(where, parts, starts, doo, don, qao, kvo, oo, qan, kvn, on, dock, memory, a2, e2, stream, grad, wq, wr, norms, wo, wp, ahead=()):
    rows, width = stream.shape
    keys, cols = kvo.shape[0], wo.shape[0]
    heads = cols // HEAD_DIM
    part = shape((width // 2, 4 * cols), BF16)
    narrow = shape((rows, cols), BF16)
    return call(
        partial(cross_back_kernel, parts, heads),
        (
            part, part, part, part, shape((keys, 2 * cols), BF16), shape((keys, 2 * cols), BF16), shape((rows, width), F32),
            shape((rows, width), BF16), narrow, narrow, shape((2, width), F32),
        ),
        far="NNVVVFFFVFFNFNFQNFO",
        far_out="FFFFFFFFFNN",
        flops=120 * rows * keys * cols,
        scalars=2,
        limit=36,
        scratch=[pltpu.VMEM((rows, cols), BF16)] * 2 + attend_back_scratch(heads, keys),
    )(where, starts, doo, don, qao, kvo, oo, qan, kvn, on, dock, memory, a2, e2, stream, grad, wq, wr, norms, wo, wp, ahead=ahead)


def self_other_back_kernel(parts, heads, stage, where_ref, starts_ref, do, qa, kv, o, dock, a1, e1, dq, dkv, keep, send, *scratch):
    attend_back_kernel(True, heads, heads // 2, stage, where_ref, starts_ref, qa, kv, do, o, dock, dq, dkv, *scratch)
    stage.send(dq, dkv)
    attention_grads_kernel(parts, stage, where_ref, a1, a1, e1, dq, dkv, o, keep, send)


def self_other_back(where, parts, starts, do, qa, kv, o, dock, a1, e1, ahead=()):
    rows, cols = do.shape
    keys, width = a1.shape
    heads = cols // HEAD_DIM
    part = shape((width // 2, 4 * cols), BF16)
    return call(
        partial(self_other_back_kernel, parts, heads),
        (shape((rows, cols), BF16), shape((keys, 2 * cols), BF16), part, part),
        far="NVVVVFF",
        far_out="FFFF",
        flops=56 * rows * keys * cols,
        scalars=2,
        scratch=attend_back_scratch(heads, keys),
    )(where, starts, do, qa, kv, o, dock, a1, e1, ahead=ahead)


def self_own_back_kernel(
    parts, heads, stage, where_ref, starts_ref, do, qa, kv, o, dock, a1, e1, dqo, dkvo, wkv, wlw, wq, wr, x,
    keep_r, send_r, d, keep, send, dq, dkv, *scratch
):
    attend_back_kernel(True, heads, heads // 2, stage, where_ref, starts_ref, qa, kv, do, o, dock, dq, dkv, *scratch)
    attention_grads_kernel(parts, stage, where_ref, a1, a1, e1, dq, dkv, o, keep, send)
    key_value_back_kernel(True, stage, where_ref, dkv, dkvo, wkv, wlw, dq, dqo, wq, wr, x, send_r, keep_r, d)


def self_own_back(where, parts, starts, do, qa, kv, o, dock, a1, e1, dqo, dkvo, wkv, wlw, wq, wr, x, ahead=()):
    rows, cols = do.shape
    keys, width = a1.shape
    heads = cols // HEAD_DIM
    part = shape((width // 2, 4 * cols), BF16)
    return call(
        partial(self_own_back_kernel, parts, heads),
        (shape((rows, width), F32), shape((rows, width), BF16), shape((2, width), F32), part, part),
        far="FFFFFLLLLLKLQL",
        far_out="FNNFF",
        flops=74 * rows * keys * cols,
        scalars=2,
        limit=36,
        scratch=[pltpu.VMEM((rows, cols), BF16), pltpu.VMEM((keys, 2 * cols), BF16)] + attend_back_scratch(heads, keys),
    )(where, starts, do, qa, kv, o, dock, a1, e1, dqo, dkvo, wkv, wlw, wq, wr, x, ahead=ahead)


def feed_grads(where, parts, e, a, du, h, chunk=768):
    rows, width = a[0].shape
    hidden = du[0].shape[1]
    out = shape((width // 2, 2 * hidden), BF16)
    return call(
        partial(feed_grads_kernel, parts, chunk),
        (out, out),
        far="NNNXXXXXXX",
        far_out="FF",
        flops=8 * rows * width * hidden,
        limit=36,
        scratch=[
            pltpu.VMEM((2 * rows, width), BF16), pltpu.VMEM((2, 2 * rows, hidden), BF16), pltpu.VMEM((2 * rows, width), BF16),
            pltpu.SemaphoreType.DMA((8,)),
        ],
    )(where, *a, *du, *h, e)


def swap_tensor(value):
    return lax.ppermute(value, "tensor", [(0, 1), (1, 0)])


def swap_dp(value, bit):
    count = lax.axis_size("dp")
    return lax.ppermute(value, "dp", [(number, number ^ (1 << bit)) for number in range(count)])


def after(value, *others):
    return lax.optimization_barrier((value,) + others)[0] if others else value


def quarter_of(query, key, value, out, part):
    width, cols = query.shape
    rows = width // 4
    pieces = [lax.dynamic_slice_in_dim(weight, part * rows, rows, 0) for weight in (query, key, value)]
    pieces.append(lax.dynamic_slice(out, ((part % 2) * rows, (part // 2) * cols), (rows, cols)))
    return jnp.concatenate(pieces, axis=1)


class Sum:
    def __init__(self, *terms):
        self.terms = [term if isinstance(term, tuple) else (term, 0) for term in terms]
        last, first = self.terms[-1]
        self.rows = last.shape[0]

    def cut(self, first, rows):
        return Sum.of([(array, start + first) for array, start in self.terms], rows)

    @classmethod
    def of(cls, terms, rows):
        made = cls.__new__(cls)
        made.terms, made.rows = terms, rows
        return made

    def plus(self, array):
        return Sum.of(self.terms + [(array, 0)], self.rows)

    def formed(self, dtype=BF16):
        pieces = [
            array.astype(F32) if array.shape[0] == self.rows else lax.dynamic_slice_in_dim(array, start, self.rows, 0).astype(F32)
            for array, start in self.terms
        ]
        return sum(pieces[1:], pieces[0]).astype(dtype)

    def tied(self, *others):
        arrays = [array for array, _ in self.terms]
        made = lax.optimization_barrier((tuple(arrays), others))
        return (Sum.of([(array, start) for array, (_, start) in zip(made[0], self.terms)], self.rows),) + tuple(made[1])


def halve(value, bit, place):
    rows = value.rows // 2
    mine = (place >> bit) & 1
    return value.cut(mine * rows, rows), swap_dp(value.cut((1 - mine) * rows, rows).formed(), bit)


def add(left, right):
    return (left.astype(F32) + right.astype(F32)).astype(BF16)


def shards(
    target_tokens, memory_tokens, output_grad, target_segments, memory_segments,
    norm1_gain, norm1_shift, self_query, self_key, self_value, self_out,
    norm2_gain, norm2_shift, cross_query, cross_key, cross_value, cross_out,
    norm3_gain, norm3_shift, ffn_up, ffn_down,
):
    _, length, width = target_tokens.shape
    cols = self_query.shape[1]
    parts = lax.axis_size("dp")
    bits = parts.bit_length() - 1
    place = lax.axis_index("dp")
    side = lax.axis_index("tensor")
    core = place & 1
    x = target_tokens[0]
    memory = memory_tokens[0]
    e3 = output_grad[0]
    norms = jnp.stack([norm1_gain, norm1_shift, norm2_gain, norm2_shift, norm3_gain, norm3_shift])
    tie = lax.optimization_barrier
    side_one = side.astype(jnp.int32).reshape(1)
    where = jnp.stack([side, core]).astype(jnp.int32)

    part = place % 4
    self_first = swap_tensor(quarter_of(self_query, self_key, self_value, self_out, part))
    cross_quarter = quarter_of(cross_query, cross_key, cross_value, cross_out, part)
    self_wo, cross_wo = self_out, cross_out
    self_wkv = jnp.concatenate([self_key, self_value], axis=1)
    cross_wkv = jnp.concatenate([cross_key, cross_value], axis=1)

    numbers = jnp.arange(DOCS + 1)[:, None]
    target_starts = jnp.sum(target_segments < numbers, 1).astype(jnp.int32)
    memory_starts = jnp.sum(memory_segments < numbers, 1).astype(jnp.int32)
    self_starts = jnp.stack([target_starts, target_starts])
    cross_starts = jnp.stack([target_starts, memory_starts])
    lane = jnp.arange(128) % 64
    hot = target_segments[0][:, None] == lane[None, :]
    doc_rows = jnp.where(hot, LOW, 0.0).astype(BF16)
    doc_target = jnp.where((lane < DOCS)[None, :] & ~hot, 1.0, 0.0).astype(BF16)
    doc_memory = jnp.where(
        (lane < DOCS)[None, :] & (memory_segments[0][:, None] != lane[None, :]), 1.0, 0.0
    ).astype(BF16)

    dh, kv2_own = prepare(e3, ffn_down, memory, cross_wkv)
    self_first, cross_quarter, x_now, dh, kv2_own, doc_rows, doc_target, doc_memory, self_wkv, norms = tie(
        (self_first, cross_quarter, x, dh, kv2_own, doc_rows, doc_target, doc_memory, self_wkv, norms)
    )
    self_second = swap_dp(self_first, 1)
    self_third = swap_dp(self_first, 0)
    cross_first = swap_tensor(cross_quarter)
    o1_own, qa1_own, a1, kv_own, o1_own_far = self_own(
        side_one, self_starts, x_now, norms, self_query, self_wkv, doc_rows, doc_target
    )
    self_second, o1_own, cross_first = tie((self_second, o1_own, cross_first))
    self_fourth = swap_dp(self_second, 0)
    self_fourth, self_third = tie((self_fourth, self_third))
    self_pieces = (self_first, self_third, self_second, self_fourth)
    cross_first, self_pieces = tie((cross_first, self_pieces))
    side_part = jnp.stack([side, part]).astype(jnp.int32)
    cross_second = swap_dp(cross_first, 1)
    cross_third = swap_dp(cross_first, 0)
    o1_oth, qa1_oth, kv_oth, stream1, a2, q2_own, self_two, kv2_near, memory_docs_near = self_other(
        side_part, self_starts, a1, self_pieces, doc_rows, doc_target, x, o1_own, self_wo, norms, cross_query,
        ahead=((kv2_own, "F"), (doc_memory, "F")),
    )
    cross_second, q2_own = tie((cross_second, q2_own))
    cross_fourth = swap_dp(cross_second, 0)
    o2_own, qa2_own, o2_own_far = cross_own(side_one, cross_starts, kv2_near, q2_own, doc_rows, memory_docs_near)
    cross_fourth, cross_third, o2_own = tie((cross_fourth, cross_third, o2_own))
    cross_pieces = (cross_first, cross_third, cross_second, cross_fourth)
    o2_oth, qa2_oth, kv2_oth, stream2, a3, a3_first, a3_second, cross_two = cross_other(
        side_part, cross_starts, memory, cross_pieces, a2, doc_rows, doc_memory, stream1, o2_own, cross_wo, norms
    )

    first_block = (side * (length // 2 // BLOCK)).astype(jnp.int32).reshape(1)
    other_block = length // 2 // BLOCK - first_block
    a3_first, a3_second = swap_tensor(a3_first), swap_tensor(a3_second)
    h_own, du_own, out_own, r3_own = feed(first_block, a3, dh, ffn_up, ffn_down, F32)
    a3_first, r3_own = tie((a3_first, r3_own))
    h_first, du_first, out_first, r3_first = feed(other_block, a3_first, dh, ffn_up, ffn_down, BF16)
    a3_second, r3_first = tie((a3_second, r3_first))
    r3_first = swap_tensor(r3_first)
    h_second, du_second, out_oth, r3_second = feed(other_block + 1, a3_second, dh, ffn_up, ffn_down, BF16, out_first)
    r3_second = swap_tensor(r3_second)
    aligned = (width // parts) % 16 == 0
    static_parts = parts if aligned else 2
    keep_f, send_f = feed_grads(
        where, static_parts, e3, (a3, a3_first, a3_second), (du_own, du_first, du_second), (h_own, h_first, h_second)
    )
    r3_first, r3_second, keep_f, send_f = tie((r3_first, r3_second, keep_f, send_f))

    def reordered(keep, send):
        if aligned:
            return keep, send
        whole = jnp.where(core == 0, jnp.concatenate([keep, send]), jnp.concatenate([send, keep]))
        order = [bit_reversed(number, bits) for number in range(parts)]
        whole = jnp.take(whole.reshape(parts, width // parts, -1), jnp.array(order), axis=0)
        whole = whole.reshape(2, width // 2, -1)
        pick = lambda index: lax.dynamic_index_in_dim(whole, index, 0, False)
        return pick(core), pick(1 - core)

    def swap_core(keep, send):
        keep, send = reordered(keep, send)
        return keep, swap_dp(send, 0)

    keep_f, recv_f = swap_core(keep_f, send_f)
    grad2, e2, do2_own, do2_oth, d3, qa2_near, kv2_near, o2_near, memory_docs_near = after_feed(
        side_one, stream2, r3_own, r3_first, r3_second, e3, norms, cross_wo, cross_two,
        ahead=((qa2_oth, "F"), (kv2_oth, "F"), (o2_oth, "F"), (doc_memory, "F")),
    )
    do2_oth, keep_f, recv_f, out_oth = tie((do2_oth, keep_f, recv_f, out_oth))
    out_recv = swap_tensor(out_oth)
    sum_f, recv_f = halve(Sum(keep_f, recv_f), 1, place)
    (
        keep_d, send_d, keep_c, send_c, dkv2_oth, dkv2_own, grad1, e1, do1_own, do1_oth, d2, wkv_near, wkv2_near
    ) = cross_back(
        where, static_parts, cross_starts, do2_oth, do2_own, qa2_near, kv2_near, o2_near, qa2_own, kv2_own, o2_own_far,
        memory_docs_near, memory, a2, e2, stream1, grad2, cross_query, cross_two, norms, self_wo, self_two,
        ahead=((cross_wkv, "F"), (cross_two, "K")),
    )
    keep_d, send_d, keep_c, send_c, recv_f, out_recv = tie((keep_d, send_d, keep_c, send_c, recv_f, out_recv))
    keep_d, recv_d = swap_core(keep_d, send_d)
    keep_c, recv_c = swap_core(keep_c, send_c)
    sum_f = sum_f.plus(recv_f)
    if bits > 2:
        sum_f, recv_f = halve(sum_f, 2, place)
    send_m, keep_m, qa1_near, kv_near, o1_near, target_near = key_value_back(
        side_one, dkv2_own, dkv2_oth, wkv_near, wkv2_near,
        ahead=((qa1_oth, "F"), (kv_oth, "F"), (o1_oth, "F"), (doc_target, "F")),
    )

    do1_oth, keep_d, recv_d, keep_c, recv_c, send_m = tie((do1_oth, keep_d, recv_d, keep_c, recv_c, send_m))
    sum_d, recv_d = halve(Sum(keep_d, recv_d), 1, place)
    recv_m = swap_tensor(send_m)
    dq1_oth, dkv1_oth, keep_t, send_t = self_other_back(
        where, static_parts, self_starts, do1_oth, qa1_near, kv_near, o1_near, target_near, a1, e1
    )
    keep_t, send_t, recv_d, recv_m, recv_f = tie((keep_t, send_t, recv_d, recv_m, recv_f))
    keep_t, recv_t = swap_core(keep_t, send_t)
    do1_own, keep_t, recv_t = tie((do1_own, keep_t, recv_t))
    sum_t, recv_t = halve(Sum(keep_t, recv_t), 1, place)
    sum_c, recv_c = halve(Sum(keep_c, recv_c), 1, place)
    sent_d = swap_tensor(sum_d.plus(recv_d).formed())
    keep_r, send_r, d1, keep_s, send_s, half_near, grad1_near = self_own_back(
        where, static_parts, self_starts, do1_own, qa1_own, kv_own, o1_own_far, doc_target, a1, e1,
        dq1_oth, dkv1_oth, self_wkv, self_two, self_query, self_two, x, ahead=((x, "H"), (grad1, "F")),
    )
    keep_s, send_s, d1, recv_c, sent_d, recv_t, recv_f = tie((keep_s, send_s, d1, recv_c, sent_d, recv_t, recv_f))
    sum_c, recv_c = sum_c.tied(recv_c)
    sum_t, recv_t = sum_t.tied(recv_t)
    keep_s, recv_s = swap_core(keep_s, send_s)
    sent_t = swap_tensor(sum_t.plus(recv_t).formed())
    sum_c = sum_c.plus(recv_c).plus(sent_d)
    if bits > 2:
        sum_c, recv_c = halve(sum_c, 2, place)
    lines = jnp.concatenate([jnp.concatenate([d[0:1], d[1:2]], axis=1) for d in (d1, d2, d3)], axis=0)
    lines = jnp.pad(lines, ((0, NORM_ROWS - 3), (0, 0))).astype(BF16)
    lines = add(lines, swap_tensor(lines))
    lines = add(lines, swap_dp(lines, 0))
    keep_s, recv_s, send_r, lines, out_recv = tie((keep_s, recv_s, send_r, lines, out_recv))
    recv_r = swap_tensor(send_r)
    layer_output = (stream2 + out_own + out_recv.astype(F32)).astype(BF16)
    if bits > 2:
        sum_f = sum_f.plus(recv_f)
    if bits > 3:
        sum_f, recv_f = halve(sum_f, 3, place)
    sum_s = Sum(keep_s, recv_s)

    def halve_with_lines(value, lines, bit):
        rows = value.rows // 2
        mine = (place >> bit) & 1
        message = jnp.concatenate([value.cut((1 - mine) * rows, rows).formed(), lines], axis=0)
        received = swap_dp(message, bit)
        return value.cut(mine * rows, rows).plus(received), add(lines, received[rows:])

    sum_s, lines = halve_with_lines(sum_s, lines, 1)
    sum_s, lines, sent_t, recv_c, recv_m, layer_output = sum_s.tied(lines, sent_t, recv_c, recv_m, layer_output)
    sum_s = sum_s.plus(sent_t)
    if bits > 2:
        sum_c = sum_c.plus(recv_c)
    for bit in range(3, bits):
        sum_c, recv_c = halve(sum_c, bit, place)
        sum_c = sum_c.plus(recv_c)
    for bit in range(2, bits):
        sum_s, lines = halve_with_lines(sum_s, lines, bit)
        if bit == 2:
            recv_r, lines, recv_f = tie((recv_r, lines, recv_f))
    for bit in range(3, bits):
        sum_f = sum_f.plus(recv_f)
        if bit + 1 < bits:
            sum_f, recv_f = halve(sum_f, bit + 1, place)
    grad_x = input_grad(side_one, half_near, grad1_near, keep_r, recv_r, norms)
    grad_memory = keep_m + recv_m.astype(F32)
    small = lines.astype(F32)
    sum_s, sum_c, sum_f = (value.formed(F32) for value in (sum_s, sum_c, sum_f))

    def four(total):
        pieces = [total[:, number * cols : (number + 1) * cols] for number in range(4)]
        return tuple(pieces[:3]) + (pieces[3].T,)

    hidden = ffn_up.shape[1]
    return (
        (layer_output[None], grad_x[None], grad_memory[None])
        + four(sum_s)
        + four(sum_c)
        + (sum_f[:, :hidden], sum_f[:, hidden:].T)
        + tuple(small[number // 2, (number % 2) * width : (number % 2 + 1) * width] for number in range(6))
    )


def solution(mesh):
    tokens = P("dp", None, None)
    columns = P(None, "tensor")
    rows = P("tensor", None)
    block = (P(), P(), columns, columns, columns, rows)
    in_specs = (tokens,) * 3 + (P("dp", None),) * 2 + block + block + (P(), P(), columns, rows)
    out_rows = P("dp", "tensor")
    out_cols = P("tensor", "dp")
    four = (out_rows, out_rows, out_rows, out_cols)
    out_specs = (P("dp", "tensor", None),) * 3 + four + four + (out_rows, out_cols) + (P(),) * 6
    return jax.shard_map(shards, mesh=mesh, in_specs=in_specs, out_specs=out_specs, check_vma=False)
```

```python
from functools import partial

import jax
import jax.numpy as jnp
from jax import lax
from jax.experimental import pallas as pl
from jax.experimental.pallas import tpu as pltpu
from jax.sharding import PartitionSpec as P

HEAD_DIM = 64
DOCS = 4
BLOCK = 256
LOW = -1e30
NORM_ROWS = 16
SPARE = 12
COST = 0.02
F32 = jnp.float32
BF16 = jnp.bfloat16
MIB = 1024 * 1024


def dot(left, right):
    return jnp.dot(left, right, preferred_element_type=F32)


def dot_nt(left, right):
    return lax.dot_general(left, right, (((1,), (1,)), ((), ())), preferred_element_type=F32)


def dot_tn(left, right):
    return lax.dot_general(left, right, (((0,), (0,)), ((), ())), preferred_element_type=F32)


def normalise(values):
    centered = values - jnp.mean(values, -1, keepdims=True)
    rstd = lax.rsqrt(jnp.mean(centered * centered, -1, keepdims=True) + 1e-05)
    return centered * rstd, rstd


def norm_backward(unit, rstd, gain, cotangent):
    scaled = cotangent * gain
    return rstd * (
        scaled
        - jnp.mean(scaled, -1, keepdims=True)
        - unit * jnp.mean(scaled * unit, -1, keepdims=True)
    )


PARTS = {"Q": (0, 1), "K": (1, 2), "O": (3, 1)}


class Staged:
    def __init__(self, arriving, late, leaving, spare):
        self.arriving, self.late, self.leaving, self.spare, self.sent = arriving, late, leaving, list(spare), []

    def fetch(self):
        for copy in self.late:
            copy.start()
        self.late = []

    def need(self, *refs):
        for number, (ref, copy) in enumerate(self.arriving):
            if copy is not None and any(ref is wanted for wanted in refs):
                copy.wait()
                self.arriving[number] = (ref, None)

    def send(self, *refs):
        for number, (ref, target, sem) in enumerate(self.leaving):
            if target is not None and any(ref is wanted for wanted in refs):
                self.sent.append(pltpu.make_async_copy(ref, target, sem))
                self.sent[-1].start()
                self.leaving[number] = (ref, None, sem)

    def send_columns(self, refs, columns, last):
        for number, (ref, target, sem) in enumerate(self.leaving):
            if target is not None and any(ref is wanted for wanted in refs):
                if not last:
                    sem = self.spare.pop()
                self.sent.append(pltpu.make_async_copy(ref.at[:, columns], target.at[:, columns], sem))
                self.sent[-1].start()
                if last:
                    self.leaving[number] = (ref, None, sem)

    def finish(self):
        self.fetch()
        self.need(*(ref for ref, _ in self.arriving))
        self.send(*(ref for ref, _, _ in self.leaving))
        for copy in self.sent:
            copy.wait()


def call(kernel, out_shape, *, far="", far_out="", flops=0, limit=36, scratch=(), scalars=1):
    shapes = out_shape if isinstance(out_shape, tuple) else (out_shape,)

    def run(*operands, ahead=()):
        vmem = pl.BlockSpec(memory_space=pltpu.VMEM)
        hbm = pl.BlockSpec(memory_space=pltpu.HBM)
        small = pl.BlockSpec(memory_space=pltpu.SMEM)
        arrays = operands[scalars:]
        marks = far.ljust(len(arrays), "N")
        out_marks = far_out.ljust(len(shapes), "N")
        assert len(marks) == len(arrays) and len(out_marks) == len(shapes), (len(arrays), len(shapes))
        also = [number for number, mark in enumerate(out_marks) if mark == "W"]
        copied = [mark not in "NVX" for mark in marks]

        def held(mark, array):
            dims = array.shape
            if mark == "H":
                dims = (dims[0] // 2,) + dims[1:]
            elif mark == "R":
                dims = (shapes[0].shape[0],) + dims[1:]
            elif mark in PARTS:
                dims = (dims[0], dims[1] // 4 * PARTS[mark][1])
            return dims, array.dtype

        def part_of(mark, source, heads):
            if mark == "H":
                rows = source.shape[0] // 2
                return source.at[pl.ds(pl.multiple_of(heads[0][0] * rows, BLOCK), rows)]
            if mark == "R":
                return source.at[pl.ds(pl.multiple_of(heads[0][0] * BLOCK, BLOCK), shapes[0].shape[0])]
            if mark in PARTS:
                quarter = source.shape[1] // 4
                return source.at[:, pl.ds(PARTS[mark][0] * quarter, PARTS[mark][1] * quarter)]
            return source

        extra = [pltpu.VMEM(*held(mark, array)) for mark, array, here in zip(marks, arrays, copied) if here]
        extra += [pltpu.VMEM(item.shape, item.dtype) for mark, item in zip(out_marks, shapes) if mark == "F"]
        copies = len(extra) + len(also) + len(ahead)
        extra.append(pltpu.SemaphoreType.DMA((copies + SPARE,)))

        def wrapped(*refs):
            refs = list(refs)

            def take(count):
                taken = refs[:count]
                del refs[:count]
                return taken

            heads, ins, coming = take(scalars), take(len(arrays)), take(len(ahead))
            outs, seconds, arrived, own = take(len(shapes)), take(len(also)), take(len(ahead)), take(len(scratch))
            buffers, sems = refs[:-1], refs[-1]
            arriving, late, leaving, place = [], [], [], 0
            for number, mark in enumerate(marks):
                if copied[number]:
                    source = part_of(mark, ins[number], heads)
                    ins[number] = buffers.pop(0)
                    copy = pltpu.make_async_copy(source, ins[number], sems.at[place])
                    if mark == "L":
                        late.append(copy)
                    else:
                        copy.start()
                    arriving.append((ins[number], copy))
                    place += 1
            for (_, mark), source, target in zip(ahead, coming, arrived):
                copy = pltpu.make_async_copy(part_of(mark, source, heads), target, sems.at[place])
                copy.start()
                arriving.append((target, copy))
                place += 1
            for number, mark in enumerate(out_marks):
                if mark == "F":
                    target, outs[number] = outs[number], buffers.pop(0)
                    leaving.append((outs[number], target, sems.at[place]))
                    place += 1
            for number, second in zip(also, seconds):
                leaving.append((outs[number], second, sems.at[place]))
                place += 1
            stage = Staged(arriving, late, leaving, [sems.at[copies + number] for number in range(SPARE)])
            kernel(stage, *heads, *ins, *outs, *own)
            stage.finish()

        places = {"F": pltpu.HBM}
        kept = [places[mark](item.shape, item.dtype) if mark in places else item for item, mark in zip(shapes, out_marks)]
        kept += [pltpu.HBM(shapes[number].shape, shapes[number].dtype) for number in also]
        kept += [shape(*held(mark, array)) for array, mark in ahead]
        pinned = [
            array if mark in "NV" else pltpu.with_memory_space_constraint(array, pltpu.HBM)
            for array, mark in zip(arrays, marks)
        ]
        pinned += [pltpu.with_memory_space_constraint(array, pltpu.HBM) for array, _ in ahead]
        results = pl.pallas_call(
            wrapped,
            out_shape=tuple(kept),
            in_specs=[small] * scalars + [vmem if mark in "NV" else hbm for mark in marks] + [hbm] * len(ahead),
            out_specs=tuple(hbm if mark == "F" else vmem for mark in out_marks) + (hbm,) * len(also) + (vmem,) * len(ahead),
            scratch_shapes=list(scratch) + extra,
            compiler_params=pltpu.CompilerParams(vmem_limit_bytes=limit * MIB),
            cost_estimate=pl.CostEstimate(flops=int(COST * flops), bytes_accessed=4096, transcendentals=0),
        )(*operands[:scalars], *pinned)
        return results[0] if len(results) == 1 else results

    return run


def shape(dims, dtype):
    return jax.ShapeDtypeStruct(dims, dtype)


def row_blocks(rows):
    return [slice(first, first + BLOCK) for first in range(0, rows, BLOCK)]


def own_half(side, rows, first=0, count=None):
    count = rows if count is None else count
    return pl.ds(pl.multiple_of(side * rows + first, BLOCK), count)


def vector(ref, number):
    return ref[number : number + 1, :]


def norm_project_kernel(stage, where_ref, x_ref, norms_ref, wq_ref, wkv_ref, a_ref, q_ref, kv_ref):
    stage.need(x_ref)
    stage.fetch()
    for at in row_blocks(x_ref.shape[0]):
        unit, _ = normalise(x_ref[at].astype(F32))
        a_ref[at] = (unit * vector(norms_ref, 0) + vector(norms_ref, 1)).astype(BF16)
    stage.send(a_ref)
    rows = q_ref.shape[0]
    stage.need(wkv_ref)
    for at in row_blocks(x_ref.shape[0]):
        kv_ref[at] = dot(a_ref[at], wkv_ref[...]).astype(BF16)
    stage.send(kv_ref)
    stage.need(wq_ref)
    q_ref[...] = dot(a_ref[own_half(where_ref[0], rows), :], wq_ref[...]).astype(BF16)


def project_kernel(stage, where_ref, a_ref, wq_ref, wkv_ref, q_ref, kv_ref):
    stage.need(a_ref, wkv_ref)
    for at in row_blocks(a_ref.shape[0]):
        kv_ref[at] = dot(a_ref[at], wkv_ref[...]).astype(BF16)
    stage.send(kv_ref)
    stage.need(wq_ref)
    q_ref[...] = dot(a_ref[own_half(where_ref[0], q_ref.shape[0]), :], wq_ref[...]).astype(BF16)


def project_memory_kernel(stage, memory_ref, wkv_ref, kv_ref):
    stage.need(memory_ref, wkv_ref)
    for at in row_blocks(memory_ref.shape[0]):
        kv_ref[at] = dot(memory_ref[at], wkv_ref[...]).astype(BF16)
    stage.send(kv_ref)


def project_both_kernel(stage, memory_ref, wkv_ref, a_ref, wq_ref, q_ref, kv_ref):
    project_memory_kernel(stage, memory_ref, wkv_ref, kv_ref)
    stage.need(a_ref, wq_ref)
    q_ref[...] = dot(a_ref[...], wq_ref[...]).astype(BF16)


def first_doc(starts_ref, row):
    doc = 0
    for number in range(1, DOCS):
        doc = doc + (starts_ref[0, number] <= row).astype(jnp.int32)
    return doc


def key_range(starts_ref, block_number, causal):
    first = block_number * BLOCK
    low = starts_ref[1, first_doc(starts_ref, first)]
    if causal:
        low = low // BLOCK
        return low * BLOCK, block_number - low
    high = starts_ref[1, first_doc(starts_ref, first + BLOCK - 1) + 1]
    low = low // 128 * 128
    count = (high - low + BLOCK - 1) // BLOCK
    return jnp.minimum(low, starts_ref[1, DOCS] - count * BLOCK), count


def lanes(rows):
    return lax.broadcasted_iota(jnp.int32, (rows, 128), 1)


def causal_mask():
    keys = lax.broadcasted_iota(jnp.int32, (BLOCK, BLOCK), 0)
    rows = lax.broadcasted_iota(jnp.int32, (BLOCK, BLOCK), 1)
    return keys <= rows


def pair_of(ref, pair, rows=slice(None)):
    return ref[rows, pair * 128 : (pair + 1) * 128]


def half_of(head):
    return slice(64 * (head % 2), 64 * (head % 2) + 64)


def in_three(value, place, otherwise):
    high = value.astype(BF16)
    rest = value - high.astype(F32)
    middle = rest.astype(BF16)
    low = (rest - middle.astype(F32)).astype(BF16)
    return jnp.where(place == 4, high, jnp.where(place == 5, middle, jnp.where(place == 6, low, otherwise)))


def walk_keys(starts_ref, block_number, causal, one_block):
    first, count = key_range(starts_ref, block_number, causal)
    if causal:
        one_block(block_number * BLOCK, causal_mask())
    lax.fori_loop(0, count, lambda number, _: (one_block(first + number * BLOCK, None), 0)[1], 0)


def attend_kernel(
    causal, heads, group, stage, where_ref, starts_ref, q_ref, kv_ref, docs_ref, dock_ref, o_ref, qa_ref,
    ka_ref, vt_ref, qs_ref, acc_ref, max_ref,
):
    keys = kv_ref.shape[0]
    pairs = heads // 2
    stage.need(kv_ref, dock_ref)
    left = lanes(keys) < 64
    for pair in range(pairs):
        turned = pair_of(kv_ref, pairs + pair).T
        for head in (2 * pair, 2 * pair + 1):
            mine = left if head % 2 == 0 else ~left
            ka_ref[head] = jnp.where(mine, pair_of(kv_ref, pair), dock_ref[...])
            vt_ref[head, :64] = turned[half_of(head)]
            vt_ref[head, 64:] = jnp.ones((16, keys), BF16)
    left = lanes(BLOCK) < 64
    place = lanes(BLOCK) % 64
    stage.need(q_ref, docs_ref)

    def one_step(step, _):
        at_rows = pl.ds(pl.multiple_of(step * BLOCK, BLOCK), BLOCK)
        block_number = where_ref[0] * (q_ref.shape[0] // BLOCK) + step
        docs = docs_ref[pl.ds(pl.multiple_of(block_number * BLOCK, BLOCK), BLOCK), :]
        for head in range(heads):
            mine = left if head % 2 == 0 else ~left
            scaled = pair_of(q_ref, head // 2, at_rows) * jnp.array(HEAD_DIM**-0.5, BF16)
            qs_ref[head] = jnp.where(mine, scaled, docs)
        max_ref[...] = jnp.full_like(max_ref, LOW)
        acc_ref[...] = jnp.zeros_like(acc_ref)

        def one_block(first_key, mask):
            at = pl.ds(pl.multiple_of(first_key, 128), BLOCK)
            for first in range(0, heads, group):
                some = range(first, first + group)
                scores = [dot_nt(ka_ref[head, at, :], qs_ref[head]) for head in some]
                if mask is not None:
                    scores = [jnp.where(mask, score, LOW) for score in scores]
                old = [max_ref[head, 0:1] for head in some]
                new = [jnp.maximum(m, jnp.max(score, 0, keepdims=True)) for m, score in zip(old, scores)]
                weights = [jnp.exp(score - m).astype(BF16) for score, m in zip(scores, new)]
                mixed = [dot(vt_ref[head, :, at], weight) for head, weight in zip(some, weights)]
                shrink = [jnp.exp(m - n) for m, n in zip(old, new)]
                for number_in, head in enumerate(some):
                    acc_ref[head] = acc_ref[head] * shrink[number_in] + mixed[number_in]
                    max_ref[head, 0:1] = new[number_in]

        walk_keys(starts_ref, block_number, causal, one_block)
        for pair in range(pairs):
            both = []
            for head in (2 * pair, 2 * pair + 1):
                mine = left if head % 2 == 0 else ~left
                acc = acc_ref[head]
                total = acc[64:65]
                both.append(acc[:64] / total)
                lse = max_ref[head, 0:1] + jnp.log(total)
                column = jnp.broadcast_to(-lse, (128, BLOCK)).T
                qa_ref[head, at_rows, :] = jnp.where(mine, qs_ref[head], in_three(column, place, docs))
            o_ref[at_rows, pair * 128 : (pair + 1) * 128] = jnp.concatenate(both, 0).T.astype(BF16)
        return 0

    lax.fori_loop(0, q_ref.shape[0] // BLOCK, one_step, 0)
    stage.send(o_ref, qa_ref)


def attend_back_kernel(
    causal, heads, group, stage, where_ref, starts_ref, qa_ref, kv_ref, do_ref, o_ref, dock_ref, dq_ref, dkv_ref,
    ka_ref, va_ref, da_ref, dqa_ref, dka_ref, dva_ref, kt_ref, qt_ref, dt_ref,
):
    keys = kv_ref.shape[0]
    pairs = heads // 2
    stage.need(kv_ref, dock_ref)
    left = lanes(keys) < 64
    place = lanes(keys) % 64
    ones = jnp.where((place >= 4) & (place < 7), 1.0, 0.0).astype(BF16)
    for head in range(heads):
        mine = left if head % 2 == 0 else ~left
        ka_ref[head] = jnp.where(mine, pair_of(kv_ref, head // 2), dock_ref[...] + ones)
        va_ref[head] = jnp.where(mine, pair_of(kv_ref, pairs + head // 2), ones)
    for pair in range(pairs):
        kt_ref[pair] = pair_of(kv_ref, pair).T
    dka_ref[...] = jnp.zeros_like(dka_ref)
    dva_ref[...] = jnp.zeros_like(dva_ref)
    stage.need(qa_ref, o_ref, do_ref)
    stage.fetch()
    left = lanes(BLOCK) < 64
    place = lanes(BLOCK) % 64

    def one_step(step, _):
        at_rows = pl.ds(pl.multiple_of(step * BLOCK, BLOCK), BLOCK)
        block_number = where_ref[0] * (do_ref.shape[0] // BLOCK) + step
        for pair in range(pairs):
            grad = pair_of(do_ref, pair, at_rows)
            dt_ref[pair] = grad.T
            product = grad.astype(F32) * pair_of(o_ref, pair, at_rows).astype(F32)
            for head in (2 * pair, 2 * pair + 1):
                mine = left if head % 2 == 0 else ~left
                delta = -jnp.sum(jnp.where(mine, product, 0.0), -1, keepdims=True)
                delta = jnp.broadcast_to(delta, (BLOCK, 128))
                da_ref[head] = jnp.where(mine, grad, in_three(delta, place, jnp.zeros((), BF16)))
            qt_ref[pair] = jnp.where(left, qa_ref[2 * pair, at_rows, :], qa_ref[2 * pair + 1, at_rows, :]).T
        dqa_ref[...] = jnp.zeros_like(dqa_ref)

        def one_block(first_key, mask):
            at = pl.ds(pl.multiple_of(first_key, 128), BLOCK)
            for first in range(0, heads, group):
                some = range(first, first + group)
                scores = [dot_nt(ka_ref[head, at, :], qa_ref[head, at_rows, :]) for head in some]
                grads = [dot_nt(va_ref[head, at, :], da_ref[head]) for head in some]
                if mask is not None:
                    scores = [jnp.where(mask, score, LOW) for score in scores]
                weights = [jnp.exp(score) for score in scores]
                grads = [(weight * grad).astype(BF16) for weight, grad in zip(weights, grads)]
                weights = [weight.astype(BF16) for weight in weights]
                values = [dot_nt(dt_ref[head // 2, half_of(head)], weight) for head, weight in zip(some, weights)]
                kept = [dot_nt(qt_ref[head // 2, half_of(head)], grad) for head, grad in zip(some, grads)]
                asked = [dot(kt_ref[head // 2, half_of(head), at], grad) for head, grad in zip(some, grads)]
                for number_in, head in enumerate(some):
                    dva_ref[head // 2, half_of(head), at] += values[number_in]
                    dka_ref[head // 2, half_of(head), at] += kept[number_in]
                    dqa_ref[head // 2, half_of(head)] += asked[number_in]

        walk_keys(starts_ref, block_number, causal, one_block)
        for pair in range(pairs):
            dq_ref[at_rows, pair * 128 : (pair + 1) * 128] = (dqa_ref[pair].T * HEAD_DIM**-0.5).astype(BF16)
        return 0

    lax.fori_loop(0, do_ref.shape[0] // BLOCK, one_step, 0)
    for pair in range(pairs):
        dkv_ref[:, pair * 128 : (pair + 1) * 128] = dka_ref[pair].astype(BF16).T
        dkv_ref[:, (pairs + pair) * 128 : (pairs + pair + 1) * 128] = dva_ref[pair].astype(BF16).T


def out_project(own, other, own_ref, other_ref):
    half = other_ref.shape[1]
    folded = [dot(other, other_ref[:half]), dot(other, other_ref[half:])]
    return dot(own, own_ref[...]) + jnp.concatenate(folded, axis=1)


def after_self_kernel(stage, x_ref, own_ref, other_ref, wo_ref, wp_ref, norms_ref, wq_ref, s_ref, a_ref, q_ref):
    stage.need(x_ref, own_ref, wo_ref, wp_ref)
    rows = s_ref.shape[0]
    for at in row_blocks(rows):
        stream = x_ref[at].astype(F32) + out_project(own_ref[at], other_ref[at], wo_ref, wp_ref)
        s_ref[at] = stream
        unit, _ = normalise(stream)
        a_ref[at] = (unit * vector(norms_ref, 2) + vector(norms_ref, 3)).astype(BF16)
    stage.send(s_ref, a_ref)
    stage.need(wq_ref)
    q_ref[...] = dot(a_ref[...], wq_ref[...]).astype(BF16)


def after_cross_kernel(stage, s_ref, own_ref, other_ref, wo_ref, wp_ref, norms_ref, t_ref, a_ref, *parts):
    stage.need(s_ref, own_ref, wo_ref, wp_ref)
    for at in row_blocks(s_ref.shape[0]):
        stream = s_ref[at] + out_project(own_ref[at], other_ref[at], wo_ref, wp_ref)
        t_ref[at] = stream
        unit, _ = normalise(stream)
        a_ref[at] = (unit * vector(norms_ref, 4) + vector(norms_ref, 5)).astype(BF16)
        parts[at.start // BLOCK][...] = a_ref[at]


def prepare_kernel(stage, e_ref, down_ref, memory_ref, wkv_ref, dh_ref, kv_ref):
    stage.need(e_ref, down_ref)
    for at in row_blocks(e_ref.shape[0]):
        dh_ref[at] = dot_nt(e_ref[at], down_ref[...]).astype(BF16)
    stage.send(dh_ref)
    project_memory_kernel(stage, memory_ref, wkv_ref, kv_ref)


def prepare(e, down, memory, wkv, ahead=()):
    rows, width = e.shape
    hidden = down.shape[0]
    return call(
        prepare_kernel,
        (shape((rows, hidden), BF16), shape((memory.shape[0], wkv.shape[1]), BF16)),
        far="FFFF",
        far_out="FF",
        flops=2 * rows * width * hidden,
        scalars=0,
    )(e, down, memory, wkv, ahead=ahead)


def attend_scratch(heads, keys):
    return [
        pltpu.VMEM((heads, keys, 128), BF16),
        pltpu.VMEM((heads, 80, keys), BF16),
        pltpu.VMEM((heads, BLOCK, 128), BF16),
        pltpu.VMEM((heads, 80, BLOCK), F32),
        pltpu.VMEM((heads, 8, BLOCK), F32),
    ]


def self_own_kernel(heads, stage, side_ref, starts_ref, x, norms, wq, wkv, docs, dock, o, qa, a, kv, q, *scratch):
    norm_project_kernel(stage, side_ref, x, norms, wq, wkv, a, q, kv)
    attend_kernel(True, heads, heads, stage, side_ref, starts_ref, q, kv, docs, dock, o, qa, *scratch)


def self_own(side, starts, x, norms, wq, wkv, docs, dock, ahead=()):
    keys, width = x.shape
    rows, cols = keys // 2, wq.shape[1]
    heads = cols // HEAD_DIM
    return call(
        partial(self_own_kernel, heads),
        (shape((rows, cols), BF16), shape((heads, rows, 128), BF16), shape((keys, width), BF16), shape((keys, 2 * cols), BF16)),
        far="FNFFFF",
        far_out="WFFF",
        flops=5 * keys * width * cols + 16 * rows * keys * cols,
        scalars=2,
        scratch=[pltpu.VMEM((rows, cols), BF16)] + attend_scratch(heads, keys),
    )(side, starts, x, norms, wq, wkv, docs, dock, ahead=ahead)


def gather(where_ref, pieces, whole, sems):
    rows = pieces[0].shape[0]
    targets = [whole.at[pl.ds(number * rows, rows)] for number in range(4)]
    for number in range(4):
        for place in range(4):
            @pl.when((where_ref[1] ^ number) == place)
            def _():
                pltpu.make_async_copy(pieces[place], targets[number], sems.at[number]).start()

    return [pltpu.make_async_copy(pieces[0], targets[number], sems.at[number]) for number in range(4)]


def split_weights(whole):
    cols = whole.shape[1] // 4
    return whole.at[:, pl.ds(0, cols)], whole.at[:, pl.ds(cols, 2 * cols)], whole.at[:, pl.ds(3 * cols, cols)]


def self_other_kernel(
    heads, stage, side_ref, starts_ref, a, p0, p1, p2, p3, docs, dock, x, own, wo, norms, wc,
    o, qa, kv, stream, a2, q2, whole, q, sems, *scratch
):
    waits = gather(side_ref, (p0, p1, p2, p3), whole, sems)
    stage.need(a)
    for copy in waits:
        copy.wait()
    stage.fetch()
    stage.send(whole)
    wq, wkv, wp = split_weights(whole)
    project_kernel(stage, side_ref, a, wq, wkv, q, kv)
    attend_kernel(True, heads, heads, stage, side_ref, starts_ref, q, kv, docs, dock, o, qa, *scratch)
    after_self_kernel(stage, x, own, o, wo, wp, norms, wc, stream, a2, q2)


def self_other(where, starts, a, pieces, docs, dock, x, own, wo, norms, wc, ahead=()):
    keys, width = a.shape
    rows, cols = own.shape
    heads = cols // HEAD_DIM
    return call(
        partial(self_other_kernel, heads),
        (
            shape((rows, cols), BF16), shape((heads, rows, 128), BF16), shape((keys, 2 * cols), BF16),
            shape((rows, width), F32), shape((rows, width), BF16), shape((rows, cols), BF16), shape((width, 4 * cols), BF16),
        ),
        far="FXXXXLLHNLNL",
        far_out="FFFFFNF",
        flops=5 * keys * width * cols + 16 * rows * keys * cols,
        scalars=2,
        scratch=[pltpu.VMEM((rows, cols), BF16), pltpu.SemaphoreType.DMA((4,))] + attend_scratch(heads, keys),
    )(where, starts, a, *pieces, docs, dock, x, own, wo, norms, wc, ahead=ahead)


def cross_own_kernel(heads, stage, side_ref, starts_ref, kv, q, docs, dock, o, qa, *scratch):
    attend_kernel(False, heads, heads, stage, side_ref, starts_ref, q, kv, docs, dock, o, qa, *scratch)


def cross_own(side, starts, kv, q, docs, dock, ahead=()):
    keys = kv.shape[0]
    rows, cols = q.shape
    heads = cols // HEAD_DIM
    return call(
        partial(cross_own_kernel, heads),
        (shape((rows, cols), BF16), shape((heads, rows, 128), BF16)),
        far="VNFV",
        far_out="WF",
        flops=16 * rows * keys * cols,
        scalars=2,
        scratch=attend_scratch(heads, keys),
    )(side, starts, kv, q, docs, dock, ahead=ahead)


def cross_other_kernel(
    heads, stage, side_ref, starts_ref, memory, p0, p1, p2, p3, a, docs, dock, stream, own, wo, norms,
    o, qa, kv, after, a3, first, second, whole, q, sems, *scratch
):
    waits = gather(side_ref, (p0, p1, p2, p3), whole, sems)
    stage.need(memory)
    for copy in waits:
        copy.wait()
    stage.fetch()
    stage.send(whole)
    wq, wkv, wp = split_weights(whole)
    project_both_kernel(stage, memory, wkv, a, wq, q, kv)
    attend_kernel(False, heads, heads, stage, side_ref, starts_ref, q, kv, docs, dock, o, qa, *scratch)
    after_cross_kernel(stage, stream, own, o, wo, wp, norms, after, a3, first, second)


def cross_other(where, starts, memory, pieces, a, docs, dock, stream, own, wo, norms, ahead=()):
    keys, width = memory.shape
    rows, cols = own.shape
    heads = cols // HEAD_DIM
    half = shape((BLOCK, width), BF16)
    return call(
        partial(cross_other_kernel, heads),
        (
            shape((rows, cols), BF16), shape((heads, rows, 128), BF16), shape((keys, 2 * cols), BF16),
            shape((rows, width), F32), shape((rows, width), BF16), half, half, shape((width, 4 * cols), BF16),
        ),
        far="FXXXXLLLLNLN",
        far_out="FFFFNNNF",
        flops=5 * keys * width * cols + 16 * rows * keys * cols,
        scalars=2,
        scratch=[pltpu.VMEM((rows, cols), BF16), pltpu.SemaphoreType.DMA((4,))] + attend_scratch(heads, keys),
    )(where, starts, memory, *pieces, a, docs, dock, stream, own, wo, norms, ahead=ahead)


def feed_kernel(chunk, joined, stage, where_ref, a_ref, dh_ref, up_ref, down_ref, *refs):
    if joined:
        before_ref, refs = refs[0], refs[1:]
    h_ref, du_ref, out_ref, r_ref, *sums = refs
    rows = a_ref.shape[0]
    if joined:
        out_ref[:rows] = before_ref[...]
        out_ref = out_ref.at[pl.ds(rows, rows)]
    out_acc, r_acc = sums if sums else (out_ref, r_ref)
    stage.need(a_ref, up_ref)
    stage.fetch()
    chunks = [slice(first, first + chunk) for first in range(0, up_ref.shape[1], chunk)]
    for some in chunks:
        for at in row_blocks(rows):
            u = dot(a_ref[at], up_ref[:, some])
            if some.start == 0 and at.start == 0:
                stage.need(dh_ref, down_ref)
            square = u * u
            curve = jnp.tanh(u * (0.7978845608028654 + 0.035677408136300125 * square))
            half = 0.5 + 0.5 * curve
            slope = half + (0.5 * u) * (1.0 - curve * curve) * (0.7978845608028654 + 0.10703222440890037 * square)
            h_ref[at, some] = (u * half).astype(BF16)
            du_ref[at, some] = (dh_ref[at, some].astype(F32) * slope).astype(BF16)
        stage.send_columns((h_ref, du_ref), some, some is chunks[-1])
        out_part = dot(h_ref[:, some], down_ref[some])
        if some.start == 0:
            out_acc[...] = out_part
        elif some is chunks[-1]:
            out_ref[...] = (out_acc[...] + out_part).astype(out_ref.dtype)
            stage.send(out_ref)
        else:
            out_acc[...] += out_part
        r_part = dot_nt(du_ref[:, some], up_ref[:, some])
        if some.start == 0:
            r_acc[...] = r_part
        elif some is chunks[-1]:
            r_ref[...] = (r_acc[...] + r_part).astype(r_ref.dtype)
        else:
            r_acc[...] += r_part


def feed(where, a, dh, up, down, dtype, *before, chunk=768, ahead=()):
    rows, width = a.shape
    hidden = up.shape[1]
    return call(
        partial(feed_kernel, chunk, len(before) > 0),
        (shape((rows, hidden), BF16),) * 2 + (shape(((1 + len(before)) * rows, width), dtype), shape((rows, width), dtype)),
        far="NRFF",
        far_out="FFFF" if dtype == F32 else "FFNN",
        flops=6 * rows * width * hidden,
        limit=24,
        scratch=[] if dtype == F32 else [pltpu.VMEM((rows, width), F32)] * 2,
    )(where, a, dh, up, down, *before, ahead=ahead)


def grad_into_heads(e, weight_ref):
    half = weight_ref.shape[1]
    if half == e.shape[1]:
        return dot_nt(e, weight_ref[...]).astype(BF16)
    return (dot_nt(e[:, :half], weight_ref[:half]) + dot_nt(e[:, half:], weight_ref[half:])).astype(BF16)


def add_rows(ref, number, value):
    ref[number : number + 1, :] += jnp.sum(value, 0, keepdims=True)


def after_feed_kernel(stage, s_ref, r_ref, recv0_ref, recv1_ref, e_ref, norms_ref, wo_ref, wp_ref, g_ref, eb_ref, own_ref, other_ref, d_ref):
    d_ref[...] = jnp.zeros_like(d_ref)
    stage.need(s_ref, r_ref, recv0_ref, recv1_ref, e_ref)
    stage.fetch()
    for at in row_blocks(s_ref.shape[0]):
        unit, rstd = normalise(s_ref[at])
        cotangent = r_ref[at] + (recv0_ref if at.start == 0 else recv1_ref)[...].astype(F32)
        add_rows(d_ref, 0, cotangent * unit)
        add_rows(d_ref, 1, cotangent)
        grad = e_ref[at].astype(F32) + norm_backward(unit, rstd, vector(norms_ref, 4), cotangent)
        g_ref[at] = grad
        eb_ref[at] = grad.astype(BF16)
    stage.send(g_ref, eb_ref)
    stage.need(wo_ref, wp_ref)
    own_ref[...] = grad_into_heads(eb_ref[...], wo_ref)
    other_ref[...] = grad_into_heads(eb_ref[...], wp_ref)


def after_cross_back_kernel(
    stage, s_ref, g_ref, dq_ref, dr_ref, wq_ref, wr_ref, norms_ref, wo_ref, wp_ref, out_ref, eb_ref, own_ref, other_ref, d_ref
):
    d_ref[...] = jnp.zeros_like(d_ref)
    stage.need(s_ref, g_ref, dr_ref, wq_ref, wr_ref)
    for at in row_blocks(s_ref.shape[0]):
        unit, rstd = normalise(s_ref[at])
        cotangent = dot_nt(dq_ref[at], wq_ref[...]) + dot_nt(dr_ref[at], wr_ref[...])
        add_rows(d_ref, 0, cotangent * unit)
        add_rows(d_ref, 1, cotangent)
        grad = g_ref[at] + norm_backward(unit, rstd, vector(norms_ref, 2), cotangent)
        out_ref[at] = grad
        eb_ref[at] = grad.astype(BF16)
    stage.send(out_ref, eb_ref)
    stage.need(wo_ref, wp_ref)
    own_ref[...] = grad_into_heads(eb_ref[...], wo_ref)
    other_ref[...] = grad_into_heads(eb_ref[...], wp_ref)


def key_value_back_kernel(with_queries, stage, where_ref, own_ref, other_ref, wkv_ref, wlw_ref, *refs):
    if with_queries:
        dq_ref, dr_ref, wq_ref, wr_ref, x_ref, send_ref, keep_ref, d_ref = refs
        d_ref[...] = jnp.zeros_like(d_ref)
    else:
        send_ref, keep_ref = refs
    stage.need(own_ref, other_ref, wkv_ref, wlw_ref)
    if with_queries:
        stage.need(x_ref)
    rows = send_ref.shape[0]
    side = where_ref[0]
    for half, target in ((1 - side, send_ref), (side, keep_ref)):
        if with_queries and target is keep_ref:
            stage.need(dq_ref, dr_ref, wq_ref, wr_ref)
        for at in row_blocks(rows):
            place = own_half(half, rows, at.start, BLOCK)
            total = dot_nt(own_ref[place, :], wkv_ref[...]) + dot_nt(other_ref[place, :], wlw_ref[...])
            if with_queries:
                if target is keep_ref:
                    total += dot_nt(dq_ref[at], wq_ref[...]) + dot_nt(dr_ref[at], wr_ref[...])
                unit, _ = normalise(x_ref[place, :].astype(F32))
                add_rows(d_ref, 0, total * unit)
                add_rows(d_ref, 1, total)
            target[at] = total.astype(target.dtype)


def key_value_back(side, own, other, wkv, wlw, queries=(), ahead=()):
    rows = own.shape[0] // 2
    width = wkv.shape[0]
    cols = wkv.shape[1] // 2
    outs = (shape((rows, width), BF16), shape((rows, width), F32))
    if queries:
        outs += (shape((2, width), F32),)
    return call(
        partial(key_value_back_kernel, len(queries) > 0),
        outs,
        far="FFVV",
        far_out="NF",
        flops=18 * rows * width * cols,
    )(side, own, other, wkv, wlw, *queries, ahead=ahead)


def input_grad_kernel(stage, where_ref, x_ref, g_ref, keep_ref, recv_ref, norms_ref, out_ref):
    stage.need(x_ref, g_ref, keep_ref, recv_ref)
    for at in row_blocks(g_ref.shape[0]):
        unit, rstd = normalise(x_ref[at].astype(F32))
        cotangent = keep_ref[at] + recv_ref[at].astype(F32)
        out_ref[at] = g_ref[at] + norm_backward(unit, rstd, vector(norms_ref, 0), cotangent)


def input_grad(side, x, grad, kept, received, norms):
    rows, width = grad.shape
    return call(
        input_grad_kernel,
        shape((rows, width), F32),
        far="VVFN",
        flops=rows * width * 20,
    )(side, x, grad, kept, received, norms)


def bit_reversed(number, bits):
    turned = 0
    for bit in range(bits):
        turned |= ((number >> bit) & 1) << (bits - 1 - bit)
    return turned


def store_parts(product, keep, send, core, parts):
    bits = parts.bit_length() - 1
    rows = product.shape[0] // parts
    product = product.astype(BF16)

    def write(target, wanted):
        for number in range(parts // 2):
            block = bit_reversed(number, bits - 1) * 2 + wanted
            target(number * rows, rows, product[block * rows : (block + 1) * rows])

    for value in (0, 1):
        @pl.when(core == value)
        def _():
            write(keep, value)
            write(send, 1 - value)


def put_columns(ref, columns):
    def put(first, count, value):
        ref[first : first + count, columns] = value

    return put


def attention_grads_kernel(parts, stage, where_ref, wide_ref, a_ref, e_ref, dq_ref, dkv_ref, o_ref, keep_ref, send_ref):
    core = where_ref[1]
    cols = dq_ref.shape[1]
    half = slice(None) if a_ref.shape == e_ref.shape else own_half(where_ref[0], dq_ref.shape[0])
    stage.need(wide_ref, a_ref, e_ref, o_ref)
    products = ((wide_ref, slice(None), dkv_ref, cols), (a_ref, half, dq_ref, 0), (e_ref, slice(None), o_ref, 3 * cols))
    for left, rows, right, first in products:
        product = dot_tn(left[rows, :], right[...])
        columns = slice(first, first + right.shape[1])
        store_parts(product, put_columns(keep_ref, columns), put_columns(send_ref, columns), core, parts)
    stage.send(keep_ref, send_ref)


def feed_grads_kernel(
    parts, chunk, stage, where_ref, a0, a1, a2, du0, du1, du2, h0, h1, h2, e_ref, keep_ref, send_ref, a_all, left, right, sems
):
    core = where_ref[1]
    rows, width = a0.shape
    hidden = du0.shape[1]
    places = [(0, rows)] + [(rows + at.start, BLOCK) for at in row_blocks(rows)]

    def fill(sources, number):
        copies = []
        for place, (source, (first, count)) in enumerate(zip(sources, places)):
            copies.append(
                pltpu.make_async_copy(source, left.at[number, pl.ds(first, count)], sems.at[3 * number + place])
            )
            copies[-1].start()
        return copies

    first_copies = fill((du0, du1, du2), 0)
    second_copies = fill((h0, h1, h2), 1)
    for place, half in enumerate((where_ref[0], 1 - where_ref[0])):
        second_copies.append(
            pltpu.make_async_copy(e_ref.at[own_half(half, rows), :], right.at[pl.ds(place * rows, rows)], sems.at[6 + place])
        )
        second_copies[-1].start()
    for source, (first, count) in zip((a0, a1, a2), places):
        a_all[first : first + count] = source[...]
    for base, copies, others in ((0, first_copies, a_all), (hidden, second_copies, right)):
        for copy in copies:
            copy.wait()
        for first in range(0, hidden, chunk):
            product = dot_tn(others[...], left[1 if base else 0, :, first : first + chunk])
            columns = slice(base + first, base + first + chunk)
            store_parts(product, put_columns(keep_ref, columns), put_columns(send_ref, columns), core, parts)
            stage.send_columns((keep_ref, send_ref), columns, columns.stop == 2 * hidden)


def attend_back_scratch(heads, keys):
    pairs = heads // 2
    return [
        pltpu.VMEM((heads, keys, 128), BF16),
        pltpu.VMEM((heads, keys, 128), BF16),
        pltpu.VMEM((heads, BLOCK, 128), BF16),
        pltpu.VMEM((pairs, 128, BLOCK), F32),
        pltpu.VMEM((pairs, 128, keys), F32),
        pltpu.VMEM((pairs, 128, keys), F32),
        pltpu.VMEM((pairs, 128, keys), BF16),
        pltpu.VMEM((pairs, 128, BLOCK), BF16),
        pltpu.VMEM((pairs, 128, BLOCK), BF16),
    ]


def after_feed(side, stream, kept, first, second, e3, norms, wo, wp, ahead=()):
    rows, width = stream.shape
    cols = wo.shape[0]
    return call(
        after_feed_kernel_of_side,
        (shape((rows, width), F32), shape((rows, width), BF16), shape((rows, cols), BF16), shape((rows, cols), BF16), shape((2, width), F32)),
        far="FFFFHNFO",
        flops=4 * rows * width * cols,
    )(side, stream, kept, first, second, e3, norms, wo, wp, ahead=ahead)


def after_feed_kernel_of_side(stage, side_ref, *refs):
    after_feed_kernel(stage, *refs)


def cross_back_kernel(
    parts, heads, stage, where_ref, starts_ref, doo, don, qao, kvo, oo, qan, kvn, on, dock, memory, a2, e2, stream, grad,
    wq, wr, norms, wo, wp,
    keep_d, send_d, keep_c, send_c, dkvo, dkvn, out, e1, own, other, d, dqo, dqn, *scratch
):
    attend_back_kernel(False, heads, heads // 2, stage, where_ref, starts_ref, qao, kvo, doo, oo, dock, dqo, dkvo, *scratch)
    stage.send(dkvo)
    attention_grads_kernel(parts, stage, where_ref, memory, a2, e2, dqo, dkvo, oo, keep_d, send_d)
    attend_back_kernel(False, heads, heads // 2, stage, where_ref, starts_ref, qan, kvn, don, on, dock, dqn, dkvn, *scratch)
    stage.send(dkvn)
    attention_grads_kernel(parts, stage, where_ref, memory, a2, e2, dqn, dkvn, on, keep_c, send_c)
    after_cross_back_kernel(stage, stream, grad, dqn, dqo, wq, wr, norms, wo, wp, out, e1, own, other, d)


def cross_back(where, parts, starts, doo, don, qao, kvo, oo, qan, kvn, on, dock, memory, a2, e2, stream, grad, wq, wr, norms, wo, wp, ahead=()):
    rows, width = stream.shape
    keys, cols = kvo.shape[0], wo.shape[0]
    heads = cols // HEAD_DIM
    part = shape((width // 2, 4 * cols), BF16)
    narrow = shape((rows, cols), BF16)
    return call(
        partial(cross_back_kernel, parts, heads),
        (
            part, part, part, part, shape((keys, 2 * cols), BF16), shape((keys, 2 * cols), BF16), shape((rows, width), F32),
            shape((rows, width), BF16), narrow, narrow, shape((2, width), F32),
        ),
        far="NNVVVFFFVFFNFNFQNFO",
        far_out="FFFFFFFFFNN",
        flops=120 * rows * keys * cols,
        scalars=2,
        limit=36,
        scratch=[pltpu.VMEM((rows, cols), BF16)] * 2 + attend_back_scratch(heads, keys),
    )(where, starts, doo, don, qao, kvo, oo, qan, kvn, on, dock, memory, a2, e2, stream, grad, wq, wr, norms, wo, wp, ahead=ahead)


def self_other_back_kernel(parts, heads, stage, where_ref, starts_ref, do, qa, kv, o, dock, a1, e1, dq, dkv, keep, send, *scratch):
    attend_back_kernel(True, heads, heads // 2, stage, where_ref, starts_ref, qa, kv, do, o, dock, dq, dkv, *scratch)
    stage.send(dq, dkv)
    attention_grads_kernel(parts, stage, where_ref, a1, a1, e1, dq, dkv, o, keep, send)


def self_other_back(where, parts, starts, do, qa, kv, o, dock, a1, e1, ahead=()):
    rows, cols = do.shape
    keys, width = a1.shape
    heads = cols // HEAD_DIM
    part = shape((width // 2, 4 * cols), BF16)
    return call(
        partial(self_other_back_kernel, parts, heads),
        (shape((rows, cols), BF16), shape((keys, 2 * cols), BF16), part, part),
        far="NVVVVFF",
        far_out="FFFF",
        flops=56 * rows * keys * cols,
        scalars=2,
        scratch=attend_back_scratch(heads, keys),
    )(where, starts, do, qa, kv, o, dock, a1, e1, ahead=ahead)


def self_own_back_kernel(
    parts, heads, stage, where_ref, starts_ref, do, qa, kv, o, dock, a1, e1, dqo, dkvo, wkv, wlw, wq, wr, x,
    keep_r, send_r, d, keep, send, dq, dkv, *scratch
):
    attend_back_kernel(True, heads, heads // 2, stage, where_ref, starts_ref, qa, kv, do, o, dock, dq, dkv, *scratch)
    attention_grads_kernel(parts, stage, where_ref, a1, a1, e1, dq, dkv, o, keep, send)
    key_value_back_kernel(True, stage, where_ref, dkv, dkvo, wkv, wlw, dq, dqo, wq, wr, x, send_r, keep_r, d)


def self_own_back(where, parts, starts, do, qa, kv, o, dock, a1, e1, dqo, dkvo, wkv, wlw, wq, wr, x, ahead=()):
    rows, cols = do.shape
    keys, width = a1.shape
    heads = cols // HEAD_DIM
    part = shape((width // 2, 4 * cols), BF16)
    return call(
        partial(self_own_back_kernel, parts, heads),
        (shape((rows, width), F32), shape((rows, width), BF16), shape((2, width), F32), part, part),
        far="FFFFFLLLLLKLQL",
        far_out="FNNFF",
        flops=74 * rows * keys * cols,
        scalars=2,
        limit=36,
        scratch=[pltpu.VMEM((rows, cols), BF16), pltpu.VMEM((keys, 2 * cols), BF16)] + attend_back_scratch(heads, keys),
    )(where, starts, do, qa, kv, o, dock, a1, e1, dqo, dkvo, wkv, wlw, wq, wr, x, ahead=ahead)


def feed_grads(where, parts, e, a, du, h, chunk=768):
    rows, width = a[0].shape
    hidden = du[0].shape[1]
    out = shape((width // 2, 2 * hidden), BF16)
    return call(
        partial(feed_grads_kernel, parts, chunk),
        (out, out),
        far="NNNXXXXXXX",
        far_out="FF",
        flops=8 * rows * width * hidden,
        limit=36,
        scratch=[
            pltpu.VMEM((2 * rows, width), BF16), pltpu.VMEM((2, 2 * rows, hidden), BF16), pltpu.VMEM((2 * rows, width), BF16),
            pltpu.SemaphoreType.DMA((8,)),
        ],
    )(where, *a, *du, *h, e)


def swap_tensor(value):
    return lax.ppermute(value, "tensor", [(0, 1), (1, 0)])


def swap_dp(value, bit):
    count = lax.axis_size("dp")
    return lax.ppermute(value, "dp", [(number, number ^ (1 << bit)) for number in range(count)])


def after(value, *others):
    return lax.optimization_barrier((value,) + others)[0] if others else value


def quarter_of(query, key, value, out, part):
    width, cols = query.shape
    rows = width // 4
    pieces = [lax.dynamic_slice_in_dim(weight, part * rows, rows, 0) for weight in (query, key, value)]
    pieces.append(lax.dynamic_slice(out, ((part % 2) * rows, (part // 2) * cols), (rows, cols)))
    return jnp.concatenate(pieces, axis=1)


class Sum:
    def __init__(self, *terms):
        self.terms = [term if isinstance(term, tuple) else (term, 0) for term in terms]
        last, first = self.terms[-1]
        self.rows = last.shape[0]

    def cut(self, first, rows):
        return Sum.of([(array, start + first) for array, start in self.terms], rows)

    @classmethod
    def of(cls, terms, rows):
        made = cls.__new__(cls)
        made.terms, made.rows = terms, rows
        return made

    def plus(self, array):
        return Sum.of(self.terms + [(array, 0)], self.rows)

    def formed(self, dtype=BF16):
        pieces = [
            array.astype(F32) if array.shape[0] == self.rows else lax.dynamic_slice_in_dim(array, start, self.rows, 0).astype(F32)
            for array, start in self.terms
        ]
        return sum(pieces[1:], pieces[0]).astype(dtype)

    def tied(self, *others):
        arrays = [array for array, _ in self.terms]
        made = lax.optimization_barrier((tuple(arrays), others))
        return (Sum.of([(array, start) for array, (_, start) in zip(made[0], self.terms)], self.rows),) + tuple(made[1])


def halve(value, bit, place):
    rows = value.rows // 2
    mine = (place >> bit) & 1
    return value.cut(mine * rows, rows), swap_dp(value.cut((1 - mine) * rows, rows).formed(), bit)


def add(left, right):
    return (left.astype(F32) + right.astype(F32)).astype(BF16)


def shards(
    target_tokens, memory_tokens, output_grad, target_segments, memory_segments,
    norm1_gain, norm1_shift, self_query, self_key, self_value, self_out,
    norm2_gain, norm2_shift, cross_query, cross_key, cross_value, cross_out,
    norm3_gain, norm3_shift, ffn_up, ffn_down,
):
    _, length, width = target_tokens.shape
    cols = self_query.shape[1]
    parts = lax.axis_size("dp")
    bits = parts.bit_length() - 1
    place = lax.axis_index("dp")
    side = lax.axis_index("tensor")
    core = place & 1
    x = target_tokens[0]
    memory = memory_tokens[0]
    e3 = output_grad[0]
    norms = jnp.stack([norm1_gain, norm1_shift, norm2_gain, norm2_shift, norm3_gain, norm3_shift])
    tie = lax.optimization_barrier
    side_one = side.astype(jnp.int32).reshape(1)
    where = jnp.stack([side, core]).astype(jnp.int32)

    part = place % 4
    self_first = swap_tensor(quarter_of(self_query, self_key, self_value, self_out, part))
    cross_quarter = quarter_of(cross_query, cross_key, cross_value, cross_out, part)
    self_wo, cross_wo = self_out, cross_out
    self_wkv = jnp.concatenate([self_key, self_value], axis=1)
    cross_wkv = jnp.concatenate([cross_key, cross_value], axis=1)

    numbers = jnp.arange(DOCS + 1)[:, None]
    target_starts = jnp.sum(target_segments < numbers, 1).astype(jnp.int32)
    memory_starts = jnp.sum(memory_segments < numbers, 1).astype(jnp.int32)
    self_starts = jnp.stack([target_starts, target_starts])
    cross_starts = jnp.stack([target_starts, memory_starts])
    lane = jnp.arange(128) % 64
    hot = target_segments[0][:, None] == lane[None, :]
    doc_rows = jnp.where(hot, LOW, 0.0).astype(BF16)
    doc_target = jnp.where((lane < DOCS)[None, :] & ~hot, 1.0, 0.0).astype(BF16)
    doc_memory = jnp.where(
        (lane < DOCS)[None, :] & (memory_segments[0][:, None] != lane[None, :]), 1.0, 0.0
    ).astype(BF16)

    dh, kv2_own = prepare(e3, ffn_down, memory, cross_wkv)
    self_first, cross_quarter, x_now, dh, kv2_own, doc_rows, doc_target, doc_memory, self_wkv, norms = tie(
        (self_first, cross_quarter, x, dh, kv2_own, doc_rows, doc_target, doc_memory, self_wkv, norms)
    )
    self_second = swap_dp(self_first, 1)
    self_third = swap_dp(self_first, 0)
    cross_first = swap_tensor(cross_quarter)
    o1_own, qa1_own, a1, kv_own, o1_own_far = self_own(
        side_one, self_starts, x_now, norms, self_query, self_wkv, doc_rows, doc_target
    )
    self_second, o1_own, cross_first = tie((self_second, o1_own, cross_first))
    self_fourth = swap_dp(self_second, 0)
    self_fourth, self_third = tie((self_fourth, self_third))
    self_pieces = (self_first, self_third, self_second, self_fourth)
    cross_first, self_pieces = tie((cross_first, self_pieces))
    side_part = jnp.stack([side, part]).astype(jnp.int32)
    cross_second = swap_dp(cross_first, 1)
    cross_third = swap_dp(cross_first, 0)
    o1_oth, qa1_oth, kv_oth, stream1, a2, q2_own, self_two, kv2_near, memory_docs_near = self_other(
        side_part, self_starts, a1, self_pieces, doc_rows, doc_target, x, o1_own, self_wo, norms, cross_query,
        ahead=((kv2_own, "F"), (doc_memory, "F")),
    )
    cross_second, q2_own = tie((cross_second, q2_own))
    cross_fourth = swap_dp(cross_second, 0)
    o2_own, qa2_own, o2_own_far = cross_own(side_one, cross_starts, kv2_near, q2_own, doc_rows, memory_docs_near)
    cross_fourth, cross_third, o2_own = tie((cross_fourth, cross_third, o2_own))
    cross_pieces = (cross_first, cross_third, cross_second, cross_fourth)
    o2_oth, qa2_oth, kv2_oth, stream2, a3, a3_first, a3_second, cross_two = cross_other(
        side_part, cross_starts, memory, cross_pieces, a2, doc_rows, doc_memory, stream1, o2_own, cross_wo, norms
    )

    first_block = (side * (length // 2 // BLOCK)).astype(jnp.int32).reshape(1)
    other_block = length // 2 // BLOCK - first_block
    a3_first, a3_second = swap_tensor(a3_first), swap_tensor(a3_second)
    h_own, du_own, out_own, r3_own = feed(first_block, a3, dh, ffn_up, ffn_down, F32)
    a3_first, r3_own = tie((a3_first, r3_own))
    h_first, du_first, out_first, r3_first = feed(other_block, a3_first, dh, ffn_up, ffn_down, BF16)
    a3_second, r3_first = tie((a3_second, r3_first))
    r3_first = swap_tensor(r3_first)
    h_second, du_second, out_oth, r3_second = feed(other_block + 1, a3_second, dh, ffn_up, ffn_down, BF16, out_first)
    r3_second = swap_tensor(r3_second)
    aligned = (width // parts) % 16 == 0
    static_parts = parts if aligned else 2
    keep_f, send_f = feed_grads(
        where, static_parts, e3, (a3, a3_first, a3_second), (du_own, du_first, du_second), (h_own, h_first, h_second)
    )
    r3_first, r3_second, keep_f, send_f = tie((r3_first, r3_second, keep_f, send_f))

    def reordered(keep, send):
        if aligned:
            return keep, send
        whole = jnp.where(core == 0, jnp.concatenate([keep, send]), jnp.concatenate([send, keep]))
        order = [bit_reversed(number, bits) for number in range(parts)]
        whole = jnp.take(whole.reshape(parts, width // parts, -1), jnp.array(order), axis=0)
        whole = whole.reshape(2, width // 2, -1)
        pick = lambda index: lax.dynamic_index_in_dim(whole, index, 0, False)
        return pick(core), pick(1 - core)

    def swap_core(keep, send):
        keep, send = reordered(keep, send)
        return keep, swap_dp(send, 0)

    keep_f, recv_f = swap_core(keep_f, send_f)
    grad2, e2, do2_own, do2_oth, d3, qa2_near, kv2_near, o2_near, memory_docs_near = after_feed(
        side_one, stream2, r3_own, r3_first, r3_second, e3, norms, cross_wo, cross_two,
        ahead=((qa2_oth, "F"), (kv2_oth, "F"), (o2_oth, "F"), (doc_memory, "F")),
    )
    do2_oth, keep_f, recv_f, out_oth = tie((do2_oth, keep_f, recv_f, out_oth))
    out_recv = swap_tensor(out_oth)
    sum_f, recv_f = halve(Sum(keep_f, recv_f), 1, place)
    (
        keep_d, send_d, keep_c, send_c, dkv2_oth, dkv2_own, grad1, e1, do1_own, do1_oth, d2, wkv_near, wkv2_near
    ) = cross_back(
        where, static_parts, cross_starts, do2_oth, do2_own, qa2_near, kv2_near, o2_near, qa2_own, kv2_own, o2_own_far,
        memory_docs_near, memory, a2, e2, stream1, grad2, cross_query, cross_two, norms, self_wo, self_two,
        ahead=((cross_wkv, "F"), (cross_two, "K")),
    )
    keep_d, send_d, keep_c, send_c, recv_f, out_recv = tie((keep_d, send_d, keep_c, send_c, recv_f, out_recv))
    keep_d, recv_d = swap_core(keep_d, send_d)
    keep_c, recv_c = swap_core(keep_c, send_c)
    sum_f = sum_f.plus(recv_f)
    if bits > 2:
        sum_f, recv_f = halve(sum_f, 2, place)
    send_m, keep_m, qa1_near, kv_near, o1_near, target_near = key_value_back(
        side_one, dkv2_own, dkv2_oth, wkv_near, wkv2_near,
        ahead=((qa1_oth, "F"), (kv_oth, "F"), (o1_oth, "F"), (doc_target, "F")),
    )

    do1_oth, keep_d, recv_d, keep_c, recv_c, send_m = tie((do1_oth, keep_d, recv_d, keep_c, recv_c, send_m))
    sum_d, recv_d = halve(Sum(keep_d, recv_d), 1, place)
    recv_m = swap_tensor(send_m)
    dq1_oth, dkv1_oth, keep_t, send_t = self_other_back(
        where, static_parts, self_starts, do1_oth, qa1_near, kv_near, o1_near, target_near, a1, e1
    )
    keep_t, send_t, recv_d, recv_m, recv_f = tie((keep_t, send_t, recv_d, recv_m, recv_f))
    keep_t, recv_t = swap_core(keep_t, send_t)
    do1_own, keep_t, recv_t = tie((do1_own, keep_t, recv_t))
    sum_t, recv_t = halve(Sum(keep_t, recv_t), 1, place)
    sum_c, recv_c = halve(Sum(keep_c, recv_c), 1, place)
    sent_d = swap_tensor(sum_d.plus(recv_d).formed())
    keep_r, send_r, d1, keep_s, send_s, half_near, grad1_near = self_own_back(
        where, static_parts, self_starts, do1_own, qa1_own, kv_own, o1_own_far, doc_target, a1, e1,
        dq1_oth, dkv1_oth, self_wkv, self_two, self_query, self_two, x, ahead=((x, "H"), (grad1, "F")),
    )
    keep_s, send_s, d1, recv_c, sent_d, recv_t, recv_f = tie((keep_s, send_s, d1, recv_c, sent_d, recv_t, recv_f))
    sum_c, recv_c = sum_c.tied(recv_c)
    sum_t, recv_t = sum_t.tied(recv_t)
    keep_s, recv_s = swap_core(keep_s, send_s)
    sent_t = swap_tensor(sum_t.plus(recv_t).formed())
    sum_c = sum_c.plus(recv_c).plus(sent_d)
    if bits > 2:
        sum_c, recv_c = halve(sum_c, 2, place)
    lines = jnp.concatenate([jnp.concatenate([d[0:1], d[1:2]], axis=1) for d in (d1, d2, d3)], axis=0)
    lines = jnp.pad(lines, ((0, NORM_ROWS - 3), (0, 0))).astype(BF16)
    lines = add(lines, swap_tensor(lines))
    lines = add(lines, swap_dp(lines, 0))
    keep_s, recv_s, send_r, lines, out_recv = tie((keep_s, recv_s, send_r, lines, out_recv))
    recv_r = swap_tensor(send_r)
    layer_output = (stream2 + out_own + out_recv.astype(F32)).astype(BF16)
    if bits > 2:
        sum_f = sum_f.plus(recv_f)
    if bits > 3:
        sum_f, recv_f = halve(sum_f, 3, place)
    sum_s = Sum(keep_s, recv_s)

    def halve_with_lines(value, lines, bit):
        rows = value.rows // 2
        mine = (place >> bit) & 1
        message = jnp.concatenate([value.cut((1 - mine) * rows, rows).formed(), lines], axis=0)
        received = swap_dp(message, bit)
        return value.cut(mine * rows, rows).plus(received), add(lines, received[rows:])

    sum_s, lines = halve_with_lines(sum_s, lines, 1)
    sum_s, lines, sent_t, recv_c, recv_m, layer_output = sum_s.tied(lines, sent_t, recv_c, recv_m, layer_output)
    sum_s = sum_s.plus(sent_t)
    if bits > 2:
        sum_c = sum_c.plus(recv_c)
    for bit in range(3, bits):
        sum_c, recv_c = halve(sum_c, bit, place)
        sum_c = sum_c.plus(recv_c)
    for bit in range(2, bits):
        sum_s, lines = halve_with_lines(sum_s, lines, bit)
        if bit == 2:
            recv_r, lines, recv_f = tie((recv_r, lines, recv_f))
    for bit in range(3, bits):
        sum_f = sum_f.plus(recv_f)
        if bit + 1 < bits:
            sum_f, recv_f = halve(sum_f, bit + 1, place)
    grad_x = input_grad(side_one, half_near, grad1_near, keep_r, recv_r, norms)
    grad_memory = keep_m + recv_m.astype(F32)
    small = lines.astype(F32)
    sum_s, sum_c, sum_f = (value.formed(F32) for value in (sum_s, sum_c, sum_f))

    def four(total):
        pieces = [total[:, number * cols : (number + 1) * cols] for number in range(4)]
        return tuple(pieces[:3]) + (pieces[3].T,)

    hidden = ffn_up.shape[1]
    return (
        (layer_output[None], grad_x[None], grad_memory[None])
        + four(sum_s)
        + four(sum_c)
        + (sum_f[:, :hidden], sum_f[:, hidden:].T)
        + tuple(small[number // 2, (number % 2) * width : (number % 2 + 1) * width] for number in range(6))
    )


def solution(mesh):
    tokens = P("dp", None, None)
    columns = P(None, "tensor")
    rows = P("tensor", None)
    block = (P(), P(), columns, columns, columns, rows)
    in_specs = (tokens,) * 3 + (P("dp", None),) * 2 + block + block + (P(), P(), columns, rows)
    out_rows = P("dp", "tensor")
    out_cols = P("tensor", "dp")
    four = (out_rows, out_rows, out_rows, out_cols)
    out_specs = (P("dp", "tensor", None),) * 3 + four + four + (out_rows, out_cols) + (P(),) * 6
    return jax.shard_map(shards, mesh=mesh, in_specs=in_specs, out_specs=out_specs, check_vma=False)
```
